128 devices in a mesh: ty: 16 (over z, y), tx: 8 (over x, core).
Axes of the slice: x: 4, y: 4, z: 4, core: 2. Of those that a mesh axis runs over, the one named last changes fastest.
Arguments:
- specimen: float32 [2, 8192, 8192], P(None, 'ty', 'tx'), may hold values from -4 to 4
- probe: float32 [2, 4, 256, 256], replicated, may hold values from -4 to 4
- amplitude: float32 [1536, 256, 256], P(('ty', 'tx')), may hold values from 0.4 to 3
- offsets: int32 [1536, 2], P(('ty', 'tx')), may hold values from 0 to 7936, as said below
Outputs:
- object_grad: float32 [2, 8192, 8192], P(None, 'ty', 'tx')
- probe_grad: float32 [2, 4, 256, 256], replicated
The draws below stay inside these ranges and needn't reach their ends.
Inputs may be any that keep to these rules, and one draw needn't show every extreme that they name: Row offsets are at most 7936 and column offsets at most 7936. A position's column offset lies in the tile column of the device that holds it (offset // 1024 equals that device's index along tx). Of the positions that one device holds, exactly 2 or none have their row offset in any one tile row (offset // 512); some tile rows are chosen by many devices.
All inputs are finite; a program needn't handle non-finite values.
Results may differ from the reference program's by a relative error of at most 0.007.
The reference program's roundings to bfloat16 on the way count: a program that leaves them out, or rounds other values in their place, can miss the bound.
Values may be sent and summed in bfloat16 or wider, within the bound.
A program may use at most 192 MiB of HBM per device.

```python
import math
import jax
import jax.numpy as jnp
from jax import lax

PATCH = 256
MODES = 4
TILE_R = 512
TILE_C = 1024
POS_DEV = 12
MOST = 2
OBJ_R = 8192
OBJ_C = 8192
POSITIONS = 1536
N_TY = 16
N_TX = 8


def draw_offsets(key, part):
    key = jax.random.fold_in(key, 11)
    keys = jax.random.split(key, 6)
    devices_all = N_TY * N_TX
    chosen = POS_DEV // MOST
    device_ids = jnp.arange(devices_all, dtype=jnp.int32)
    tile_ids = jnp.arange(N_TY, dtype=jnp.int32)
    crowded = jnp.where(jax.random.randint(keys[0], (N_TY,), 0, 4) == 0, 96, 0)
    forced_rows = (device_ids < N_TX)[:, None] & (tile_ids == N_TY - 2)[None, :]
    scores = jax.random.randint(keys[1], (devices_all, N_TY), 0, 64) + crowded[None, :]
    scores = scores + jnp.where(forced_rows, 1000, 0)
    scores = scores * N_TY + tile_ids[None, :]
    _, picked = jax.lax.top_k(scores, chosen)
    tile_rows = jnp.repeat(picked.astype(jnp.int32), MOST, axis=1)
    shuffle = jax.random.randint(keys[2], (devices_all, POS_DEV), 0, 4096) * POS_DEV + jnp.arange(POS_DEV, dtype=jnp.int32)[None, :]
    order = jnp.argsort(shuffle, axis=1, stable=True)
    tile_rows = jnp.take_along_axis(tile_rows, order, axis=1)
    inner = jax.random.randint(keys[3], (devices_all, POS_DEV), 0, TILE_R)
    low_inner = TILE_R - PATCH // 2 + jax.random.randint(keys[5], (devices_all, POS_DEV), 0, PATCH // 2)
    pushed = (device_ids < N_TX)[:, None] & (tile_rows == N_TY - 2)
    inner = jnp.where(pushed, low_inner, inner)
    row_pos = tile_rows * TILE_R + inner
    row_pos = jnp.minimum(row_pos, OBJ_R - PATCH)
    column_tile = (device_ids % N_TX)[:, None]
    col_pos = column_tile * TILE_C + jax.random.randint(keys[4], (devices_all, POS_DEV), 0, TILE_C)
    col_pos = jnp.minimum(col_pos, OBJ_C - PATCH)
    return jnp.stack([row_pos.reshape(-1), col_pos.reshape(-1)], axis=1).astype(jnp.int32)


def level_of(stream_key, extent, shards, smallest, high):
    factor_of, own = 1.0, jax.random.fold_in(stream_key, 6)
    for position, parts in shards:
        heights = jnp.exp(jax.random.uniform(jax.random.fold_in(own, position), (parts,), jnp.float32, smallest / len(shards), high / len(shards)))
        factor_of = factor_of * jnp.repeat(heights, extent[position] // parts).reshape([-1 if axis == position else 1 for axis in range(len(extent))])
    return factor_of


def gaussian(stream_key, shape, width, limit, cuts=(), kind=jnp.bfloat16):
    values = jax.random.normal(stream_key, shape, jnp.float32) * width
    if len(cuts) > 0:
        values = level_of(stream_key, shape, cuts, -0.22, 0.18) * values
    return jnp.clip(values, min=-limit, max=limit).astype(kind)


def setup_inputs(seed: int = 0) -> dict:
    streams_of = jax.random.split(jax.random.key(seed), 5)
    return {
        "specimen": gaussian(streams_of[0], (2, OBJ_R, OBJ_C), 0.7, 4.0, ((1, 16), (2, 8)), jnp.float32),
        "probe": gaussian(streams_of[1], (2, MODES, PATCH, PATCH), 0.5, 4.0, (), jnp.float32),
        "amplitude": jnp.clip(jnp.exp(math.log(3.0) - 2.014903 * jax.random.uniform(streams_of[2], (POSITIONS, PATCH, PATCH), jnp.float32) ** level_of(streams_of[2], (POSITIONS, PATCH, PATCH), ((0, 128),), -0.2, 0.2)), 0.4, 3.0),
        "offsets": draw_offsets(jax.random.fold_in(streams_of[4], 71), 0),
    }


def make_tables(size):
    index = jnp.arange(size, dtype=jnp.int32)
    phase = index[:, None] * index[None, :] % size
    angle = phase.astype(jnp.float32) * (2.0 * math.pi / size)
    factor = 1.0 / math.sqrt(size)
    return ((jnp.cos(angle) * factor).astype(jnp.bfloat16), (-jnp.sin(angle) * factor).astype(jnp.bfloat16))

def right_product(left_re, left_im, table_re, table_im):
    a_re = left_re.astype(jnp.float32)
    a_im = left_im.astype(jnp.float32)
    b_re = table_re.astype(jnp.float32)
    b_im = table_im.astype(jnp.float32)
    out_re = jnp.einsum('msk,kn->msn', a_re, b_re) - jnp.einsum('msk,kn->msn', a_im, b_im)
    out_im = jnp.einsum('msk,kn->msn', a_re, b_im) + jnp.einsum('msk,kn->msn', a_im, b_re)
    return (out_re, out_im)

def left_product(table_re, table_im, right_re, right_im):
    a_re = table_re.astype(jnp.float32)
    a_im = table_im.astype(jnp.float32)
    b_re = right_re.astype(jnp.float32)
    b_im = right_im.astype(jnp.float32)
    out_re = jnp.einsum('sk,mkn->msn', a_re, b_re) - jnp.einsum('sk,mkn->msn', a_im, b_im)
    out_im = jnp.einsum('sk,mkn->msn', a_re, b_im) + jnp.einsum('sk,mkn->msn', a_im, b_re)
    return (out_re, out_im)

def position_terms(patch, measured, probe, four_re, four_im):
    patch_re = patch[0].astype(jnp.float32)
    patch_im = patch[1].astype(jnp.float32)
    probe_re = probe[0]
    probe_im = probe[1]
    exit_re = (probe_re * patch_re - probe_im * patch_im).astype(jnp.bfloat16)
    exit_im = (probe_re * patch_im + probe_im * patch_re).astype(jnp.bfloat16)
    half_re, half_im = right_product(exit_re, exit_im, four_re, four_im)
    far_re, far_im = left_product(four_re, four_im, half_re.astype(jnp.bfloat16), half_im.astype(jnp.bfloat16))
    intensity = lax.optimization_barrier(jnp.sum(far_re * far_re + far_im * far_im, axis=0))
    factor = 1.0 - measured / jnp.sqrt(jnp.maximum(intensity, 0.25))
    resid_re = (far_re * factor).astype(jnp.bfloat16)
    resid_im = (far_im * factor).astype(jnp.bfloat16)
    conj_im = -four_im
    back_re, back_im = right_product(resid_re, resid_im, four_re, conj_im)
    back_re, back_im = left_product(four_re, conj_im, back_re.astype(jnp.bfloat16), back_im.astype(jnp.bfloat16))
    grad_re = lax.optimization_barrier(jnp.sum(probe_re * back_re + probe_im * back_im, axis=0))
    grad_im = lax.optimization_barrier(jnp.sum(probe_re * back_im - probe_im * back_re, axis=0))
    grad = jnp.stack([grad_re, grad_im]).astype(jnp.bfloat16)
    term = jnp.stack([patch_re * back_re + patch_im * back_im, patch_re * back_im - patch_im * back_re])
    return (grad, term)

def reference(specimen, probe, amplitude, offsets):
    half_object = specimen.astype(jnp.bfloat16)
    four_re, four_im = make_tables(PATCH)

    def advance(carry, item):
        field, total = carry
        measured, place = item
        start = (jnp.int32(0), place[0].astype(jnp.int32), place[1].astype(jnp.int32))
        patch = lax.dynamic_slice(half_object, start, (2, PATCH, PATCH))
        grad, term = position_terms(patch, measured, probe, four_re, four_im)
        current = lax.dynamic_slice(field, start, (2, PATCH, PATCH))
        field = lax.dynamic_update_slice(field, current + grad.astype(jnp.float32), start)
        return ((field, total + term), None)
    field = jnp.zeros((2, OBJ_R, OBJ_C), jnp.float32)
    total = jnp.zeros((2, MODES, PATCH, PATCH), jnp.float32)
    (field, total), _ = lax.scan(advance, (field, total), (amplitude, offsets))
    return (field, total * (MODES / math.sqrt(POSITIONS)))
```

```python
import jax
import jax.numpy as jnp
import ml_dtypes
import numpy as np
from jax import lax
from jax.experimental import pallas as pl
from jax.experimental.pallas import tpu as pltpu
from jax.sharding import PartitionSpec as P

bf = jnp.bfloat16
f32 = jnp.float32
N = 256
H = 128
TILE_R = 512
TILE_C = 1024
POS = 12
VMEM_LIMIT = 60 * 2**20


def make_tables():
    k = np.arange(N)
    ang = ((k[:, None] * k[None, :]) % N).astype(np.float64) * (2 * np.pi / N)
    re = (np.cos(ang) / 16).astype(np.float32).astype(ml_dtypes.bfloat16).astype(np.float32)
    im = (-np.sin(ang) / 16).astype(np.float32).astype(ml_dtypes.bfloat16).astype(np.float32)
    order = np.arange(128).reshape(8, 16).T.reshape(-1)
    def mix(a, b):
        return np.stack([a.reshape(16, 8, -1), b.reshape(16, 8, -1)], 1).reshape(256, -1)
    out = []
    for par in (0, 1):
        r, i = re[:H, par::2], im[:H, par::2]
        out.append(np.block([[r, i], [-i, r]]))
    for par in (0, 1):
        r, i = re[par::2][:, order], im[par::2][:, order]
        out.append(mix(np.block([r, -i]), np.block([i, r])))
    for par in (0, 1):
        r, i = re[par::2, :H], -im[par::2, :H]
        out.append(np.block([[r, i], [-i, r]]))
    for par in (0, 1):
        r, i = re[order][:, par::2], -im[order][:, par::2]
        out.append(mix(np.block([r, -i]), np.block([i, r])))
    return np.stack(out).astype(ml_dtypes.bfloat16)

def arrange(x):
    lead = x.shape[:-2]
    return jnp.swapaxes(jnp.moveaxis(x.reshape(*lead, 2, 8, 16, x.shape[-1]), -2, -4), -3, -3).reshape(*lead, 256, x.shape[-1])

def restore(x):
    lead = x.shape[:-2]
    return jnp.moveaxis(x.reshape(*lead, 16, 2, 8, x.shape[-1]), -4, -2).reshape(*lead, 256, x.shape[-1])

def dot(a, b):
    return jnp.dot(a, b, preferred_element_type=f32)

def halves(x):
    x = x.reshape(16, 2, 8, x.shape[-1])
    return x[:, 0].reshape(128, x.shape[-1]), x[:, 1].reshape(128, x.shape[-1])

def p1(m, probe, pat, A):
    for c in range(2):
        ch = slice(c * H, c * H + H)
    pr, pi = probe[0, m], probe[1, m]
    qr, qi = pat[0], pat[1]
    er = pr * qr - pi * qi
    ei = pr * qi + pi * qr
    A[m, 0, :, :H] = (er[:, :H] + er[:, H:]).astype(bf)
    A[m, 0, :, H:] = (ei[:, :H] + ei[:, H:]).astype(bf)
    A[m, 1, :, :H] = (er[:, :H] - er[:, H:]).astype(bf)
    A[m, 1, :, H:] = (ei[:, :H] - ei[:, H:]).astype(bf)

def p2(m, tab, A, B):
    for p in (0, 1):
        t, b = halves(dot(A[m, p], tab[p]))
        s = (t + b).astype(bf)
        d = (t - b).astype(bf)
        ls = slice(p * H, p * H + H)
        B[m, 0, :H, ls] = s[:, :H]
        B[m, 0, H:, ls] = s[:, H:]
        B[m, 1, :H, ls] = d[:, :H]
        B[m, 1, H:, ls] = d[:, H:]

def p3(m, tab, B, far, inten):
    for p in (0, 1):
        r, i = halves(dot(tab[2 + p], B[m, p]))
        far[m, p, 0] = r
        far[m, p, 1] = i
        t = r * r + i * i
        if m == 0:
            inten[p] = t
        else:
            inten[p] += t

def p4(amp, inten):
    for p in (0, 1):
        a = amp[p * H:(p + 1) * H].astype(f32)
        inten[p] = 1.0 - a * lax.rsqrt(jnp.maximum(inten[p], 0.25))

def p5(m, far, fac, C):
    for p in (0, 1):
        f = fac[p]
        rr = (far[m, p, 0] * f).astype(bf)
        ri = (far[m, p, 1] * f).astype(bf)
        rs = slice(p * H, p * H + H)
        C[m, 0, rs, :H] = rr[:, :H]
        C[m, 0, rs, H:] = ri[:, :H]
        C[m, 1, rs, :H] = rr[:, H:]
        C[m, 1, rs, H:] = ri[:, H:]

def p6(m, tab, C, G):
    e = dot(C[m, 0], tab[4])
    o = dot(C[m, 1], tab[5])
    s = (e + o).astype(bf)
    d = (e - o).astype(bf)
    for p in (0, 1):
        rs = slice(p * H, p * H + H)
        G[m, p, :H, :H] = s[rs, :H]
        G[m, p, :H, H:] = d[rs, :H]
        G[m, p, H:, :H] = s[rs, H:]
        G[m, p, H:, H:] = d[rs, H:]

def p7(m, tab, G, probe, pat, grad, total):
    e = dot(tab[6], G[m, 0])
    o = dot(tab[7], G[m, 1])
    er, ei = halves(e)
    r_, i_ = halves(o)
    def both(a, b):
        return jnp.stack([a.reshape(16, 8, 256), b.reshape(16, 8, 256)], 1).reshape(256, 256)
    br = both(er + r_, er - r_)
    bi = both(ei + i_, ei - i_)
    pr, pi = probe[0, m], probe[1, m]
    qr, qi = pat[0], pat[1]
    gr = pr * br + pi * bi
    gi = pr * bi - pi * br
    if m == 0:
        grad[0] = gr
        grad[1] = gi
    else:
        grad[0] += gr
        grad[1] += gi
    total[0, m] += qr * br + qi * bi
    total[1, m] += qr * bi - qi * br

def position(probe, pat, amp, tab, A, B, far, C, G, total, grad, inten):
    M = 4
    for t in range(M + 2):
        if t - 2 >= 0: p3(t - 2, tab, B, far, inten)
        if 0 <= t - 1 < M: p2(t - 1, tab, A, B)
        if t < M: p1(t, probe, pat, A)
    p4(amp, inten)
    for t in range(M + 2):
        if t - 2 >= 0: p7(t - 2, tab, G, probe, pat, grad, total)
        if 0 <= t - 1 < M: p6(t - 1, tab, C, G)
        if t < M: p5(t, far, inten, C)

def fetch(ext, pat, r, c):
    ct = c // 128
    sh = c % 128
    lane = lax.broadcasted_iota(jnp.int32, (128, 128), 1)
    keep = lane < 128 - sh
    for k in (0, 1):
        for h in (0, 1):
            x = []
            for t in range(3):
                v = jnp.concatenate([ext[k, ct + t, pl.ds(r + 128 * h + i, 8, stride=16)] for i in range(16)], axis=0)
                x.append(pltpu.roll(v, 128 - sh, axis=1))
            for t in (0, 1):
                y = jnp.where(keep, x[t], x[t + 1])
                for i in range(16):
                    pat[k, 16 * i + 8 * h:16 * i + 8 * h + 8, t * H:t * H + H] = y[8 * i:8 * i + 8]

def deposit(grid, grad, r, c):
    ct = c // 128
    sh = c % 128
    lane = lax.broadcasted_iota(jnp.int32, (256, 128), 1)
    keep = lane >= sh
    for k in (0, 1):
        x = grad[k].astype(bf).astype(f32)
        a = pltpu.roll(x[:, :H], sh, axis=1)
        b = pltpu.roll(x[:, H:], sh, axis=1)
        z = jnp.zeros_like(a)
        for t, y in enumerate((jnp.where(keep, a, z), jnp.where(keep, b, a), jnp.where(keep, z, b))):
            for i in range(16):
                for h in (0, 1):
                    ds = pl.ds(r + 128 * h + i, 8, stride=16)
                    grid[k, ct + t, ds] = grid[k, ct + t, ds] + y[16 * i + 8 * h:16 * i + 8 * h + 8]


def parity_matrix():
    order = np.concatenate([np.arange(0, N, 2), np.arange(1, N, 2)])
    return np.eye(N)[order].astype(ml_dtypes.bfloat16)


def slot_of(off, i):
    tile = off[2 * i] // TILE_R
    rank = jnp.int32(0)
    for j in range(POS):
        same = (off[2 * j] // TILE_R == tile) & (j < i)
        rank = rank + same.astype(jnp.int32)
    return tile, rank


def prep_kernel(off, amp, perm, out):
    a = amp[0].astype(bf)
    a = dot(perm[...], a).astype(bf)
    out[0, 0] = lax.dot_general(a, perm[...], (((1,), (1,)), ((), ())), preferred_element_type=f32).astype(bf)


def prepare(off, amplitude, sources):
    def place(i, off):
        tile, rank = slot_of(off, i)
        return (tile, rank, 0, 0)

    return pl.pallas_call(
        prep_kernel,
        out_shape=jax.ShapeDtypeStruct((sources, 2, N, N), bf),
        grid_spec=pltpu.PrefetchScalarGridSpec(
            num_scalar_prefetch=1,
            grid=(POS,),
            in_specs=[pl.BlockSpec((1, N, N), lambda i, o: (i, 0, 0)), pl.BlockSpec((N, N), lambda i, o: (0, 0))],
            out_specs=pl.BlockSpec((1, 1, N, N), place),
        ),
    )(off, amplitude, parity_matrix())


def find(off, source, tile):
    rows, cols = [jnp.int32(-1)] * 2, [jnp.int32(0)] * 2
    seen = jnp.int32(0)
    for i in range(POS):
        base = (source * POS + i) * 2
        r, c = off[base], off[base + 1]
        mine = r // TILE_R == tile
        for q in range(2):
            take = mine & (seen == q)
            rows[q] = jnp.where(take, r % TILE_R, rows[q])
            cols[q] = jnp.where(take, c % TILE_C, cols[q])
        seen = seen + mine.astype(jnp.int32)
    return rows, cols


def tile_kernel(off, spec, right, lower, corner, probe, amp, tab, main_o, down_o, right_o, corner_o, total, ext, grid, pat, A, B, far, C, G, grad, inten):
    s = pl.program_id(0)
    @pl.when(s == 0)
    def _():
        for c in (0, 1):
            for t in range(10):
                ls = slice(t * H, t * H + H)
                l2 = slice(t * H - 1024, t * H - 1024 + H)
                ext[c, t, :512] = (spec[c, :, ls] if t < 8 else right[c, :, l2]).astype(bf).astype(f32)
                ext[c, t, 512:] = (lower[c, :, ls] if t < 8 else corner[c, :, l2]).astype(f32)
        grid[...] = jnp.zeros_like(grid)
        total[...] = jnp.zeros_like(total)
    rows, cols = find(off, s, lax.axis_index("ty"))
    for q in range(2):
        @pl.when(rows[q] >= 0)
        def _():
            r = rows[q]
            c = cols[q]
            fetch(ext, pat, r, c)
            position(probe, pat, amp.at[0, q], tab, A, B, far, C, G, total, grad, inten)
            deposit(grid, grad, r, c)
    @pl.when(s == pl.num_programs(0) - 1)
    def _():
        for c in (0, 1):
            for t in range(10):
                ls = slice(t * H, t * H + H)
                l2 = slice(t * H - 1024, t * H - 1024 + H)
                if t < 8:
                    main_o[c, :, ls] = grid[c, t, :512]
                    down_o[c, :, ls] = grid[c, t, 512:].astype(bf)
                else:
                    right_o[c, :, l2] = grid[c, t, :512].astype(bf)
                    corner_o[c, :, l2] = grid[c, t, 512:].astype(bf)

def compute(off, spec, right, lower, corner, probe, amp, tab):
    probe = arrange(probe)
    full = lambda *shape: pl.BlockSpec(shape, lambda i, o: (0,) * len(shape), pipeline_mode=pl.Buffered(1))
    main, down, rt, cn, total = pl.pallas_call(
        tile_kernel,
        out_shape=[jax.ShapeDtypeStruct((2, 512, 1024), f32), jax.ShapeDtypeStruct((2, 256, 1024), bf),
                   jax.ShapeDtypeStruct((2, 512, 256), bf), jax.ShapeDtypeStruct((2, 256, 256), bf),
                   jax.ShapeDtypeStruct((2, 4, 256, 256), f32)],
        grid_spec=pltpu.PrefetchScalarGridSpec(
            num_scalar_prefetch=1, grid=(amp.shape[0],),
            in_specs=[full(2, 512, 1024), full(2, 512, 256), full(2, 256, 1024), full(2, 256, 256),
                      full(2, 4, 256, 256), pl.BlockSpec((1, 2, 256, 256), lambda i, o: (i, 0, 0, 0)), full(8, 256, 256)],
            out_specs=[full(2, 512, 1024), full(2, 256, 1024), full(2, 512, 256), full(2, 256, 256), full(2, 4, 256, 256)],
            scratch_shapes=[pltpu.VMEM((2, 10, 768, 128), f32), pltpu.VMEM((2, 10, 768, 128), f32), pltpu.VMEM((2, 256, 256), f32),
                            pltpu.VMEM((4, 2, 256, 256), bf), pltpu.VMEM((4, 2, 256, 256), bf), pltpu.VMEM((4, 2, 2, 128, 256), f32),
                            pltpu.VMEM((4, 2, 256, 256), bf), pltpu.VMEM((4, 2, 256, 256), bf), pltpu.VMEM((2, 256, 256), f32),
                            pltpu.VMEM((2, 128, 256), f32)]),
        compiler_params=pltpu.CompilerParams(vmem_limit_bytes=VMEM_LIMIT),
    )(off, spec, right, lower, corner, probe, amp, tab)
    return main, down, rt, cn, restore(total)


def shift(value, d_ty, d_tx, n_ty, n_tx):
    pairs = []
    for y in range(n_ty):
        for x in range(n_tx):
            if 0 <= y + d_ty < n_ty and 0 <= x + d_tx < n_tx:
                pairs.append((y * n_tx + x, (y + d_ty) * n_tx + x + d_tx))
    return lax.ppermute(value, ("ty", "tx"), pairs)


def on_device(specimen, probe, amplitude, offsets):
    n_ty, n_tx = lax.axis_size("ty"), lax.axis_size("tx")
    positions = offsets.shape[0] * n_ty * n_tx
    right = shift(specimen[:, :, :N].astype(bf), 0, -1, n_ty, n_tx)
    lower = shift(specimen[:, :N, :].astype(bf), -1, 0, n_ty, n_tx)
    corner = shift(specimen[:, :N, :N].astype(bf), -1, -1, n_ty, n_tx)
    everyone = lax.all_gather(offsets.reshape(-1), "ty", tiled=True)
    slots = prepare(offsets.reshape(-1), amplitude, n_ty)
    arrived = lax.all_to_all(slots, "ty", split_axis=0, concat_axis=0, tiled=True)
    main, down, rt, cn, total = compute(everyone, specimen, right, lower, corner, probe, arrived, make_tables())
    down = shift(down, 1, 0, n_ty, n_tx).astype(f32)
    rt = shift(rt, 0, 1, n_ty, n_tx).astype(f32)
    cn = shift(cn, 1, 1, n_ty, n_tx).astype(f32)
    main = main.at[:, :N, :].add(down).at[:, :, :N].add(rt).at[:, :N, :N].add(cn)
    probe_grad = lax.psum(total, ("ty", "tx")) * (probe.shape[1] / np.sqrt(positions))
    return (main, probe_grad.astype(f32))


def solution(mesh):
    in_specs = (P(None, "ty", "tx"), P(), P(("ty", "tx"), None, None), P(("ty", "tx"), None))
    out_specs = (P(None, "ty", "tx"), P())
    return jax.shard_map(on_device, mesh=mesh, in_specs=in_specs, out_specs=out_specs, check_vma=False)
```

```python
import functools

import jax
import jax.numpy as jnp
import ml_dtypes
import numpy as np
from jax import lax
from jax.experimental import pallas as pl
from jax.experimental.pallas import tpu as pltpu
from jax.sharding import PartitionSpec as P

bf = jnp.bfloat16
f32 = jnp.float32
N = 256
H = 128
TILE_R = 512
TILE_C = 1024
POS = 12
VMEM_LIMIT = 60 * 2**20
MESH = pl.DeviceIdType.MESH
S = 2
B = 16 // S

def row0(i):
    return i // S * 8 * S + i % S

def make_tables():
    k = np.arange(N)
    ang = ((k[:, None] * k[None, :]) % N).astype(np.float64) * (2 * np.pi / N)
    re = (np.cos(ang) / 16).astype(np.float32).astype(ml_dtypes.bfloat16).astype(np.float32)
    im = (-np.sin(ang) / 16).astype(np.float32).astype(ml_dtypes.bfloat16).astype(np.float32)
    order = np.arange(128).reshape(B, 8, S).swapaxes(1, 2).reshape(-1)
    def mix(a, b):
        return np.stack([a.reshape(16, 8, -1), b.reshape(16, 8, -1)], 1).reshape(256, -1)
    out = []
    for par in (0, 1):
        r, i = re[:H, par::2], im[:H, par::2]
        out.append(np.block([[r, i], [-i, r]]))
    for par in (0, 1):
        r, i = re[par::2][:, order], im[par::2][:, order]
        out.append(mix(np.block([r, -i]), np.block([i, r])))
    for par in (0, 1):
        r, i = re[par::2, :H], -im[par::2, :H]
        out.append(np.block([[r, i], [-i, r]]))
    for par in (0, 1):
        r, i = re[order][:, par::2], -im[order][:, par::2]
        out.append(mix(np.block([r, -i]), np.block([i, r])))
    return np.stack(out).astype(ml_dtypes.bfloat16)

def arrange(x):
    lead = x.shape[:-2]
    x = x.reshape(*lead, 2, B, 8, S, x.shape[-1])
    k = len(lead)
    return jnp.transpose(x, (*range(k), k + 1, k + 3, k, k + 2, k + 4)).reshape(*lead, 256, x.shape[-1])

def restore(x):
    lead = x.shape[:-2]
    x = x.reshape(*lead, B, S, 2, 8, x.shape[-1])
    k = len(lead)
    return jnp.transpose(x, (*range(k), k + 2, k, k + 3, k + 1, k + 4)).reshape(*lead, 256, x.shape[-1])

def dot(a, b):
    return jnp.dot(a, b, preferred_element_type=f32)

def halves(x):
    x = x.reshape(16, 2, 8, x.shape[-1])
    return x[:, 0].reshape(128, x.shape[-1]), x[:, 1].reshape(128, x.shape[-1])


def parity_matrix():
    order = np.concatenate([np.arange(0, N, 2), np.arange(1, N, 2)])
    return np.eye(N)[order].astype(ml_dtypes.bfloat16)


def slot_of(off, i):
    tile = off[2 * i] // TILE_R
    rank = jnp.int32(0)
    for j in range(POS):
        same = (off[2 * j] // TILE_R == tile) & (j < i)
        rank = rank + same.astype(jnp.int32)
    return tile, rank


def prep_kernel(off, amp, perm, out):
    a = amp[0].astype(bf)
    a = dot(perm[...], a).astype(bf)
    out[0, 0] = lax.dot_general(a, perm[...], (((1,), (1,)), ((), ())), preferred_element_type=f32).astype(bf)


def prepare(off, amplitude, sources):
    def place(i, off):
        tile, rank = slot_of(off, i)
        return (tile, rank, 0, 0)

    return pl.pallas_call(
        prep_kernel,
        out_shape=jax.ShapeDtypeStruct((sources, 2, N, N), bf),
        grid_spec=pltpu.PrefetchScalarGridSpec(
            num_scalar_prefetch=1,
            grid=(POS,),
            in_specs=[pl.BlockSpec((1, N, N), lambda i, o: (i, 0, 0)), pl.BlockSpec((N, N), lambda i, o: (0, 0))],
            out_specs=pl.BlockSpec((1, 1, N, N), place),
        ),
    )(off, amplitude, parity_matrix())


def find(off, source, tile):
    rows, cols = [jnp.int32(-1)] * 2, [jnp.int32(0)] * 2
    seen = jnp.int32(0)
    for i in range(POS):
        base = (source * POS + i) * 2
        r, c = off[base], off[base + 1]
        mine = r // TILE_R == tile
        for q in range(2):
            take = mine & (seen == q)
            rows[q] = jnp.where(take, r % TILE_R, rows[q])
            cols[q] = jnp.where(take, c % TILE_C, cols[q])
        seen = seen + mine.astype(jnp.int32)
    return rows, cols


def p1(probe, pat, A):
    pr, pi = probe[0], probe[1]
    qr, qi = pat[0], pat[1]
    er = pr * qr - pi * qi
    ei = pr * qi + pi * qr
    A[0, :, :H] = (er[:, :H] + er[:, H:]).astype(bf)
    A[0, :, H:] = (ei[:, :H] + ei[:, H:]).astype(bf)
    A[1, :, :H] = (er[:, :H] - er[:, H:]).astype(bf)
    A[1, :, H:] = (ei[:, :H] - ei[:, H:]).astype(bf)


def p2(tab, A, Bb):
    for p in (0, 1):
        t, b = halves(dot(A[p], tab[p]))
        s = (t + b).astype(bf)
        d = (t - b).astype(bf)
        ls = slice(p * H, p * H + H)
        Bb[0, :H, ls] = s[:, :H]
        Bb[0, H:, ls] = s[:, H:]
        Bb[1, :H, ls] = d[:, :H]
        Bb[1, H:, ls] = d[:, H:]


def p3(first, tab, Bb, far, inten):
    for p in (0, 1):
        r, i = halves(dot(tab[2 + p], Bb[p]))
        far[p, 0] = r
        far[p, 1] = i
        t = r * r + i * i
        inten[p] = t if first else inten[p] + t


def p4(amp, inten, fac):
    for p in (0, 1):
        a = amp[p * H:(p + 1) * H].astype(f32)
        fac[p] = 1.0 - a * lax.rsqrt(jnp.maximum(inten[p], 0.25))


def p5(far, fac, C):
    for p in (0, 1):
        f = fac[p]
        rr = (far[p, 0] * f).astype(bf)
        ri = (far[p, 1] * f).astype(bf)
        rs = slice(p * H, p * H + H)
        C[0, rs, :H] = rr[:, :H]
        C[0, rs, H:] = ri[:, :H]
        C[1, rs, :H] = rr[:, H:]
        C[1, rs, H:] = ri[:, H:]


def p6(tab, C, G):
    e = dot(C[0], tab[4])
    o = dot(C[1], tab[5])
    s = (e + o).astype(bf)
    d = (e - o).astype(bf)
    for p in (0, 1):
        rs = slice(p * H, p * H + H)
        G[p, :H, :H] = s[rs, :H]
        G[p, :H, H:] = d[rs, :H]
        G[p, H:, :H] = s[rs, H:]
        G[p, H:, H:] = d[rs, H:]


def both(a, b):
    return jnp.stack([a.reshape(16, 8, 256), b.reshape(16, 8, 256)], 1).reshape(256, 256)


def p7(first, tab, G, probe, pat, grad, total, m):
    er, ei = halves(dot(tab[6], G[0]))
    r_, i_ = halves(dot(tab[7], G[1]))
    br = both(er + r_, er - r_)
    bi = both(ei + i_, ei - i_)
    pr, pi = probe[0], probe[1]
    qr, qi = pat[0], pat[1]
    gr = pr * br + pi * bi
    gi = pr * bi - pi * br
    grad[0] = gr if first else grad[0] + gr
    grad[1] = gi if first else grad[1] + gi
    total[0, m] += qr * br + qi * bi
    total[1, m] += qr * bi - qi * br


def fetch(ext, pat, r, c):
    ct = c // 128
    sh = c % 128
    lane = lax.broadcasted_iota(jnp.int32, (128, 128), 1)
    keep = lane < 128 - sh
    for k in (0, 1):
        for h in (0, 1):
            x = []
            for t in range(3):
                v = jnp.concatenate([ext[k, ct + t, pl.ds(r + 128 * h + row0(i), 8, stride=S)] for i in range(16)], axis=0)
                x.append(pltpu.roll(v, 128 - sh, axis=1))
            for t in (0, 1):
                y = jnp.where(keep, x[t], x[t + 1])
                for i in range(16):
                    pat[k, 16 * i + 8 * h:16 * i + 8 * h + 8, t * H:t * H + H] = y[8 * i:8 * i + 8]

def deposit(grid, grad, r, c):
    ct = c // 128
    sh = c % 128
    lane = lax.broadcasted_iota(jnp.int32, (256, 128), 1)
    keep = lane >= sh
    for k in (0, 1):
        x = grad[k].astype(bf).astype(f32)
        a = pltpu.roll(x[:, :H], sh, axis=1)
        b = pltpu.roll(x[:, H:], sh, axis=1)
        z = jnp.zeros_like(a)
        for t, y in enumerate((jnp.where(keep, a, z), jnp.where(keep, b, a), jnp.where(keep, z, b))):
            for i in range(16):
                for h in (0, 1):
                    ds = pl.ds(r + 128 * h + row0(i), 8, stride=S)
                    grid[k, ct + t, ds] = grid[k, ct + t, ds] + y[16 * i + 8 * h:16 * i + 8 * h + 8]


def forward_kernel(off, spec, right, lower, corner, probe, tab, far, pat, inten, ext, A, Bb):
    s = pl.program_id(0)

    @pl.when(s == 0)
    def _():
        for c in (0, 1):
            for t in range(10):
                ls = slice(t * H, t * H + H)
                l2 = slice(t * H - 1024, t * H - 1024 + H)
                ext[c, t, :512] = (spec[c, :, ls] if t < 8 else right[c, :, l2]).astype(bf).astype(f32)
                ext[c, t, 512:] = (lower[c, :, ls] if t < 8 else corner[c, :, l2]).astype(f32)

    rows, cols = find(off, s, lax.axis_index("ty"))

    @pl.when(rows[0] >= 0)
    def _():
        items = [(q, m) for q in range(2) for m in range(4)]
        for t in range(len(items) + 2):
            if 0 <= t - 1 < len(items):
                q, m = items[t - 1]
                p2(tab, A.at[q, m], Bb.at[q, m])
            if 0 <= t - 2 < len(items):
                q, m = items[t - 2]
                p3(m == 0, tab, Bb.at[q, m], far.at[0, q, m], inten.at[0, q])
            if t < len(items):
                q, m = items[t]
                if m == 0:
                    fetch(ext, pat.at[0, q], rows[q], cols[q])
                p1(probe.at[:, m], pat.at[0, q], A.at[q, m])


def backward_kernel(off, probe, tab, amp, far, pat, inten, main_o, down_o, right_o, corner_o, total, grid, fac, C, G, grad):
    s = pl.program_id(0)

    @pl.when(s == 0)
    def _():
        grid[...] = jnp.zeros_like(grid)
        total[...] = jnp.zeros_like(total)

    rows, cols = find(off, s, lax.axis_index("ty"))

    @pl.when(rows[0] >= 0)
    def _():
        items = [(q, m) for q in range(2) for m in range(4)]
        for t in range(len(items) + 2):
            if 0 <= t - 1 < len(items):
                q, m = items[t - 1]
                p6(tab, C.at[q, m], G.at[q, m])
            if 0 <= t - 2 < len(items):
                q, m = items[t - 2]
                p7(m == 0, tab, G.at[q, m], probe.at[:, m], pat.at[0, q], grad.at[q], total, m)
                if m == 3:
                    deposit(grid, grad.at[q], rows[q], cols[q])
            if t < len(items):
                q, m = items[t]
                if m == 0:
                    p4(amp.at[0, q], inten.at[0, q], fac.at[q])
                p5(far.at[0, q, m], fac.at[q], C.at[q, m])

    @pl.when(s == pl.num_programs(0) - 1)
    def _():
        for c in (0, 1):
            for t in range(10):
                ls = slice(t * H, t * H + H)
                l2 = slice(t * H - 1024, t * H - 1024 + H)
                if t < 8:
                    main_o[c, :, ls] = grid[c, t, :512]
                    down_o[c, :, ls] = grid[c, t, 512:].astype(bf)
                else:
                    right_o[c, :, l2] = grid[c, t, :512].astype(bf)
                    corner_o[c, :, l2] = grid[c, t, 512:].astype(bf)


def whole(*shape):
    return pl.BlockSpec(shape, lambda i, o: (0,) * len(shape), pipeline_mode=pl.Buffered(1))


def each(*shape):
    return pl.BlockSpec((1, *shape), lambda i, o: (i,) + (0,) * len(shape))


def like(shape, dtype):
    return jax.ShapeDtypeStruct(shape, dtype)


def forward(off, spec, right, lower, corner, probe, tab, sources):
    return pl.pallas_call(
        forward_kernel,
        out_shape=[like((sources, 2, 4, 2, 2, 128, 256), f32), like((sources, 2, 2, 256, 256), f32), like((sources, 2, 2, 128, 256), f32)],
        grid_spec=pltpu.PrefetchScalarGridSpec(
            num_scalar_prefetch=1, grid=(sources,),
            in_specs=[whole(2, 512, 1024), whole(2, 512, 256), whole(2, 256, 1024), whole(2, 256, 256), whole(2, 4, 256, 256), whole(8, 256, 256)],
            out_specs=[each(2, 4, 2, 2, 128, 256), each(2, 2, 256, 256), each(2, 2, 128, 256)],
            scratch_shapes=[pltpu.VMEM((2, 10, 768, 128), f32), pltpu.VMEM((2, 4, 2, 256, 256), bf), pltpu.VMEM((2, 4, 2, 256, 256), bf)]),
        compiler_params=pltpu.CompilerParams(vmem_limit_bytes=VMEM_LIMIT),
        cost_estimate=pl.CostEstimate(flops=32 * 2**29, bytes_accessed=100 * 2**20, transcendentals=0),
    )(off, spec, right, lower, corner, probe, tab)


def backward(off, probe, tab, amp, far, pat, inten, sources):
    return pl.pallas_call(
        backward_kernel,
        out_shape=[like((2, 512, 1024), f32), like((2, 256, 1024), bf), like((2, 512, 256), bf), like((2, 256, 256), bf), like((2, 4, 256, 256), f32)],
        grid_spec=pltpu.PrefetchScalarGridSpec(
            num_scalar_prefetch=1, grid=(sources,),
            in_specs=[whole(2, 4, 256, 256), whole(8, 256, 256), each(2, 256, 256), each(2, 4, 2, 2, 128, 256), each(2, 2, 256, 256), each(2, 2, 128, 256)],
            out_specs=[whole(2, 512, 1024), whole(2, 256, 1024), whole(2, 512, 256), whole(2, 256, 256), whole(2, 4, 256, 256)],
            scratch_shapes=[pltpu.VMEM((2, 10, 768, 128), f32), pltpu.VMEM((2, 2, 128, 256), f32), pltpu.VMEM((2, 4, 2, 256, 256), bf),
                            pltpu.VMEM((2, 4, 2, 256, 256), bf), pltpu.VMEM((2, 2, 256, 256), f32)]),
        compiler_params=pltpu.CompilerParams(vmem_limit_bytes=VMEM_LIMIT),
        cost_estimate=pl.CostEstimate(flops=32 * 2**29, bytes_accessed=100 * 2**20, transcendentals=0),
    )(off, probe, tab, amp, far, pat, inten)


def spread(axis, size, reach):
    lax.fori_loop(1, size, lambda d, c: (reach(d), c)[1], 0)


def beyond(axis, d, size):
    place = {"ty": lax.axis_index("ty"), "tx": lax.axis_index("tx")}
    place[axis] = lax.rem(place[axis] + d, size)
    return (place["ty"], place["tx"])


def gather_kernel(n_ty, own, out, send, recv):
    me = lax.axis_index("ty")
    barrier = pltpu.get_barrier_semaphore()
    spread("ty", n_ty, lambda d: pl.semaphore_signal(barrier, inc=1, device_id=beyond("ty", d, n_ty), device_id_type=MESH))
    pl.semaphore_wait(barrier, n_ty - 1)

    def copy(d):
        return pltpu.make_async_remote_copy(
            src_ref=own, dst_ref=out.at[me], send_sem=send.at[d], recv_sem=recv.at[d],
            device_id=beyond("ty", d, n_ty), device_id_type=MESH)

    spread("ty", n_ty, lambda d: copy(d).start())
    out[me] = own[...]
    spread("ty", n_ty, lambda d: copy(d).wait())


def gather_offsets(offsets, n_ty):
    own = jnp.zeros((8, 128), jnp.int32).at[0, : 2 * POS].set(offsets)
    out = pl.pallas_call(
        functools.partial(gather_kernel, n_ty),
        out_shape=like((n_ty, 8, 128), jnp.int32),
        in_specs=[pl.BlockSpec(memory_space=pltpu.VMEM)],
        out_specs=pl.BlockSpec(memory_space=pltpu.VMEM),
        scratch_shapes=[pltpu.SemaphoreType.DMA((n_ty,)), pltpu.SemaphoreType.DMA((n_ty,))],
        compiler_params=pltpu.CompilerParams(collective_id=0, has_side_effects=True),
    )(own)
    return out[:, 0, : 2 * POS].reshape(-1)


def finish_kernel(n_ty, n_tx, scale, total, down, right, corner, probe_o, down_o, right_o, corner_o,
                  cast, rax, ray, sx, sy, rbx, rby, gx, gy, hx, hy, send_ty, recv_ty, send_tx, recv_tx, send_h, recv_h):
    ty, tx = lax.axis_index("ty"), lax.axis_index("tx")
    nx, ny = 1024 // n_tx, 1024 // n_ty
    barrier = pltpu.get_barrier_semaphore()

    def greet(device):
        pl.semaphore_signal(barrier, inc=1, device_id=device, device_id_type=MESH)

    spread("ty", n_ty, lambda d: greet(beyond("ty", d, n_ty)))
    spread("tx", n_tx, lambda d: greet(beyond("tx", d, n_tx)))
    greet((lax.rem(ty + n_ty - 1, n_ty), lax.rem(tx + n_tx - 1, n_tx)))
    cast[...] = total[...].astype(bf)
    pl.semaphore_wait(barrier, n_ty + n_tx - 1)

    def over_ty(stage, d, src, dst):
        return pltpu.make_async_remote_copy(
            src_ref=src, dst_ref=dst, send_sem=send_ty.at[stage, d], recv_sem=recv_ty.at[stage, d],
            device_id=beyond("ty", d, n_ty), device_id_type=MESH)

    def over_tx(stage, d, src, dst):
        return pltpu.make_async_remote_copy(
            src_ref=src, dst_ref=dst, send_sem=send_tx.at[stage, d], recv_sem=recv_tx.at[stage, d],
            device_id=beyond("tx", d, n_tx), device_id_type=MESH)

    def rows(k, n):
        return pl.ds(pl.multiple_of(k * n, 8), n)

    def halo(k, src, dst, device):
        return pltpu.make_async_remote_copy(
            src_ref=src, dst_ref=dst, send_sem=send_h.at[k], recv_sem=recv_h.at[k], device_id=device, device_id_type=MESH)

    below, beside = lax.rem(ty + 1, n_ty), lax.rem(tx + 1, n_tx)
    halos = [halo(0, down, down_o, (below, tx)), halo(1, right, right_o, (ty, beside)), halo(2, corner, corner_o, (below, beside))]

    def ax(d):
        peer = lax.rem(tx + d, n_tx)
        return over_tx(0, d, cast.at[0, rows(peer, nx)], rax.at[d])

    def ay(d):
        peer = lax.rem(ty + d, n_ty)
        return over_ty(0, d, cast.at[1, rows(peer, ny)], ray.at[d])

    spread("tx", n_tx, lambda d: ax(d).start())
    spread("ty", n_ty, lambda d: ay(d).start())
    for h in halos:
        h.start()
    spread("tx", n_tx, lambda d: ax(d).wait())
    sx[...] = lax.fori_loop(1, n_tx, lambda d, t: t + rax[d].astype(f32), total[0, rows(tx, nx)])

    def bx(d):
        peer = lax.rem(ty + d, n_ty)
        return over_ty(1, d, sx.at[rows(peer, 8)], rbx.at[d])

    spread("ty", n_ty, lambda d: bx(d).start())
    spread("ty", n_ty, lambda d: ay(d).wait())
    sy[...] = lax.fori_loop(1, n_ty, lambda d, t: t + ray[d].astype(f32), total[1, rows(ty, ny)])

    def by(d):
        peer = lax.rem(tx + d, n_tx)
        return over_tx(1, d, sy.at[rows(peer, 8)], rby.at[d])

    spread("tx", n_tx, lambda d: by(d).start())
    spread("ty", n_ty, lambda d: bx(d).wait())
    gx[rows(ty, 8)] = scale * lax.fori_loop(1, n_ty, lambda d, t: t + rbx[d], sx[rows(ty, 8)])

    def cx(d):
        return over_ty(2, d, gx.at[rows(ty, 8)], gx.at[rows(ty, 8)])

    spread("ty", n_ty, lambda d: cx(d).start())
    spread("tx", n_tx, lambda d: by(d).wait())
    gy[rows(tx, 8)] = scale * lax.fori_loop(1, n_tx, lambda d, t: t + rby[d], sy[rows(tx, 8)])

    def cy(d):
        return over_tx(2, d, gy.at[rows(tx, 8)], gy.at[rows(tx, 8)])

    spread("tx", n_tx, lambda d: cy(d).start())
    spread("ty", n_ty, lambda d: cx(d).wait())
    hx[...] = gx[...].astype(bf)

    def dx(d):
        return over_tx(3, d, hx, probe_o.at[0, rows(tx, nx)])

    spread("tx", n_tx, lambda d: dx(d).start())
    probe_o[0, rows(tx, nx)] = hx[...]
    spread("tx", n_tx, lambda d: cy(d).wait())
    hy[...] = gy[...].astype(bf)

    def dy(d):
        return over_ty(3, d, hy, probe_o.at[1, rows(ty, ny)])

    spread("ty", n_ty, lambda d: dy(d).start())
    probe_o[1, rows(ty, ny)] = hy[...]
    spread("tx", n_tx, lambda d: dx(d).wait())
    spread("ty", n_ty, lambda d: dy(d).wait())
    for h in halos:
        h.wait()


def finish(total, down, right, corner, scale, n_ty, n_tx):
    nx, ny = 1024 // n_tx, 1024 // n_ty
    vmem = pl.BlockSpec(memory_space=pltpu.VMEM)
    hbm = pl.BlockSpec(memory_space=pl.ANY)
    dma = pltpu.SemaphoreType.DMA
    return pl.pallas_call(
        functools.partial(finish_kernel, n_ty, n_tx, scale),
        out_shape=[like((2, 1024, N), bf), like(down.shape, bf), like(right.shape, bf), like(corner.shape, bf)],
        in_specs=[vmem, hbm, hbm, hbm],
        out_specs=[vmem, hbm, hbm, hbm],
        scratch_shapes=[
            pltpu.VMEM((2, 1024, N), bf), pltpu.VMEM((n_tx, nx, N), bf), pltpu.VMEM((n_ty, ny, N), bf),
            pltpu.VMEM((nx, N), f32), pltpu.VMEM((ny, N), f32), pltpu.VMEM((n_ty, 8, N), f32), pltpu.VMEM((n_tx, 8, N), f32),
            pltpu.VMEM((nx, N), f32), pltpu.VMEM((ny, N), f32), pltpu.VMEM((nx, N), bf), pltpu.VMEM((ny, N), bf),
            dma((4, n_ty)), dma((4, n_ty)), dma((4, n_tx)), dma((4, n_tx)), dma((3,)), dma((3,))],
        compiler_params=pltpu.CompilerParams(collective_id=1, has_side_effects=True, vmem_limit_bytes=VMEM_LIMIT),
    )(total.reshape(2, 1024, N), down, right, corner)


def shift(value, d_ty, d_tx, n_ty, n_tx):
    pairs = []
    for y in range(n_ty):
        for x in range(n_tx):
            if 0 <= y + d_ty < n_ty and 0 <= x + d_tx < n_tx:
                pairs.append((y * n_tx + x, (y + d_ty) * n_tx + x + d_tx))
    return lax.ppermute(value, ("ty", "tx"), pairs)


def on_device(specimen, probe, amplitude, offsets):
    n_ty, n_tx = lax.axis_size("ty"), lax.axis_size("tx")
    positions = offsets.shape[0] * n_ty * n_tx
    right = shift(specimen[:, :, :N].astype(bf), 0, -1, n_ty, n_tx)
    lower = shift(specimen[:, :N, :].astype(bf), -1, 0, n_ty, n_tx)
    corner = shift(specimen[:, :N, :N].astype(bf), -1, -1, n_ty, n_tx)
    own = offsets.reshape(-1)
    slots = prepare(own, amplitude, n_ty)
    arrived = lax.all_to_all(slots, "ty", split_axis=0, concat_axis=0, tiled=True)
    everyone = gather_offsets(own, n_ty)
    tables = make_tables()
    arranged = arrange(probe)
    far, pat, inten = forward(everyone, specimen, right, lower, corner, arranged, tables, n_ty)
    main, down, rt, cn, total = backward(everyone, arranged, tables, arrived, far, pat, inten, n_ty)
    scale = float(probe.shape[1] / np.sqrt(positions))
    probe_grad, down, rt, cn = finish(total, down, rt, cn, scale, n_ty, n_tx)
    main = main.at[:, :N, :].add(down.astype(f32)).at[:, :, :N].add(rt.astype(f32)).at[:, :N, :N].add(cn.astype(f32))
    return (main, restore(probe_grad.reshape(probe.shape)).astype(f32))


def solution(mesh):
    in_specs = (P(None, "ty", "tx"), P(), P(("ty", "tx"), None, None), P(("ty", "tx"), None))
    out_specs = (P(None, "ty", "tx"), P())
    return jax.shard_map(on_device, mesh=mesh, in_specs=in_specs, out_specs=out_specs, check_vma=False)
```

```python
import functools

import jax
import jax.numpy as jnp
import ml_dtypes
import numpy as np
from jax import lax
from jax.experimental import pallas as pl
from jax.experimental.pallas import tpu as pltpu
from jax.sharding import PartitionSpec as P

bf = jnp.bfloat16
f32 = jnp.float32
N = 256
H = 128
TILE_R = 512
TILE_C = 1024
POS = 12
VMEM_LIMIT = 60 * 2**20
ROWS = 2048
PIECES = 4
MESH = pl.DeviceIdType.MESH
S = 2
B = 16 // S

def row0(i):
    return i // S * 8 * S + i % S

def make_tables():
    k = np.arange(N)
    ang = ((k[:, None] * k[None, :]) % N).astype(np.float64) * (2 * np.pi / N)
    re = (np.cos(ang) / 16).astype(np.float32).astype(ml_dtypes.bfloat16).astype(np.float32)
    im = (-np.sin(ang) / 16).astype(np.float32).astype(ml_dtypes.bfloat16).astype(np.float32)
    order = np.arange(128).reshape(B, 8, S).swapaxes(1, 2).reshape(-1)
    def mix(a, b):
        return np.stack([a.reshape(16, 8, -1), b.reshape(16, 8, -1)], 1).reshape(256, -1)
    out = []
    for par in (0, 1):
        r, i = re[:H, par::2], im[:H, par::2]
        out.append(np.block([[r, i], [-i, r]]))
    for par in (0, 1):
        r, i = re[par::2][:, order], im[par::2][:, order]
        out.append(mix(np.block([r, -i]), np.block([i, r])))
    for par in (0, 1):
        r, i = re[par::2, :H], -im[par::2, :H]
        out.append(np.block([[r, i], [-i, r]]))
    for par in (0, 1):
        r, i = re[order][:, par::2], -im[order][:, par::2]
        out.append(mix(np.block([r, -i]), np.block([i, r])))
    return np.stack(out).astype(ml_dtypes.bfloat16)

def arrange(x):
    lead = x.shape[:-2]
    x = x.reshape(*lead, 2, B, 8, S, x.shape[-1])
    k = len(lead)
    return jnp.transpose(x, (*range(k), k + 1, k + 3, k, k + 2, k + 4)).reshape(*lead, 256, x.shape[-1])

def restore(x):
    lead = x.shape[:-2]
    x = x.reshape(*lead, B, S, 2, 8, x.shape[-1])
    k = len(lead)
    return jnp.transpose(x, (*range(k), k + 2, k, k + 3, k + 1, k + 4)).reshape(*lead, 256, x.shape[-1])

def dot(a, b):
    return jnp.dot(a, b, preferred_element_type=f32)

def halves(x):
    x = x.reshape(16, 2, 8, x.shape[-1])
    return x[:, 0].reshape(128, x.shape[-1]), x[:, 1].reshape(128, x.shape[-1])


def parity_matrix():
    order = np.concatenate([np.arange(0, N, 2), np.arange(1, N, 2)])
    return np.eye(N)[order].astype(ml_dtypes.bfloat16)


def prep_kernel(off, amp, perm, out, buf, sem):
    copies = []
    for i in range(POS):
        a = dot(perm[...], amp[i].astype(bf)).astype(bf)
        buf[i] = lax.dot_general(a, perm[...], (((1,), (1,)), ((), ())), preferred_element_type=f32).astype(bf)
        tile = off[2 * i] // TILE_R
        rank = jnp.int32(0)
        for j in range(i):
            rank = rank + (off[2 * j] // TILE_R == tile).astype(jnp.int32)
        copies.append(pltpu.make_async_copy(buf.at[i], out.at[tile, rank], sem.at[i]))
        copies[i].start()
    for copy in copies:
        copy.wait()


def prepare(off, amplitude, sources):
    return pl.pallas_call(
        prep_kernel,
        out_shape=jax.ShapeDtypeStruct((sources, 2, N, N), bf),
        in_specs=[pl.BlockSpec(memory_space=pltpu.SMEM), pl.BlockSpec(memory_space=pltpu.VMEM), pl.BlockSpec(memory_space=pltpu.VMEM)],
        out_specs=pl.BlockSpec(memory_space=pl.ANY),
        scratch_shapes=[pltpu.VMEM((POS, N, N), bf), pltpu.SemaphoreType.DMA((POS,))],
        compiler_params=pltpu.CompilerParams(vmem_limit_bytes=VMEM_LIMIT),
    )(off, amplitude, parity_matrix())


def find(off, source, tile):
    rows, cols = [jnp.int32(-1)] * 2, [jnp.int32(0)] * 2
    seen = jnp.int32(0)
    for i in range(POS):
        base = (source * POS + i) * 2
        r, c = off[base], off[base + 1]
        mine = r // TILE_R == tile
        for q in range(2):
            take = mine & (seen == q)
            rows[q] = jnp.where(take, r % TILE_R, rows[q])
            cols[q] = jnp.where(take, c % TILE_C, cols[q])
        seen = seen + mine.astype(jnp.int32)
    return rows, cols


def p1(probe, pat, A):
    pr, pi = probe[0], probe[1]
    qr, qi = pat[0], pat[1]
    er = pr * qr - pi * qi
    ei = pr * qi + pi * qr
    A[0, :, :H] = (er[:, :H] + er[:, H:]).astype(bf)
    A[0, :, H:] = (ei[:, :H] + ei[:, H:]).astype(bf)
    A[1, :, :H] = (er[:, :H] - er[:, H:]).astype(bf)
    A[1, :, H:] = (ei[:, :H] - ei[:, H:]).astype(bf)


def p2(tab, A, Bb):
    for p in (0, 1):
        t, b = halves(dot(A[p], tab[p]))
        s = (t + b).astype(bf)
        d = (t - b).astype(bf)
        ls = slice(p * H, p * H + H)
        Bb[0, :H, ls] = s[:, :H]
        Bb[0, H:, ls] = s[:, H:]
        Bb[1, :H, ls] = d[:, :H]
        Bb[1, H:, ls] = d[:, H:]


def p3(first, tab, Bb, far, inten):
    for p in (0, 1):
        r, i = halves(dot(tab[2 + p], Bb[p]))
        far[p, 0] = r
        far[p, 1] = i
        t = r * r + i * i
        inten[p] = t if first else inten[p] + t


def p4(amp, inten, fac):
    for p in (0, 1):
        a = amp[p * H:(p + 1) * H].astype(f32)
        fac[p] = 1.0 - a * lax.rsqrt(jnp.maximum(inten[p], 0.25))


def p5(far, fac, C):
    for p in (0, 1):
        f = fac[p]
        rr = (far[p, 0] * f).astype(bf)
        ri = (far[p, 1] * f).astype(bf)
        rs = slice(p * H, p * H + H)
        C[0, rs, :H] = rr[:, :H]
        C[0, rs, H:] = ri[:, :H]
        C[1, rs, :H] = rr[:, H:]
        C[1, rs, H:] = ri[:, H:]


def p6(tab, C, G):
    e = dot(C[0], tab[4])
    o = dot(C[1], tab[5])
    s = (e + o).astype(bf)
    d = (e - o).astype(bf)
    for p in (0, 1):
        rs = slice(p * H, p * H + H)
        G[p, :H, :H] = s[rs, :H]
        G[p, :H, H:] = d[rs, :H]
        G[p, H:, :H] = s[rs, H:]
        G[p, H:, H:] = d[rs, H:]


def both(a, b):
    return jnp.stack([a.reshape(16, 8, 256), b.reshape(16, 8, 256)], 1).reshape(256, 256)


def p7(first, tab, G, probe, pat, grad, total, m):
    er, ei = halves(dot(tab[6], G[0]))
    r_, i_ = halves(dot(tab[7], G[1]))
    br = both(er + r_, er - r_)
    bi = both(ei + i_, ei - i_)
    pr, pi = probe[0], probe[1]
    qr, qi = pat[0], pat[1]
    gr = pr * br + pi * bi
    gi = pr * bi - pi * br
    grad[0] = gr if first else grad[0] + gr
    grad[1] = gi if first else grad[1] + gi
    total[0, m] += qr * br + qi * bi
    total[1, m] += qr * bi - qi * br


def fetch(ext, pat, r, c):
    ct = c // 128
    sh = c % 128
    lane = lax.broadcasted_iota(jnp.int32, (128, 128), 1)
    keep = lane < 128 - sh
    for k in (0, 1):
        for h in (0, 1):
            x = []
            for t in range(3):
                v = jnp.concatenate([ext[k, ct + t, pl.ds(r + 128 * h + row0(i), 8, stride=S)] for i in range(16)], axis=0)
                x.append(pltpu.roll(v, 128 - sh, axis=1))
            for t in (0, 1):
                y = jnp.where(keep, x[t], x[t + 1])
                for i in range(16):
                    pat[k, 16 * i + 8 * h:16 * i + 8 * h + 8, t * H:t * H + H] = y[8 * i:8 * i + 8]

def deposit(grid, grad, r, c):
    ct = c // 128
    sh = c % 128
    lane = lax.broadcasted_iota(jnp.int32, (256, 128), 1)
    keep = lane >= sh
    for k in (0, 1):
        x = grad[k].astype(bf).astype(f32)
        a = pltpu.roll(x[:, :H], sh, axis=1)
        b = pltpu.roll(x[:, H:], sh, axis=1)
        z = jnp.zeros_like(a)
        for t, y in enumerate((jnp.where(keep, a, z), jnp.where(keep, b, a), jnp.where(keep, z, b))):
            for i in range(16):
                for h in (0, 1):
                    ds = pl.ds(r + 128 * h + row0(i), 8, stride=S)
                    grid[k, ct + t, ds] = grid[k, ct + t, ds] + y[16 * i + 8 * h:16 * i + 8 * h + 8]


def forward_kernel(off, spec, right, lower, corner, probe, tab, far, pat, inten, ext, A, Bb):
    s = pl.program_id(0)

    @pl.when(s == 0)
    def _():
        for c in (0, 1):
            for t in range(10):
                ls = slice(t * H, t * H + H)
                l2 = slice(t * H - 1024, t * H - 1024 + H)
                ext[c, t, :512] = (spec[c, :, ls] if t < 8 else right[c, :, l2]).astype(bf).astype(f32)
                ext[c, t, 512:] = (lower[c, :, ls] if t < 8 else corner[c, :, l2]).astype(f32)

    rows, cols = find(off, s, lax.axis_index("ty"))

    @pl.when(rows[0] >= 0)
    def _():
        items = [(q, m) for q in range(2) for m in range(4)]
        for t in range(len(items) + 2):
            if 0 <= t - 1 < len(items):
                q, m = items[t - 1]
                p2(tab, A.at[q, m], Bb.at[q, m])
            if 0 <= t - 2 < len(items):
                q, m = items[t - 2]
                p3(m == 0, tab, Bb.at[q, m], far.at[0, q, m], inten.at[0, q])
            if t < len(items):
                q, m = items[t]
                if m == 0:
                    fetch(ext, pat.at[0, q], rows[q], cols[q])
                p1(probe.at[:, m], pat.at[0, q], A.at[q, m])


def backward_kernel(off, probe, tab, amp, far, pat, inten, main_o, down_o, right_o, corner_o, total_o, grid, total, fac, C, G, grad):
    s = pl.program_id(0)

    @pl.when(s == 0)
    def _():
        grid[...] = jnp.zeros_like(grid)
        total[...] = jnp.zeros_like(total)

    rows, cols = find(off, s, lax.axis_index("ty"))

    @pl.when(rows[0] >= 0)
    def _():
        items = [(q, m) for q in range(2) for m in range(4)]
        for t in range(len(items) + 2):
            if 0 <= t - 1 < len(items):
                q, m = items[t - 1]
                p6(tab, C.at[q, m], G.at[q, m])
            if 0 <= t - 2 < len(items):
                q, m = items[t - 2]
                p7(m == 0, tab, G.at[q, m], probe.at[:, m], pat.at[0, q], grad.at[q], total, m)
                if m == 3:
                    deposit(grid, grad.at[q], rows[q], cols[q])
            if t < len(items):
                q, m = items[t]
                if m == 0:
                    p4(amp.at[0, q], inten.at[0, q], fac.at[q])
                p5(far.at[0, q, m], fac.at[q], C.at[q, m])

    @pl.when(s == pl.num_programs(0) - 1)
    def _():
        for c in (0, 1):
            for t in range(10):
                ls = slice(t * H, t * H + H)
                l2 = slice(t * H - 1024, t * H - 1024 + H)
                if t < 8:
                    main_o[c, :, ls] = grid[c, t, :512]
                    down_o[c, :, ls] = grid[c, t, 512:].astype(bf)
                else:
                    right_o[c, :, l2] = grid[c, t, :512].astype(bf)
                    corner_o[c, :, l2] = grid[c, t, 512:].astype(bf)
            for m in range(4):
                for i in range(32):
                    for t in range(2):
                        ds = pl.ds(128 * (i % 2) + row0(i // 2), 8, stride=S)
                        total_o[c, m, t, ds] = total[c, m, 8 * i:8 * i + 8, t * H:t * H + H]


def whole(*shape):
    return pl.BlockSpec(shape, lambda i, o: (0,) * len(shape), pipeline_mode=pl.Buffered(1))


def each(*shape):
    return pl.BlockSpec((1, *shape), lambda i, o: (i,) + (0,) * len(shape))


def like(shape, dtype):
    return jax.ShapeDtypeStruct(shape, dtype)


def forward(off, spec, right, lower, corner, probe, tab, sources):
    return pl.pallas_call(
        forward_kernel,
        out_shape=[like((sources, 2, 4, 2, 2, 128, 256), f32), like((sources, 2, 2, 256, 256), f32), like((sources, 2, 2, 128, 256), f32)],
        grid_spec=pltpu.PrefetchScalarGridSpec(
            num_scalar_prefetch=1, grid=(sources,),
            in_specs=[whole(2, 512, 1024), whole(2, 512, 256), whole(2, 256, 1024), whole(2, 256, 256), whole(2, 4, 256, 256), whole(8, 256, 256)],
            out_specs=[each(2, 4, 2, 2, 128, 256), each(2, 2, 256, 256), each(2, 2, 128, 256)],
            scratch_shapes=[pltpu.VMEM((2, 10, 768, 128), f32), pltpu.VMEM((2, 4, 2, 256, 256), bf), pltpu.VMEM((2, 4, 2, 256, 256), bf)]),
        compiler_params=pltpu.CompilerParams(vmem_limit_bytes=VMEM_LIMIT),
        cost_estimate=pl.CostEstimate(flops=32 * 2**29, bytes_accessed=100 * 2**20, transcendentals=0),
    )(off, spec, right, lower, corner, probe, tab)


def backward(off, probe, tab, amp, far, pat, inten, sources):
    return pl.pallas_call(
        backward_kernel,
        out_shape=[like((2, 512, 1024), f32), like((2, 256, 1024), bf), like((2, 512, 256), bf), like((2, 256, 256), bf), like((2, 4, 2, 256, 128), f32)],
        grid_spec=pltpu.PrefetchScalarGridSpec(
            num_scalar_prefetch=1, grid=(sources,),
            in_specs=[whole(2, 4, 256, 256), whole(8, 256, 256), each(2, 256, 256), each(2, 4, 2, 2, 128, 256), each(2, 2, 256, 256), each(2, 2, 128, 256)],
            out_specs=[whole(2, 512, 1024), whole(2, 256, 1024), whole(2, 512, 256), whole(2, 256, 256), whole(2, 4, 2, 256, 128)],
            scratch_shapes=[pltpu.VMEM((2, 10, 768, 128), f32), pltpu.VMEM((2, 4, 256, 256), f32), pltpu.VMEM((2, 2, 128, 256), f32), pltpu.VMEM((2, 4, 2, 256, 256), bf),
                            pltpu.VMEM((2, 4, 2, 256, 256), bf), pltpu.VMEM((2, 2, 256, 256), f32)]),
        compiler_params=pltpu.CompilerParams(vmem_limit_bytes=VMEM_LIMIT),
        cost_estimate=pl.CostEstimate(flops=32 * 2**29, bytes_accessed=100 * 2**20, transcendentals=0),
    )(off, probe, tab, amp, far, pat, inten)


def spread(axis, size, reach):
    lax.fori_loop(1, size, lambda d, c: (reach(d), c)[1], 0)


def beyond(axis, d, size):
    place = {"ty": lax.axis_index("ty"), "tx": lax.axis_index("tx")}
    place[axis] = lax.rem(place[axis] + d, size)
    return (place["ty"], place["tx"])


def gather_kernel(n_ty, own, out, send, recv):
    me = lax.axis_index("ty")
    barrier = pltpu.get_barrier_semaphore()
    spread("ty", n_ty, lambda d: pl.semaphore_signal(barrier, inc=1, device_id=beyond("ty", d, n_ty), device_id_type=MESH))
    pl.semaphore_wait(barrier, n_ty - 1)

    def copy(d):
        return pltpu.make_async_remote_copy(
            src_ref=own, dst_ref=out.at[me], send_sem=send.at[d], recv_sem=recv.at[d],
            device_id=beyond("ty", d, n_ty), device_id_type=MESH)

    spread("ty", n_ty, lambda d: copy(d).start())
    out[me] = own[...]
    spread("ty", n_ty, lambda d: copy(d).wait())


def gather_offsets(offsets, n_ty):
    own = jnp.zeros((8, 128), jnp.int32).at[0, : 2 * POS].set(offsets)
    out = pl.pallas_call(
        functools.partial(gather_kernel, n_ty),
        out_shape=like((n_ty, 8, 128), jnp.int32),
        in_specs=[pl.BlockSpec(memory_space=pltpu.VMEM)],
        out_specs=pl.BlockSpec(memory_space=pltpu.VMEM),
        scratch_shapes=[pltpu.SemaphoreType.DMA((n_ty,)), pltpu.SemaphoreType.DMA((n_ty,))],
        compiler_params=pltpu.CompilerParams(collective_id=0, has_side_effects=True),
    )(own)
    return out[:, 0, : 2 * POS].reshape(-1)


def finish_kernel(n_ty, n_tx, scale, total, down, right, corner, probe_o, down_o, right_o, corner_o,
                  cast, rax, ray, sx, sy, rbx, rby, gx, gy, hx, hy, send_ty, recv_ty, send_tx, recv_tx, send_h, recv_h):
    ty, tx = lax.axis_index("ty"), lax.axis_index("tx")
    nx, ny, sub = ROWS // n_tx, ROWS // n_ty, ROWS // n_tx // n_ty
    barrier = pltpu.get_barrier_semaphore()

    def greet(device):
        pl.semaphore_signal(barrier, inc=1, device_id=device, device_id_type=MESH)

    spread("ty", n_ty, lambda d: greet(beyond("ty", d, n_ty)))
    spread("tx", n_tx, lambda d: greet(beyond("tx", d, n_tx)))
    greet((lax.rem(ty + n_ty - 1, n_ty), lax.rem(tx + n_tx - 1, n_tx)))
    cast[...] = total[...].astype(bf)
    pl.semaphore_wait(barrier, n_ty + n_tx - 1)

    def over_ty(stage, d, src, dst):
        return pltpu.make_async_remote_copy(
            src_ref=src, dst_ref=dst, send_sem=send_ty.at[stage, d], recv_sem=recv_ty.at[stage, d],
            device_id=beyond("ty", d, n_ty), device_id_type=MESH)

    def over_tx(stage, d, src, dst):
        return pltpu.make_async_remote_copy(
            src_ref=src, dst_ref=dst, send_sem=send_tx.at[stage, d], recv_sem=recv_tx.at[stage, d],
            device_id=beyond("tx", d, n_tx), device_id_type=MESH)

    def rows(k, n):
        return pl.ds(pl.multiple_of(k * n, 16), n)

    def halo(k, src, dst, device):
        return pltpu.make_async_remote_copy(
            src_ref=src, dst_ref=dst, send_sem=send_h.at[k], recv_sem=recv_h.at[k], device_id=device, device_id_type=MESH)

    below, beside = lax.rem(ty + 1, n_ty), lax.rem(tx + 1, n_tx)
    part = N // PIECES
    pieces = [halo(k, down.at[:, k * part:k * part + part], down_o.at[:, k * part:k * part + part], (below, tx)) for k in range(PIECES)]
    halos = pieces + [halo(PIECES, right, right_o, (ty, beside)), halo(PIECES + 1, corner, corner_o, (below, beside))]

    def ax(d):
        peer = lax.rem(tx + d, n_tx)
        return over_tx(0, d, cast.at[0, rows(peer, nx)], rax.at[d])

    def ay(d):
        peer = lax.rem(ty + d, n_ty)
        return over_ty(0, d, cast.at[1, rows(peer, ny)], ray.at[d])

    spread("tx", n_tx, lambda d: ax(d).start())
    spread("ty", n_ty, lambda d: ay(d).start())
    halos[0].start()
    spread("tx", n_tx, lambda d: ax(d).wait())
    sx[...] = lax.fori_loop(1, n_tx, lambda d, t: t + rax[d].astype(f32), total[0, rows(tx, nx)])

    def bx(d):
        peer = lax.rem(ty + d, n_ty)
        return over_ty(1, d, sx.at[rows(peer, sub)], rbx.at[d])

    spread("ty", n_ty, lambda d: bx(d).start())
    spread("ty", n_ty, lambda d: ay(d).wait())
    sy[...] = lax.fori_loop(1, n_ty, lambda d, t: t + ray[d].astype(f32), total[1, rows(ty, ny)])

    def by(d):
        peer = lax.rem(tx + d, n_tx)
        return over_tx(1, d, sy.at[rows(peer, sub)], rby.at[d])

    spread("tx", n_tx, lambda d: by(d).start())
    halos[1].start()
    spread("ty", n_ty, lambda d: bx(d).wait())
    gx[rows(ty, sub)] = scale * lax.fori_loop(1, n_ty, lambda d, t: t + rbx[d], sx[rows(ty, sub)])

    def cx(d):
        return over_ty(2, d, gx.at[rows(ty, sub)], gx.at[rows(ty, sub)])

    spread("ty", n_ty, lambda d: cx(d).start())
    spread("tx", n_tx, lambda d: by(d).wait())
    gy[rows(tx, sub)] = scale * lax.fori_loop(1, n_tx, lambda d, t: t + rby[d], sy[rows(tx, sub)])

    def cy(d):
        return over_tx(2, d, gy.at[rows(tx, sub)], gy.at[rows(tx, sub)])

    spread("tx", n_tx, lambda d: cy(d).start())
    halos[2].start()
    spread("ty", n_ty, lambda d: cx(d).wait())
    hx[...] = gx[...].astype(bf)

    def dx(d):
        return over_tx(3, d, hx, probe_o.at[0, rows(tx, nx)])

    spread("tx", n_tx, lambda d: dx(d).start())
    probe_o[0, rows(tx, nx)] = hx[...]
    spread("tx", n_tx, lambda d: cy(d).wait())
    hy[...] = gy[...].astype(bf)

    def dy(d):
        return over_ty(3, d, hy, probe_o.at[1, rows(ty, ny)])

    spread("ty", n_ty, lambda d: dy(d).start())
    for h in halos[3:]:
        h.start()
    probe_o[1, rows(ty, ny)] = hy[...]
    spread("tx", n_tx, lambda d: dx(d).wait())
    spread("ty", n_ty, lambda d: dy(d).wait())
    for h in halos:
        h.wait()


def finish(total, down, right, corner, scale, n_ty, n_tx):
    nx, ny, sub = ROWS // n_tx, ROWS // n_ty, ROWS // n_tx // n_ty
    vmem = pl.BlockSpec(memory_space=pltpu.VMEM)
    hbm = pl.BlockSpec(memory_space=pl.ANY)
    dma = pltpu.SemaphoreType.DMA
    return pl.pallas_call(
        functools.partial(finish_kernel, n_ty, n_tx, scale),
        out_shape=[like((2, ROWS, H), bf), like(down.shape, bf), like(right.shape, bf), like(corner.shape, bf)],
        in_specs=[vmem, hbm, hbm, hbm],
        out_specs=[vmem, hbm, hbm, hbm],
        scratch_shapes=[
            pltpu.VMEM((2, ROWS, H), bf), pltpu.VMEM((n_tx, nx, H), bf), pltpu.VMEM((n_ty, ny, H), bf),
            pltpu.VMEM((nx, H), f32), pltpu.VMEM((ny, H), f32), pltpu.VMEM((n_ty, sub, H), f32), pltpu.VMEM((n_tx, sub, H), f32),
            pltpu.VMEM((nx, H), f32), pltpu.VMEM((ny, H), f32), pltpu.VMEM((nx, H), bf), pltpu.VMEM((ny, H), bf),
            dma((4, n_ty)), dma((4, n_ty)), dma((4, n_tx)), dma((4, n_tx)), dma((PIECES + 2,)), dma((PIECES + 2,))],
        compiler_params=pltpu.CompilerParams(collective_id=1, has_side_effects=True, vmem_limit_bytes=VMEM_LIMIT),
    )(total.reshape(2, ROWS, H), down, right, corner)


def shift(value, d_ty, d_tx, n_ty, n_tx):
    pairs = []
    for y in range(n_ty):
        for x in range(n_tx):
            if 0 <= y + d_ty < n_ty and 0 <= x + d_tx < n_tx:
                pairs.append((y * n_tx + x, (y + d_ty) * n_tx + x + d_tx))
    return lax.ppermute(value, ("ty", "tx"), pairs)


def on_device(specimen, probe, amplitude, offsets):
    n_ty, n_tx = lax.axis_size("ty"), lax.axis_size("tx")
    positions = offsets.shape[0] * n_ty * n_tx
    own = offsets.reshape(-1)
    half = (specimen[:, :, :N].astype(bf), specimen[:, :N, :].astype(bf))
    everyone = gather_offsets(own, n_ty)
    everyone, (side, top) = lax.optimization_barrier((everyone, half))
    lower = shift(top, -1, 0, n_ty, n_tx)
    right = shift(side, 0, -1, n_ty, n_tx)
    corner = shift(top[:, :, :N], -1, -1, n_ty, n_tx)
    slots = prepare(own, amplitude, n_ty)
    slots, everyone = lax.optimization_barrier((slots, everyone))
    arrived = lax.all_to_all(slots, "ty", split_axis=0, concat_axis=0, tiled=True)
    tables = make_tables()
    arranged = arrange(probe)
    far, pat, inten = forward(everyone, specimen, right, lower, corner, arranged, tables, n_ty)
    main, down, rt, cn, total = backward(everyone, arranged, tables, arrived, far, pat, inten, n_ty)
    scale = float(probe.shape[1] / np.sqrt(positions))
    probe_grad, down, rt, cn = finish(total, down, rt, cn, scale, n_ty, n_tx)

    def spot(piece):
        rows, cols = TILE_R - piece.shape[1], TILE_C - piece.shape[2]
        return jnp.pad(piece.astype(f32), ((0, 0), (0, rows), (0, cols)))

    object_grad = main + spot(down) + spot(rt) + spot(cn)
    probe_grad = jnp.swapaxes(probe_grad.reshape(2, 4, 2, N, H), 2, 3).reshape(probe.shape).astype(f32)
    return (object_grad, probe_grad)


def solution(mesh):
    in_specs = (P(None, "ty", "tx"), P(), P(("ty", "tx"), None, None), P(("ty", "tx"), None))
    out_specs = (P(None, "ty", "tx"), P())
    return jax.shard_map(on_device, mesh=mesh, in_specs=in_specs, out_specs=out_specs, check_vma=False)
```

```python
import functools

import jax
import jax.numpy as jnp
import ml_dtypes
import numpy as np
from jax import lax
from jax.experimental import pallas as pl
from jax.experimental.pallas import tpu as pltpu
from jax.sharding import PartitionSpec as P

bf = jnp.bfloat16
f32 = jnp.float32
N = 256
H = 128
TILE_R = 512
TILE_C = 1024
POS = 12
VMEM_LIMIT = 60 * 2**20
ROWS = 2048
PIECES = 4
MESH = pl.DeviceIdType.MESH
S = 2
B = 16 // S

def row0(i):
    return i // S * 8 * S + i % S

def make_tables():
    k = np.arange(N)
    ang = ((k[:, None] * k[None, :]) % N).astype(np.float64) * (2 * np.pi / N)
    re = (np.cos(ang) / 16).astype(np.float32).astype(ml_dtypes.bfloat16).astype(np.float32)
    im = (-np.sin(ang) / 16).astype(np.float32).astype(ml_dtypes.bfloat16).astype(np.float32)
    order = np.arange(128).reshape(B, 8, S).swapaxes(1, 2).reshape(-1)
    def mix(a, b):
        return np.stack([a.reshape(16, 8, -1), b.reshape(16, 8, -1)], 1).reshape(256, -1)
    out = []
    for par in (0, 1):
        r, i = re[:H, par::2], im[:H, par::2]
        out.append(np.block([[r, i], [-i, r]]))
    for par in (0, 1):
        r, i = re[par::2][:, order], im[par::2][:, order]
        out.append(mix(np.block([r, -i]), np.block([i, r])))
    for par in (0, 1):
        r, i = re[par::2, :H], -im[par::2, :H]
        out.append(np.block([[r, i], [-i, r]]))
    for par in (0, 1):
        r, i = re[order][:, par::2], -im[order][:, par::2]
        out.append(mix(np.block([r, -i]), np.block([i, r])))
    return np.stack(out).astype(ml_dtypes.bfloat16)

def dot(a, b):
    return jnp.dot(a, b, preferred_element_type=f32)

def halves(x):
    x = x.reshape(16, 2, 8, x.shape[-1])
    return x[:, 0].reshape(128, x.shape[-1]), x[:, 1].reshape(128, x.shape[-1])


def parity_matrix():
    order = np.concatenate([np.arange(0, N, 2), np.arange(1, N, 2)])
    return np.eye(N)[order].astype(ml_dtypes.bfloat16)


def prep_kernel(off, amp, perm, out, buf, sem):
    copies = []
    for i in range(POS):
        a = dot(perm[...], amp[i].astype(bf)).astype(bf)
        buf[i] = lax.dot_general(a, perm[...], (((1,), (1,)), ((), ())), preferred_element_type=f32).astype(bf)
        tile = off[2 * i] // TILE_R
        rank = jnp.int32(0)
        for j in range(i):
            rank = rank + (off[2 * j] // TILE_R == tile).astype(jnp.int32)
        copies.append(pltpu.make_async_copy(buf.at[i], out.at[tile, rank], sem.at[i]))
        copies[i].start()
    for copy in copies:
        copy.wait()


def prepare(off, amplitude, sources):
    return pl.pallas_call(
        prep_kernel,
        out_shape=jax.ShapeDtypeStruct((sources, 2, N, N), bf),
        in_specs=[pl.BlockSpec(memory_space=pltpu.SMEM), pl.BlockSpec(memory_space=pltpu.VMEM), pl.BlockSpec(memory_space=pltpu.VMEM)],
        out_specs=pl.BlockSpec(memory_space=pl.ANY),
        scratch_shapes=[pltpu.VMEM((POS, N, N), bf), pltpu.SemaphoreType.DMA((POS,))],
        compiler_params=pltpu.CompilerParams(vmem_limit_bytes=VMEM_LIMIT),
    )(off, amplitude, parity_matrix())


def find(off, source, tile):
    rows, cols = [jnp.int32(-1)] * 2, [jnp.int32(0)] * 2
    seen = jnp.int32(0)
    for i in range(POS):
        base = (source * POS + i) * 2
        r, c = off[base], off[base + 1]
        mine = r // TILE_R == tile
        for q in range(2):
            take = mine & (seen == q)
            rows[q] = jnp.where(take, r % TILE_R, rows[q])
            cols[q] = jnp.where(take, c % TILE_C, cols[q])
        seen = seen + mine.astype(jnp.int32)
    return rows, cols


def p1(probe, pat, A):
    pr, pi = probe[0], probe[1]
    qr, qi = pat[0], pat[1]
    er = pr * qr - pi * qi
    ei = pr * qi + pi * qr
    A[0, :, :H] = (er[:, :H] + er[:, H:]).astype(bf)
    A[0, :, H:] = (ei[:, :H] + ei[:, H:]).astype(bf)
    A[1, :, :H] = (er[:, :H] - er[:, H:]).astype(bf)
    A[1, :, H:] = (ei[:, :H] - ei[:, H:]).astype(bf)


def p2(tab, A, Bb):
    for p in (0, 1):
        t, b = halves(dot(A[p], tab[p]))
        s = (t + b).astype(bf)
        d = (t - b).astype(bf)
        ls = slice(p * H, p * H + H)
        Bb[0, :H, ls] = s[:, :H]
        Bb[0, H:, ls] = s[:, H:]
        Bb[1, :H, ls] = d[:, :H]
        Bb[1, H:, ls] = d[:, H:]


def p3(first, tab, Bb, far, inten):
    for p in (0, 1):
        r, i = halves(dot(tab[2 + p], Bb[p]))
        far[p, 0] = r
        far[p, 1] = i
        t = r * r + i * i
        inten[p] = t if first else inten[p] + t


def p4(amp, inten, fac):
    for p in (0, 1):
        a = amp[p * H:(p + 1) * H].astype(f32)
        fac[p] = 1.0 - a * lax.rsqrt(jnp.maximum(inten[p], 0.25))


def p5(far, fac, C):
    for p in (0, 1):
        f = fac[p]
        rr = (far[p, 0] * f).astype(bf)
        ri = (far[p, 1] * f).astype(bf)
        rs = slice(p * H, p * H + H)
        C[0, rs, :H] = rr[:, :H]
        C[0, rs, H:] = ri[:, :H]
        C[1, rs, :H] = rr[:, H:]
        C[1, rs, H:] = ri[:, H:]


def p6(tab, C, G):
    e = dot(C[0], tab[4])
    o = dot(C[1], tab[5])
    s = (e + o).astype(bf)
    d = (e - o).astype(bf)
    for p in (0, 1):
        rs = slice(p * H, p * H + H)
        G[p, :H, :H] = s[rs, :H]
        G[p, :H, H:] = d[rs, :H]
        G[p, H:, :H] = s[rs, H:]
        G[p, H:, H:] = d[rs, H:]


def both(a, b):
    return jnp.stack([a.reshape(16, 8, 256), b.reshape(16, 8, 256)], 1).reshape(256, 256)


def p7(first, tab, G, probe, pat, grad, total, m):
    er, ei = halves(dot(tab[6], G[0]))
    r_, i_ = halves(dot(tab[7], G[1]))
    br = both(er + r_, er - r_)
    bi = both(ei + i_, ei - i_)
    pr, pi = probe[0], probe[1]
    qr, qi = pat[0], pat[1]
    gr = pr * br + pi * bi
    gi = pr * bi - pi * br
    grad[0] = gr if first else grad[0] + gr
    grad[1] = gi if first else grad[1] + gi
    total[0, m] += qr * br + qi * bi
    total[1, m] += qr * bi - qi * br


def fetch(ext, pat, r, c):
    ct = c // 128
    sh = c % 128
    lane = lax.broadcasted_iota(jnp.int32, (128, 128), 1)
    keep = lane < 128 - sh
    for k in (0, 1):
        for h in (0, 1):
            x = []
            for t in range(3):
                v = jnp.concatenate([ext[k, ct + t, pl.ds(r + 128 * h + row0(i), 8, stride=S)] for i in range(16)], axis=0)
                x.append(pltpu.roll(v, 128 - sh, axis=1))
            for t in (0, 1):
                y = jnp.where(keep, x[t], x[t + 1])
                for i in range(16):
                    pat[k, 16 * i + 8 * h:16 * i + 8 * h + 8, t * H:t * H + H] = y[8 * i:8 * i + 8]

def deposit(grid, grad, r, c):
    ct = c // 128
    sh = c % 128
    lane = lax.broadcasted_iota(jnp.int32, (256, 128), 1)
    keep = lane >= sh
    for k in (0, 1):
        x = grad[k].astype(bf).astype(f32)
        a = pltpu.roll(x[:, :H], sh, axis=1)
        b = pltpu.roll(x[:, H:], sh, axis=1)
        z = jnp.zeros_like(a)
        for t, y in enumerate((jnp.where(keep, a, z), jnp.where(keep, b, a), jnp.where(keep, z, b))):
            for i in range(16):
                for h in (0, 1):
                    ds = pl.ds(r + 128 * h + row0(i), 8, stride=S)
                    grid[k, ct + t, ds] = grid[k, ct + t, ds] + y[16 * i + 8 * h:16 * i + 8 * h + 8]


def forward_kernel(off, spec, right, lower, corner, probe, tab, far, pat, inten, ext, A, Bb):
    s = pl.program_id(0)

    @pl.when(s == 0)
    def _():
        for c in (0, 1):
            for t in range(10):
                ls = slice(t * H, t * H + H)
                l2 = slice(t * H - 1024, t * H - 1024 + H)
                ext[c, t, :512] = (spec[c, :, ls] if t < 8 else right[c, :, l2]).astype(bf).astype(f32)
                ext[c, t, 512:] = (lower[c, :, ls] if t < 8 else corner[c, :, l2]).astype(f32)

    rows, cols = find(off, s, lax.axis_index("ty"))

    @pl.when(rows[0] >= 0)
    def _():
        items = [(q, m) for q in range(2) for m in range(4)]
        for t in range(len(items) + 2):
            if 0 <= t - 1 < len(items):
                q, m = items[t - 1]
                p2(tab, A.at[q, m], Bb.at[q, m])
            if 0 <= t - 2 < len(items):
                q, m = items[t - 2]
                p3(m == 0, tab, Bb.at[q, m], far.at[0, q, m], inten.at[0, q])
            if t < len(items):
                q, m = items[t]
                if m == 0:
                    fetch(ext, pat.at[0, q], rows[q], cols[q])
                p1(probe.at[:, m], pat.at[0, q], A.at[q, m])


def backward_kernel(off, probe, tab, amp, far, pat, inten, main_o, down_o, right_o, corner_o, total_o, grid, total, fac, C, G, grad):
    s = pl.program_id(0)

    @pl.when(s == 0)
    def _():
        grid[...] = jnp.zeros_like(grid)
        total[...] = jnp.zeros_like(total)

    rows, cols = find(off, s, lax.axis_index("ty"))

    @pl.when(rows[0] >= 0)
    def _():
        items = [(q, m) for q in range(2) for m in range(4)]
        for t in range(len(items) + 2):
            if 0 <= t - 1 < len(items):
                q, m = items[t - 1]
                p6(tab, C.at[q, m], G.at[q, m])
            if 0 <= t - 2 < len(items):
                q, m = items[t - 2]
                p7(m == 0, tab, G.at[q, m], probe.at[:, m], pat.at[0, q], grad.at[q], total, m)
                if m == 3:
                    deposit(grid, grad.at[q], rows[q], cols[q])
            if t < len(items):
                q, m = items[t]
                if m == 0:
                    p4(amp.at[0, q], inten.at[0, q], fac.at[q])
                p5(far.at[0, q, m], fac.at[q], C.at[q, m])

    @pl.when(s == pl.num_programs(0) - 1)
    def _():
        for c in (0, 1):
            for t in range(10):
                ls = slice(t * H, t * H + H)
                l2 = slice(t * H - 1024, t * H - 1024 + H)
                if t < 8:
                    main_o[c, :, ls] = grid[c, t, :512]
                    down_o[c, :, ls] = grid[c, t, 512:].astype(bf)
                else:
                    right_o[c, :, l2] = grid[c, t, :512].astype(bf)
                    corner_o[c, :, l2] = grid[c, t, 512:].astype(bf)
            for m in range(4):
                for i in range(32):
                    for t in range(2):
                        ds = pl.ds(128 * (i % 2) + row0(i // 2), 8, stride=S)
                        total_o[c, m, t, ds] = total[c, m, 8 * i:8 * i + 8, t * H:t * H + H]


def whole(*shape):
    return pl.BlockSpec(shape, lambda i, o: (0,) * len(shape), pipeline_mode=pl.Buffered(1))


def each(*shape):
    return pl.BlockSpec((1, *shape), lambda i, o: (i,) + (0,) * len(shape))


def like(shape, dtype):
    return jax.ShapeDtypeStruct(shape, dtype)


def forward(off, spec, right, lower, corner, probe, tab, sources):
    return pl.pallas_call(
        forward_kernel,
        out_shape=[like((sources, 2, 4, 2, 2, 128, 256), f32), like((sources, 2, 2, 256, 256), f32), like((sources, 2, 2, 128, 256), f32)],
        grid_spec=pltpu.PrefetchScalarGridSpec(
            num_scalar_prefetch=1, grid=(sources,),
            in_specs=[whole(2, 512, 1024), whole(2, 512, 256), whole(2, 256, 1024), whole(2, 256, 256), whole(2, 4, 256, 256), whole(8, 256, 256)],
            out_specs=[each(2, 4, 2, 2, 128, 256), each(2, 2, 256, 256), each(2, 2, 128, 256)],
            scratch_shapes=[pltpu.VMEM((2, 10, 768, 128), f32), pltpu.VMEM((2, 4, 2, 256, 256), bf), pltpu.VMEM((2, 4, 2, 256, 256), bf)]),
        compiler_params=pltpu.CompilerParams(vmem_limit_bytes=VMEM_LIMIT),
        cost_estimate=pl.CostEstimate(flops=32 * 2**29, bytes_accessed=100 * 2**20, transcendentals=0),
    )(off, spec, right, lower, corner, probe, tab)


def backward(off, probe, tab, amp, far, pat, inten, sources):
    return pl.pallas_call(
        backward_kernel,
        out_shape=[like((2, 512, 1024), f32), like((2, 256, 1024), bf), like((2, 512, 256), bf), like((2, 256, 256), bf), like((2, 4, 2, 256, 128), f32)],
        grid_spec=pltpu.PrefetchScalarGridSpec(
            num_scalar_prefetch=1, grid=(sources,),
            in_specs=[whole(2, 4, 256, 256), whole(8, 256, 256), each(2, 256, 256), each(2, 4, 2, 2, 128, 256), each(2, 2, 256, 256), each(2, 2, 128, 256)],
            out_specs=[whole(2, 512, 1024), whole(2, 256, 1024), whole(2, 512, 256), whole(2, 256, 256), whole(2, 4, 2, 256, 128)],
            scratch_shapes=[pltpu.VMEM((2, 10, 768, 128), f32), pltpu.VMEM((2, 4, 256, 256), f32), pltpu.VMEM((2, 2, 128, 256), f32), pltpu.VMEM((2, 4, 2, 256, 256), bf),
                            pltpu.VMEM((2, 4, 2, 256, 256), bf), pltpu.VMEM((2, 2, 256, 256), f32)]),
        compiler_params=pltpu.CompilerParams(vmem_limit_bytes=VMEM_LIMIT),
        cost_estimate=pl.CostEstimate(flops=32 * 2**29, bytes_accessed=100 * 2**20, transcendentals=0),
    )(off, probe, tab, amp, far, pat, inten)


def spread(axis, size, reach):
    lax.fori_loop(1, size, lambda d, c: (reach(d), c)[1], 0)


def beyond(axis, d, size):
    place = {"ty": lax.axis_index("ty"), "tx": lax.axis_index("tx")}
    place[axis] = lax.rem(place[axis] + d, size)
    return (place["ty"], place["tx"])


def gather_kernel(n_ty, n_tx, own, spec, probe, out, lower_o, right_o, corner_o, probe_o,
                  top, side, half_top, half_side, split, send, recv, send_h, recv_h, sem):
    ty, tx = lax.axis_index("ty"), lax.axis_index("tx")
    above, left = lax.rem(ty + n_ty - 1, n_ty), lax.rem(tx + n_tx - 1, n_tx)
    barrier = pltpu.get_barrier_semaphore()

    def greet(device):
        pl.semaphore_signal(barrier, inc=1, device_id=device, device_id_type=MESH)

    spread("ty", n_ty, lambda d: greet(beyond("ty", d, n_ty)))
    greet((ty, lax.rem(tx + 1, n_tx)))
    greet((lax.rem(ty + 1, n_ty), lax.rem(tx + 1, n_tx)))
    load_side = pltpu.make_async_copy(spec.at[:, :, 0:N], side, sem.at[0])
    load_top = pltpu.make_async_copy(spec.at[:, 0:N], top, sem.at[1])
    load_top.start()
    load_side.start()
    pl.semaphore_wait(barrier, n_ty + 1)

    def copy(d):
        return pltpu.make_async_remote_copy(
            src_ref=own, dst_ref=out.at[ty], send_sem=send.at[d], recv_sem=recv.at[d],
            device_id=beyond("ty", d, n_ty), device_id_type=MESH)

    def halo(k, src, dst, device):
        return pltpu.make_async_remote_copy(
            src_ref=src, dst_ref=dst, send_sem=send_h.at[k], recv_sem=recv_h.at[k], device_id=device, device_id_type=MESH)

    spread("ty", n_ty, lambda d: copy(d).start())
    out[ty] = own[...]
    load_top.wait()
    half_top[...] = top[...].astype(bf)
    lower = halo(0, half_top, lower_o, (above, tx))
    lower.start()
    corner = halo(1, half_top.at[:, :, 0:N], corner_o, (above, left))
    corner.start()
    load_side.wait()
    half_side[...] = side[...].astype(bf)
    right = halo(2, half_side, right_o, (ty, left))
    right.start()
    for c in (0, 1):
        for t in (0, 1):
            split[c, :, t] = probe[c, :, :, t * H:t * H + H]
    for c in (0, 1):
        for m in range(4):
            for t in (0, 1):
                for i in range(32):
                    ds = pl.ds(128 * (i % 2) + row0(i // 2), 8, stride=S)
                    probe_o[c, m, 8 * i:8 * i + 8, t * H:t * H + H] = split[c, m, t, ds]
    spread("ty", n_ty, lambda d: copy(d).wait())
    right.wait()
    corner.wait()
    lower.wait()


def gather(offsets, specimen, probe, n_ty, n_tx):
    own = jnp.pad(offsets.reshape(1, 2 * POS), ((0, 7), (0, 128 - 2 * POS)))
    vmem = pl.BlockSpec(memory_space=pltpu.VMEM)
    hbm = pl.BlockSpec(memory_space=pl.ANY)
    dma = pltpu.SemaphoreType.DMA
    out, lower, right, corner, arranged = pl.pallas_call(
        functools.partial(gather_kernel, n_ty, n_tx),
        out_shape=[like((n_ty, 8, 128), jnp.int32), like((2, N, TILE_C), bf), like((2, TILE_R, N), bf), like((2, N, N), bf),
                   like(probe.shape, f32)],
        in_specs=[vmem, hbm, vmem],
        out_specs=[vmem, hbm, hbm, hbm, vmem],
        scratch_shapes=[
            pltpu.VMEM((2, N, TILE_C), f32), pltpu.VMEM((2, TILE_R, N), f32),
            pltpu.VMEM((2, N, TILE_C), bf), pltpu.VMEM((2, TILE_R, N), bf), pltpu.VMEM((2, 4, 2, N, H), f32),
            dma((n_ty,)), dma((n_ty,)), dma((3,)), dma((3,)), dma((2,))],
        compiler_params=pltpu.CompilerParams(collective_id=0, has_side_effects=True, vmem_limit_bytes=VMEM_LIMIT),
    )(own, specimen, probe)
    return out[:, 0, : 2 * POS].reshape(-1), lower, right, corner, arranged


def finish_kernel(n_ty, n_tx, scale, total, down, right, corner, probe_o, down_o, right_o, corner_o,
                  cast, rax, ray, sx, sy, rbx, rby, gx, gy, hx, hy, send_ty, recv_ty, send_tx, recv_tx, send_h, recv_h):
    ty, tx = lax.axis_index("ty"), lax.axis_index("tx")
    nx, ny, sub = ROWS // n_tx, ROWS // n_ty, ROWS // n_tx // n_ty
    barrier = pltpu.get_barrier_semaphore()

    def greet(device):
        pl.semaphore_signal(barrier, inc=1, device_id=device, device_id_type=MESH)

    spread("ty", n_ty, lambda d: greet(beyond("ty", d, n_ty)))
    spread("tx", n_tx, lambda d: greet(beyond("tx", d, n_tx)))
    greet((lax.rem(ty + n_ty - 1, n_ty), lax.rem(tx + n_tx - 1, n_tx)))
    cast[...] = total[...].astype(bf)
    pl.semaphore_wait(barrier, n_ty + n_tx - 1)

    def over_ty(stage, d, src, dst):
        return pltpu.make_async_remote_copy(
            src_ref=src, dst_ref=dst, send_sem=send_ty.at[stage, d], recv_sem=recv_ty.at[stage, d],
            device_id=beyond("ty", d, n_ty), device_id_type=MESH)

    def over_tx(stage, d, src, dst):
        return pltpu.make_async_remote_copy(
            src_ref=src, dst_ref=dst, send_sem=send_tx.at[stage, d], recv_sem=recv_tx.at[stage, d],
            device_id=beyond("tx", d, n_tx), device_id_type=MESH)

    def rows(k, n):
        return pl.ds(pl.multiple_of(k * n, 16), n)

    def halo(k, src, dst, device):
        return pltpu.make_async_remote_copy(
            src_ref=src, dst_ref=dst, send_sem=send_h.at[k], recv_sem=recv_h.at[k], device_id=device, device_id_type=MESH)

    below, beside = lax.rem(ty + 1, n_ty), lax.rem(tx + 1, n_tx)
    part = N // PIECES
    pieces = [halo(k, down.at[:, k * part:k * part + part], down_o.at[:, k * part:k * part + part], (below, tx)) for k in range(PIECES)]
    halos = pieces + [halo(PIECES, right, right_o, (ty, beside)), halo(PIECES + 1, corner, corner_o, (below, beside))]

    def ax(d):
        peer = lax.rem(tx + d, n_tx)
        return over_tx(0, d, cast.at[0, rows(peer, nx)], rax.at[d])

    def ay(d):
        peer = lax.rem(ty + d, n_ty)
        return over_ty(0, d, cast.at[1, rows(peer, ny)], ray.at[d])

    spread("tx", n_tx, lambda d: ax(d).start())
    spread("ty", n_ty, lambda d: ay(d).start())
    halos[0].start()
    spread("tx", n_tx, lambda d: ax(d).wait())
    sx[...] = lax.fori_loop(1, n_tx, lambda d, t: t + rax[d].astype(f32), total[0, rows(tx, nx)])

    def bx(d):
        peer = lax.rem(ty + d, n_ty)
        return over_ty(1, d, sx.at[rows(peer, sub)], rbx.at[d])

    spread("ty", n_ty, lambda d: bx(d).start())
    spread("ty", n_ty, lambda d: ay(d).wait())
    sy[...] = lax.fori_loop(1, n_ty, lambda d, t: t + ray[d].astype(f32), total[1, rows(ty, ny)])

    def by(d):
        peer = lax.rem(tx + d, n_tx)
        return over_tx(1, d, sy.at[rows(peer, sub)], rby.at[d])

    spread("tx", n_tx, lambda d: by(d).start())
    halos[1].start()
    spread("ty", n_ty, lambda d: bx(d).wait())
    gx[rows(ty, sub)] = scale * lax.fori_loop(1, n_ty, lambda d, t: t + rbx[d], sx[rows(ty, sub)])

    def cx(d):
        return over_ty(2, d, gx.at[rows(ty, sub)], gx.at[rows(ty, sub)])

    spread("ty", n_ty, lambda d: cx(d).start())
    spread("tx", n_tx, lambda d: by(d).wait())
    gy[rows(tx, sub)] = scale * lax.fori_loop(1, n_tx, lambda d, t: t + rby[d], sy[rows(tx, sub)])

    def cy(d):
        return over_tx(2, d, gy.at[rows(tx, sub)], gy.at[rows(tx, sub)])

    spread("tx", n_tx, lambda d: cy(d).start())
    halos[2].start()
    spread("ty", n_ty, lambda d: cx(d).wait())
    hx[...] = gx[...].astype(bf)

    def dx(d):
        return over_tx(3, d, hx, probe_o.at[0, rows(tx, nx)])

    spread("tx", n_tx, lambda d: dx(d).start())
    probe_o[0, rows(tx, nx)] = hx[...]
    spread("tx", n_tx, lambda d: cy(d).wait())
    hy[...] = gy[...].astype(bf)

    def dy(d):
        return over_ty(3, d, hy, probe_o.at[1, rows(ty, ny)])

    spread("ty", n_ty, lambda d: dy(d).start())
    for h in halos[3:]:
        h.start()
    probe_o[1, rows(ty, ny)] = hy[...]
    spread("tx", n_tx, lambda d: dx(d).wait())
    spread("ty", n_ty, lambda d: dy(d).wait())
    for h in halos:
        h.wait()


def finish(total, down, right, corner, scale, n_ty, n_tx):
    nx, ny, sub = ROWS // n_tx, ROWS // n_ty, ROWS // n_tx // n_ty
    vmem = pl.BlockSpec(memory_space=pltpu.VMEM)
    hbm = pl.BlockSpec(memory_space=pl.ANY)
    dma = pltpu.SemaphoreType.DMA
    return pl.pallas_call(
        functools.partial(finish_kernel, n_ty, n_tx, scale),
        out_shape=[like((2, ROWS, H), bf), like(down.shape, bf), like(right.shape, bf), like(corner.shape, bf)],
        in_specs=[vmem, hbm, hbm, hbm],
        out_specs=[vmem, hbm, hbm, hbm],
        scratch_shapes=[
            pltpu.VMEM((2, ROWS, H), bf), pltpu.VMEM((n_tx, nx, H), bf), pltpu.VMEM((n_ty, ny, H), bf),
            pltpu.VMEM((nx, H), f32), pltpu.VMEM((ny, H), f32), pltpu.VMEM((n_ty, sub, H), f32), pltpu.VMEM((n_tx, sub, H), f32),
            pltpu.VMEM((nx, H), f32), pltpu.VMEM((ny, H), f32), pltpu.VMEM((nx, H), bf), pltpu.VMEM((ny, H), bf),
            dma((4, n_ty)), dma((4, n_ty)), dma((4, n_tx)), dma((4, n_tx)), dma((PIECES + 2,)), dma((PIECES + 2,))],
        compiler_params=pltpu.CompilerParams(collective_id=1, has_side_effects=True, vmem_limit_bytes=VMEM_LIMIT),
    )(total.reshape(2, ROWS, H), down, right, corner)


def on_device(specimen, probe, amplitude, offsets):
    n_ty, n_tx = lax.axis_size("ty"), lax.axis_size("tx")
    positions = offsets.shape[0] * n_ty * n_tx
    own = offsets.reshape(-1)
    everyone, lower, right, corner, arranged = gather(own, specimen, probe, n_ty, n_tx)
    slots = prepare(own, amplitude, n_ty)
    slots, everyone = lax.optimization_barrier((slots, everyone))
    arrived = lax.all_to_all(slots, "ty", split_axis=0, concat_axis=0, tiled=True)
    tables = make_tables()
    far, pat, inten = forward(everyone, specimen, right, lower, corner, arranged, tables, n_ty)
    main, down, rt, cn, total = backward(everyone, arranged, tables, arrived, far, pat, inten, n_ty)
    scale = float(probe.shape[1] / np.sqrt(positions))
    probe_grad, down, rt, cn = finish(total, down, rt, cn, scale, n_ty, n_tx)

    def spot(piece):
        rows, cols = TILE_R - piece.shape[1], TILE_C - piece.shape[2]
        return jnp.pad(piece.astype(f32), ((0, 0), (0, rows), (0, cols)))

    object_grad = main + spot(down) + spot(rt) + spot(cn)
    probe_grad = jnp.swapaxes(probe_grad.reshape(2, 4, 2, N, H), 2, 3).reshape(probe.shape).astype(f32)
    return (object_grad, probe_grad)


def solution(mesh):
    in_specs = (P(None, "ty", "tx"), P(), P(("ty", "tx"), None, None), P(("ty", "tx"), None))
    out_specs = (P(None, "ty", "tx"), P())
    return jax.shard_map(on_device, mesh=mesh, in_specs=in_specs, out_specs=out_specs, check_vma=False)
```

```python
import functools

import jax
import jax.numpy as jnp
import ml_dtypes
import numpy as np
from jax import lax
from jax.experimental import pallas as pl
from jax.experimental.pallas import tpu as pltpu
from jax.sharding import PartitionSpec as P

bf = jnp.bfloat16
f32 = jnp.float32
N = 256
H = 128
TILE_R = 512
TILE_C = 1024
POS = 12
VMEM_LIMIT = 60 * 2**20
ROWS = 2048
PIECES = 4
MESH = pl.DeviceIdType.MESH
S = 2
B = 16 // S

def row0(i):
    return i // S * 8 * S + i % S

def make_tables():
    k = np.arange(N)
    ang = ((k[:, None] * k[None, :]) % N).astype(np.float64) * (2 * np.pi / N)
    re = (np.cos(ang) / 16).astype(np.float32).astype(ml_dtypes.bfloat16).astype(np.float32)
    im = (-np.sin(ang) / 16).astype(np.float32).astype(ml_dtypes.bfloat16).astype(np.float32)
    order = np.arange(128).reshape(B, 8, S).swapaxes(1, 2).reshape(-1)
    def mix(a, b):
        return np.stack([a.reshape(16, 8, -1), b.reshape(16, 8, -1)], 1).reshape(256, -1)
    out = []
    for par in (0, 1):
        r, i = re[:H, par::2], im[:H, par::2]
        out.append(np.block([[r, i], [-i, r]]))
    for par in (0, 1):
        r, i = re[par::2][:, order], im[par::2][:, order]
        out.append(mix(np.block([r, -i]), np.block([i, r])))
    for par in (0, 1):
        r, i = re[par::2, :H], -im[par::2, :H]
        out.append(np.block([[r, i], [-i, r]]))
    for par in (0, 1):
        r, i = re[order][:, par::2], -im[order][:, par::2]
        out.append(mix(np.block([r, -i]), np.block([i, r])))
    return np.stack(out).astype(ml_dtypes.bfloat16)

def dot(a, b):
    return jnp.dot(a, b, preferred_element_type=f32)

def halves(x):
    x = x.reshape(16, 2, 8, x.shape[-1])
    return x[:, 0].reshape(128, x.shape[-1]), x[:, 1].reshape(128, x.shape[-1])


def parity_matrix():
    order = np.concatenate([np.arange(0, N, 2), np.arange(1, N, 2)])
    return np.eye(N)[order].astype(ml_dtypes.bfloat16)


def prep_kernel(sources, off, amp, perm, out, places, buf, sem):
    ty = lax.axis_index("ty")
    copies = []
    for i in range(POS):
        a = dot(perm[...], amp[i].astype(bf)).astype(bf)
        buf[i] = lax.dot_general(a, perm[...], (((1,), (1,)), ((), ())), preferred_element_type=f32).astype(bf)
        tile = off[ty, 0, 2 * i] // TILE_R
        rank = jnp.int32(0)
        for j in range(i):
            rank = rank + (off[ty, 0, 2 * j] // TILE_R == tile).astype(jnp.int32)
        copies.append(pltpu.make_async_copy(buf.at[i], out.at[tile, rank], sem.at[i]))
        copies[i].start()

    def one(s, carry):
        rows, cols = [jnp.int32(-1)] * 2, [jnp.int32(0)] * 2
        seen = jnp.int32(0)
        for i in range(POS):
            r, c = off[s, 0, 2 * i], off[s, 0, 2 * i + 1]
            mine = r // TILE_R == ty
            for q in range(2):
                take = mine & (seen == q)
                rows[q] = jnp.where(take, r % TILE_R, rows[q])
                cols[q] = jnp.where(take, c % TILE_C, cols[q])
            seen = seen + mine.astype(jnp.int32)
        for q in range(2):
            places[s * 4 + 2 * q] = rows[q]
            places[s * 4 + 2 * q + 1] = cols[q]
        return carry

    lax.fori_loop(0, sources, one, 0)
    for copy in copies:
        copy.wait()


def prepare(everyone, amplitude, sources):
    vmem = pl.BlockSpec(memory_space=pltpu.VMEM)
    smem = pl.BlockSpec(memory_space=pltpu.SMEM)
    return pl.pallas_call(
        functools.partial(prep_kernel, sources),
        out_shape=[jax.ShapeDtypeStruct((sources, 2, N, N), bf), jax.ShapeDtypeStruct((4 * sources,), jnp.int32)],
        in_specs=[smem, vmem, vmem],
        out_specs=[pl.BlockSpec(memory_space=pl.ANY), smem],
        scratch_shapes=[pltpu.VMEM((POS, N, N), bf), pltpu.SemaphoreType.DMA((POS,))],
        compiler_params=pltpu.CompilerParams(vmem_limit_bytes=VMEM_LIMIT),
    )(everyone, amplitude, parity_matrix())


def find(places, source):
    return [places[4 * source], places[4 * source + 2]], [places[4 * source + 1], places[4 * source + 3]]


def p1(probe, pat, A):
    pr, pi = probe[0], probe[1]
    qr, qi = pat[0], pat[1]
    er = pr * qr - pi * qi
    ei = pr * qi + pi * qr
    A[0, :, :H] = (er[:, :H] + er[:, H:]).astype(bf)
    A[0, :, H:] = (ei[:, :H] + ei[:, H:]).astype(bf)
    A[1, :, :H] = (er[:, :H] - er[:, H:]).astype(bf)
    A[1, :, H:] = (ei[:, :H] - ei[:, H:]).astype(bf)


def p2(tab, A, Bb):
    for p in (0, 1):
        t, b = halves(dot(A[p], tab[p]))
        s = (t + b).astype(bf)
        d = (t - b).astype(bf)
        ls = slice(p * H, p * H + H)
        Bb[0, :H, ls] = s[:, :H]
        Bb[0, H:, ls] = s[:, H:]
        Bb[1, :H, ls] = d[:, :H]
        Bb[1, H:, ls] = d[:, H:]


def p3(first, tab, Bb, far, inten):
    for p in (0, 1):
        r, i = halves(dot(tab[2 + p], Bb[p]))
        far[p, 0] = r
        far[p, 1] = i
        t = r * r + i * i
        inten[p] = t if first else inten[p] + t


def p4(amp, inten, fac):
    for p in (0, 1):
        a = amp[p * H:(p + 1) * H].astype(f32)
        fac[p] = 1.0 - a * lax.rsqrt(jnp.maximum(inten[p], 0.25))


def p5(far, fac, C):
    for p in (0, 1):
        f = fac[p]
        rr = (far[p, 0] * f).astype(bf)
        ri = (far[p, 1] * f).astype(bf)
        rs = slice(p * H, p * H + H)
        C[0, rs, :H] = rr[:, :H]
        C[0, rs, H:] = ri[:, :H]
        C[1, rs, :H] = rr[:, H:]
        C[1, rs, H:] = ri[:, H:]


def p6(tab, C, G):
    e = dot(C[0], tab[4])
    o = dot(C[1], tab[5])
    s = (e + o).astype(bf)
    d = (e - o).astype(bf)
    for p in (0, 1):
        rs = slice(p * H, p * H + H)
        G[p, :H, :H] = s[rs, :H]
        G[p, :H, H:] = d[rs, :H]
        G[p, H:, :H] = s[rs, H:]
        G[p, H:, H:] = d[rs, H:]


def both(a, b):
    return jnp.stack([a.reshape(16, 8, 256), b.reshape(16, 8, 256)], 1).reshape(256, 256)


def p7(first, tab, G, probe, pat, grad, total, m):
    er, ei = halves(dot(tab[6], G[0]))
    r_, i_ = halves(dot(tab[7], G[1]))
    br = both(er + r_, er - r_)
    bi = both(ei + i_, ei - i_)
    pr, pi = probe[0], probe[1]
    qr, qi = pat[0], pat[1]
    gr = pr * br + pi * bi
    gi = pr * bi - pi * br
    grad[0] = gr if first else grad[0] + gr
    grad[1] = gi if first else grad[1] + gi
    total[0, m] += qr * br + qi * bi
    total[1, m] += qr * bi - qi * br


def fetch(ext, pat, r, c):
    ct = c // 128
    sh = c % 128
    lane = lax.broadcasted_iota(jnp.int32, (128, 128), 1)
    keep = lane < 128 - sh
    for k in (0, 1):
        for h in (0, 1):
            x = []
            for t in range(3):
                v = jnp.concatenate([ext[k, ct + t, pl.ds(r + 128 * h + row0(i), 8, stride=S)] for i in range(16)], axis=0)
                x.append(pltpu.roll(v, 128 - sh, axis=1))
            for t in (0, 1):
                y = jnp.where(keep, x[t], x[t + 1])
                for i in range(16):
                    pat[k, 16 * i + 8 * h:16 * i + 8 * h + 8, t * H:t * H + H] = y[8 * i:8 * i + 8]

def deposit(grid, grad, r, c):
    ct = c // 128
    sh = c % 128
    lane = lax.broadcasted_iota(jnp.int32, (256, 128), 1)
    keep = lane >= sh
    for k in (0, 1):
        x = grad[k].astype(bf).astype(f32)
        a = pltpu.roll(x[:, :H], sh, axis=1)
        b = pltpu.roll(x[:, H:], sh, axis=1)
        z = jnp.zeros_like(a)
        for t, y in enumerate((jnp.where(keep, a, z), jnp.where(keep, b, a), jnp.where(keep, z, b))):
            for i in range(16):
                for h in (0, 1):
                    ds = pl.ds(r + 128 * h + row0(i), 8, stride=S)
                    grid[k, ct + t, ds] = grid[k, ct + t, ds] + y[16 * i + 8 * h:16 * i + 8 * h + 8]


def forward_kernel(off, spec, right, lower, corner, probe, tab, far, pat, inten, ext, A, Bb):
    s = pl.program_id(0)

    @pl.when(s == 0)
    def _():
        for c in (0, 1):
            for t in range(10):
                ls = slice(t * H, t * H + H)
                l2 = slice(t * H - 1024, t * H - 1024 + H)
                ext[c, t, :512] = (spec[c, :, ls] if t < 8 else right[c, :, l2]).astype(bf).astype(f32)
                ext[c, t, 512:] = (lower[c, :, ls] if t < 8 else corner[c, :, l2]).astype(f32)

    rows, cols = find(off, s)

    @pl.when(rows[0] >= 0)
    def _():
        items = [(q, m) for q in range(2) for m in range(4)]
        for t in range(len(items) + 2):
            if 0 <= t - 1 < len(items):
                q, m = items[t - 1]
                p2(tab, A.at[q, m], Bb.at[q, m])
            if 0 <= t - 2 < len(items):
                q, m = items[t - 2]
                p3(m == 0, tab, Bb.at[q, m], far.at[0, q, m], inten.at[0, q])
            if t < len(items):
                q, m = items[t]
                if m == 0:
                    fetch(ext, pat.at[0, q], rows[q], cols[q])
                p1(probe.at[:, m], pat.at[0, q], A.at[q, m])


def backward_kernel(off, probe, tab, amp, far, pat, inten, main_o, down_o, right_o, corner_o, total_o, grid, total, fac, C, G, grad):
    s = pl.program_id(0)

    @pl.when(s == 0)
    def _():
        grid[...] = jnp.zeros_like(grid)
        total[...] = jnp.zeros_like(total)

    rows, cols = find(off, s)

    @pl.when(rows[0] >= 0)
    def _():
        items = [(q, m) for q in range(2) for m in range(4)]
        for t in range(len(items) + 2):
            if 0 <= t - 1 < len(items):
                q, m = items[t - 1]
                p6(tab, C.at[q, m], G.at[q, m])
            if 0 <= t - 2 < len(items):
                q, m = items[t - 2]
                p7(m == 0, tab, G.at[q, m], probe.at[:, m], pat.at[0, q], grad.at[q], total, m)
                if m == 3:
                    deposit(grid, grad.at[q], rows[q], cols[q])
            if t < len(items):
                q, m = items[t]
                if m == 0:
                    p4(amp.at[0, q], inten.at[0, q], fac.at[q])
                p5(far.at[0, q, m], fac.at[q], C.at[q, m])

    @pl.when(s == pl.num_programs(0) - 1)
    def _():
        for c in (0, 1):
            for t in range(10):
                ls = slice(t * H, t * H + H)
                l2 = slice(t * H - 1024, t * H - 1024 + H)
                if t < 8:
                    main_o[c, :, ls] = grid[c, t, :512]
                    down_o[c, :, ls] = grid[c, t, 512:].astype(bf)
                else:
                    right_o[c, :, l2] = grid[c, t, :512].astype(bf)
                    corner_o[c, :, l2] = grid[c, t, 512:].astype(bf)
            for m in range(4):
                for i in range(32):
                    for t in range(2):
                        ds = pl.ds(128 * (i % 2) + row0(i // 2), 8, stride=S)
                        total_o[c, m, t, ds] = total[c, m, 8 * i:8 * i + 8, t * H:t * H + H]


def whole(*shape):
    return pl.BlockSpec(shape, lambda i, o: (0,) * len(shape), pipeline_mode=pl.Buffered(1))


def each(*shape):
    return pl.BlockSpec((1, *shape), lambda i, o: (i,) + (0,) * len(shape))


def like(shape, dtype):
    return jax.ShapeDtypeStruct(shape, dtype)


def forward(off, spec, right, lower, corner, probe, tab, sources):
    return pl.pallas_call(
        forward_kernel,
        out_shape=[like((sources, 2, 4, 2, 2, 128, 256), f32), like((sources, 2, 2, 256, 256), f32), like((sources, 2, 2, 128, 256), f32)],
        grid_spec=pltpu.PrefetchScalarGridSpec(
            num_scalar_prefetch=1, grid=(sources,),
            in_specs=[whole(2, 512, 1024), whole(2, 512, 256), whole(2, 256, 1024), whole(2, 256, 256), whole(2, 4, 256, 256), whole(8, 256, 256)],
            out_specs=[each(2, 4, 2, 2, 128, 256), each(2, 2, 256, 256), each(2, 2, 128, 256)],
            scratch_shapes=[pltpu.VMEM((2, 10, 768, 128), f32), pltpu.VMEM((2, 4, 2, 256, 256), bf), pltpu.VMEM((2, 4, 2, 256, 256), bf)]),
        compiler_params=pltpu.CompilerParams(vmem_limit_bytes=VMEM_LIMIT),
        cost_estimate=pl.CostEstimate(flops=32 * 2**29, bytes_accessed=100 * 2**20, transcendentals=0),
    )(off, spec, right, lower, corner, probe, tab)


def backward(off, probe, tab, amp, far, pat, inten, sources):
    return pl.pallas_call(
        backward_kernel,
        out_shape=[like((2, 512, 1024), f32), like((2, 256, 1024), bf), like((2, 512, 256), bf), like((2, 256, 256), bf), like((2, 4, 2, 256, 128), f32)],
        grid_spec=pltpu.PrefetchScalarGridSpec(
            num_scalar_prefetch=1, grid=(sources,),
            in_specs=[whole(2, 4, 256, 256), whole(8, 256, 256), each(2, 256, 256), each(2, 4, 2, 2, 128, 256), each(2, 2, 256, 256), each(2, 2, 128, 256)],
            out_specs=[whole(2, 512, 1024), whole(2, 256, 1024), whole(2, 512, 256), whole(2, 256, 256), whole(2, 4, 2, 256, 128)],
            scratch_shapes=[pltpu.VMEM((2, 10, 768, 128), f32), pltpu.VMEM((2, 4, 256, 256), f32), pltpu.VMEM((2, 2, 128, 256), f32), pltpu.VMEM((2, 4, 2, 256, 256), bf),
                            pltpu.VMEM((2, 4, 2, 256, 256), bf), pltpu.VMEM((2, 2, 256, 256), f32)]),
        compiler_params=pltpu.CompilerParams(vmem_limit_bytes=VMEM_LIMIT),
        cost_estimate=pl.CostEstimate(flops=32 * 2**29, bytes_accessed=100 * 2**20, transcendentals=0),
    )(off, probe, tab, amp, far, pat, inten)


def spread(axis, size, reach):
    lax.fori_loop(1, size, lambda d, c: (reach(d), c)[1], 0)


def beyond(axis, d, size):
    place = {"ty": lax.axis_index("ty"), "tx": lax.axis_index("tx")}
    place[axis] = lax.rem(place[axis] + d, size)
    return (place["ty"], place["tx"])


def gather_kernel(n_ty, n_tx, own, spec, probe, out, lower_o, right_o, corner_o, probe_o,
                  top, side, half_top, half_side, split, send, recv, send_h, recv_h, sem):
    ty, tx = lax.axis_index("ty"), lax.axis_index("tx")
    above, left = lax.rem(ty + n_ty - 1, n_ty), lax.rem(tx + n_tx - 1, n_tx)
    barrier = pltpu.get_barrier_semaphore()

    def greet(device):
        pl.semaphore_signal(barrier, inc=1, device_id=device, device_id_type=MESH)

    spread("ty", n_ty, lambda d: greet(beyond("ty", d, n_ty)))
    greet((ty, lax.rem(tx + 1, n_tx)))
    load_side = pltpu.make_async_copy(spec.at[:, :, 0:N], side, sem.at[0])
    load_top = pltpu.make_async_copy(spec.at[:, 0:N], top, sem.at[1])
    load_top.start()
    load_side.start()
    pl.semaphore_wait(barrier, n_ty)

    def copy(d):
        return pltpu.make_async_remote_copy(
            src_ref=own, dst_ref=out.at[ty], send_sem=send.at[d], recv_sem=recv.at[d],
            device_id=beyond("ty", d, n_ty), device_id_type=MESH)

    def halo(k, src, dst, device):
        return pltpu.make_async_remote_copy(
            src_ref=src, dst_ref=dst, send_sem=send_h.at[k], recv_sem=recv_h.at[k], device_id=device, device_id_type=MESH)

    spread("ty", n_ty, lambda d: copy(d).start())
    out[ty] = own[...]
    load_top.wait()
    half_top[:, :, 0:N] = top[:, :, 0:N].astype(bf)
    first = halo(0, half_top.at[:, :, 0:N], lower_o.at[:, :, 0:N], (above, tx))
    first.start()
    half_top[:, :, N:TILE_C] = top[:, :, N:TILE_C].astype(bf)
    rest = halo(1, half_top.at[:, :, N:TILE_C], lower_o.at[:, :, N:TILE_C], (above, tx))
    rest.start()
    load_side.wait()
    half_side[...] = side[...].astype(bf)
    right = halo(2, half_side, right_o, (ty, left))
    right.start()
    first.wait()
    corner = halo(3, lower_o.at[:, :, 0:N], corner_o, (ty, left))
    corner.start()
    for c in (0, 1):
        for t in (0, 1):
            split[c, :, t] = probe[c, :, :, t * H:t * H + H]
    for c in (0, 1):
        for m in range(4):
            for t in (0, 1):
                for i in range(32):
                    ds = pl.ds(128 * (i % 2) + row0(i // 2), 8, stride=S)
                    probe_o[c, m, 8 * i:8 * i + 8, t * H:t * H + H] = split[c, m, t, ds]
    spread("ty", n_ty, lambda d: copy(d).wait())
    right.wait()
    corner.wait()
    rest.wait()


def gather(offsets, specimen, probe, n_ty, n_tx):
    own = jnp.pad(offsets.reshape(1, 2 * POS), ((0, 7), (0, 128 - 2 * POS)))
    vmem = pl.BlockSpec(memory_space=pltpu.VMEM)
    hbm = pl.BlockSpec(memory_space=pl.ANY)
    dma = pltpu.SemaphoreType.DMA
    out, lower, right, corner, arranged = pl.pallas_call(
        functools.partial(gather_kernel, n_ty, n_tx),
        out_shape=[like((n_ty, 8, 128), jnp.int32), like((2, N, TILE_C), bf), like((2, TILE_R, N), bf), like((2, N, N), bf),
                   like(probe.shape, f32)],
        in_specs=[vmem, hbm, vmem],
        out_specs=[vmem, hbm, hbm, hbm, vmem],
        scratch_shapes=[
            pltpu.VMEM((2, N, TILE_C), f32), pltpu.VMEM((2, TILE_R, N), f32),
            pltpu.VMEM((2, N, TILE_C), bf), pltpu.VMEM((2, TILE_R, N), bf), pltpu.VMEM((2, 4, 2, N, H), f32),
            dma((n_ty,)), dma((n_ty,)), dma((4,)), dma((4,)), dma((2,))],
        compiler_params=pltpu.CompilerParams(collective_id=0, has_side_effects=True, vmem_limit_bytes=VMEM_LIMIT),
    )(own, specimen, probe)
    return out, lower, right, corner, arranged


def finish_kernel(n_ty, n_tx, scale, total, down, right, corner, probe_o, down_o, right_o,
                  cast, rax, ray, sx, sy, rbx, rby, gx, gy, hx, hy, arrived, edge, send_ty, recv_ty, send_tx, recv_tx, send_h, recv_h, sem):
    ty, tx = lax.axis_index("ty"), lax.axis_index("tx")
    nx, ny, sub = ROWS // n_tx, ROWS // n_ty, ROWS // n_tx // n_ty
    barrier = pltpu.get_barrier_semaphore()

    def greet(device):
        pl.semaphore_signal(barrier, inc=1, device_id=device, device_id_type=MESH)

    spread("ty", n_ty, lambda d: greet(beyond("ty", d, n_ty)))
    spread("tx", n_tx, lambda d: greet(beyond("tx", d, n_tx)))
    load = pltpu.make_async_copy(down.at[:, :, 0:N], edge, sem)
    load.start()
    cast[...] = total[...].astype(bf)
    load.wait()
    pl.semaphore_wait(barrier, n_ty + n_tx - 2)

    def over_ty(stage, d, src, dst):
        return pltpu.make_async_remote_copy(
            src_ref=src, dst_ref=dst, send_sem=send_ty.at[stage, d], recv_sem=recv_ty.at[stage, d],
            device_id=beyond("ty", d, n_ty), device_id_type=MESH)

    def over_tx(stage, d, src, dst):
        return pltpu.make_async_remote_copy(
            src_ref=src, dst_ref=dst, send_sem=send_tx.at[stage, d], recv_sem=recv_tx.at[stage, d],
            device_id=beyond("tx", d, n_tx), device_id_type=MESH)

    def rows(k, n):
        return pl.ds(pl.multiple_of(k * n, 16), n)

    def halo(k, src, dst, device):
        return pltpu.make_async_remote_copy(
            src_ref=src, dst_ref=dst, send_sem=send_h.at[k], recv_sem=recv_h.at[k], device_id=device, device_id_type=MESH)

    below, beside = lax.rem(ty + 1, n_ty), lax.rem(tx + 1, n_tx)
    cross = halo(0, corner, arrived, (ty, beside))
    side = halo(1, right, right_o, (ty, beside))
    pieces = [halo(2 + k, edge if k == 0 else down.at[:, :, k * N:k * N + N], down_o.at[:, :, k * N:k * N + N], (below, tx)) for k in range(PIECES)]
    cross.start()
    side.start()

    def ax(d):
        peer = lax.rem(tx + d, n_tx)
        return over_tx(0, d, cast.at[0, rows(peer, nx)], rax.at[d])

    def ay(d):
        peer = lax.rem(ty + d, n_ty)
        return over_ty(0, d, cast.at[1, rows(peer, ny)], ray.at[d])

    spread("tx", n_tx, lambda d: ax(d).start())
    spread("ty", n_ty, lambda d: ay(d).start())
    pieces[1].start()
    spread("tx", n_tx, lambda d: ax(d).wait())
    sx[...] = lax.fori_loop(1, n_tx, lambda d, t: t + rax[d].astype(f32), total[0, rows(tx, nx)])

    def bx(d):
        peer = lax.rem(ty + d, n_ty)
        return over_ty(1, d, sx.at[rows(peer, sub)], rbx.at[d])

    spread("ty", n_ty, lambda d: bx(d).start())
    spread("ty", n_ty, lambda d: ay(d).wait())
    sy[...] = lax.fori_loop(1, n_ty, lambda d, t: t + ray[d].astype(f32), total[1, rows(ty, ny)])

    def by(d):
        peer = lax.rem(tx + d, n_tx)
        return over_tx(1, d, sy.at[rows(peer, sub)], rby.at[d])

    spread("tx", n_tx, lambda d: by(d).start())
    pieces[2].start()
    spread("ty", n_ty, lambda d: bx(d).wait())
    gx[rows(ty, sub)] = scale * lax.fori_loop(1, n_ty, lambda d, t: t + rbx[d], sx[rows(ty, sub)])

    def cx(d):
        return over_ty(2, d, gx.at[rows(ty, sub)], gx.at[rows(ty, sub)])

    spread("ty", n_ty, lambda d: cx(d).start())
    spread("tx", n_tx, lambda d: by(d).wait())
    gy[rows(tx, sub)] = scale * lax.fori_loop(1, n_tx, lambda d, t: t + rby[d], sy[rows(tx, sub)])

    def cy(d):
        return over_tx(2, d, gy.at[rows(tx, sub)], gy.at[rows(tx, sub)])

    spread("tx", n_tx, lambda d: cy(d).start())
    cross.wait()
    edge[...] = (edge[...].astype(f32) + arrived[...].astype(f32)).astype(bf)
    pieces[0].start()
    spread("ty", n_ty, lambda d: cx(d).wait())
    hx[...] = gx[...].astype(bf)

    def dx(d):
        return over_tx(3, d, hx, probe_o.at[0, rows(tx, nx)])

    spread("tx", n_tx, lambda d: dx(d).start())
    probe_o[0, rows(tx, nx)] = hx[...]
    spread("tx", n_tx, lambda d: cy(d).wait())
    hy[...] = gy[...].astype(bf)

    def dy(d):
        return over_ty(3, d, hy, probe_o.at[1, rows(ty, ny)])

    spread("ty", n_ty, lambda d: dy(d).start())
    pieces[3].start()
    probe_o[1, rows(ty, ny)] = hy[...]
    spread("tx", n_tx, lambda d: dx(d).wait())
    spread("ty", n_ty, lambda d: dy(d).wait())
    for h in (side, *pieces):
        h.wait()


def finish(total, down, right, corner, scale, n_ty, n_tx):
    nx, ny, sub = ROWS // n_tx, ROWS // n_ty, ROWS // n_tx // n_ty
    vmem = pl.BlockSpec(memory_space=pltpu.VMEM)
    hbm = pl.BlockSpec(memory_space=pl.ANY)
    dma = pltpu.SemaphoreType.DMA
    return pl.pallas_call(
        functools.partial(finish_kernel, n_ty, n_tx, scale),
        out_shape=[like((2, ROWS, H), bf), like(down.shape, bf), like(right.shape, bf)],
        in_specs=[vmem, hbm, hbm, hbm],
        out_specs=[vmem, hbm, hbm],
        scratch_shapes=[
            pltpu.VMEM((2, ROWS, H), bf), pltpu.VMEM((n_tx, nx, H), bf), pltpu.VMEM((n_ty, ny, H), bf),
            pltpu.VMEM((nx, H), f32), pltpu.VMEM((ny, H), f32), pltpu.VMEM((n_ty, sub, H), f32), pltpu.VMEM((n_tx, sub, H), f32),
            pltpu.VMEM((nx, H), f32), pltpu.VMEM((ny, H), f32), pltpu.VMEM((nx, H), bf), pltpu.VMEM((ny, H), bf),
            pltpu.VMEM((2, N, N), bf), pltpu.VMEM((2, N, N), bf),
            dma((4, n_ty)), dma((4, n_ty)), dma((4, n_tx)), dma((4, n_tx)), dma((PIECES + 2,)), dma((PIECES + 2,)), dma],
        compiler_params=pltpu.CompilerParams(collective_id=1, has_side_effects=True, vmem_limit_bytes=VMEM_LIMIT),
    )(total.reshape(2, ROWS, H), down, right, corner)


def close_kernel(main, down, right, probe, object_o, probe_o):
    b = pl.program_id(1)

    @pl.when(b == 0)
    def _():
        object_o[0, :, 0:N] = main[0, :, 0:N] + (down[0, :, 0:N].astype(f32) + right[0].astype(f32))
        object_o[0, :, N:TILE_C] = main[0, :, N:TILE_C] + down[0, :, N:TILE_C].astype(f32)

    @pl.when(b == 1)
    def _():
        object_o[0, :, 0:N] = main[0, :, 0:N] + right[0].astype(f32)
        object_o[0, :, N:TILE_C] = main[0, :, N:TILE_C]

    for m in (0, 1):
        for t in (0, 1):
            at = (2 * m + t) * N
            probe_o[0, m, :, t * H:t * H + H] = probe[0, at:at + N].astype(f32)


def close(main, down, right, probe):
    def spec(*shape):
        return pl.BlockSpec((1, *shape), lambda c, b: (c, b) + (0,) * (len(shape) - 1))

    return pl.pallas_call(
        close_kernel,
        out_shape=[like(main.shape, f32), like((2, 4, N, N), f32)],
        grid=(2, TILE_R // N),
        in_specs=[spec(N, TILE_C), pl.BlockSpec((1, N, TILE_C), lambda c, b: (c, 0, 0)), spec(N, N), spec(ROWS // 2, H)],
        out_specs=[spec(N, TILE_C), spec(2, N, N)],
        compiler_params=pltpu.CompilerParams(vmem_limit_bytes=VMEM_LIMIT),
    )(main, down, right, probe)


def on_device(specimen, probe, amplitude, offsets):
    n_ty, n_tx = lax.axis_size("ty"), lax.axis_size("tx")
    positions = offsets.shape[0] * n_ty * n_tx
    everyone, lower, right, corner, arranged = gather(offsets.reshape(-1), specimen, probe, n_ty, n_tx)
    slots, places = prepare(everyone, amplitude, n_ty)
    slots, places = lax.optimization_barrier((slots, places))
    arrived = lax.all_to_all(slots, "ty", split_axis=0, concat_axis=0, tiled=True)
    tables = make_tables()
    far, pat, inten = forward(places, specimen, right, lower, corner, arranged, tables, n_ty)
    main, down, rt, cn, total = backward(places, arranged, tables, arrived, far, pat, inten, n_ty)
    scale = float(probe.shape[1] / np.sqrt(positions))
    probe_grad, down, rt = finish(total, down, rt, cn, scale, n_ty, n_tx)
    object_grad, probe_grad = close(main, down, rt, probe_grad)
    return (object_grad, probe_grad)


def solution(mesh):
    in_specs = (P(None, "ty", "tx"), P(), P(("ty", "tx"), None, None), P(("ty", "tx"), None))
    out_specs = (P(None, "ty", "tx"), P())
    return jax.shard_map(on_device, mesh=mesh, in_specs=in_specs, out_specs=out_specs, check_vma=False)
```

```python
import functools

import jax
import jax.numpy as jnp
import ml_dtypes
import numpy as np
from jax import lax
from jax.experimental import pallas as pl
from jax.experimental.pallas import tpu as pltpu
from jax.sharding import PartitionSpec as P

bf = jnp.bfloat16
f32 = jnp.float32
N = 256
H = 128
TILE_R = 512
TILE_C = 1024
POS = 12
VMEM_LIMIT = 60 * 2**20
ROWS = 4096
ROWS_X = 3072
PIECES = 4
MESH = pl.DeviceIdType.MESH
S = 2
B = 16 // S

def row0(i):
    return i // S * 8 * S + i % S

def make_tables():
    k = np.arange(N)
    ang = ((k[:, None] * k[None, :]) % N).astype(np.float64) * (2 * np.pi / N)
    re = (np.cos(ang) / 16).astype(np.float32).astype(ml_dtypes.bfloat16).astype(np.float32)
    im = (-np.sin(ang) / 16).astype(np.float32).astype(ml_dtypes.bfloat16).astype(np.float32)
    order = np.arange(128).reshape(B, 8, S).swapaxes(1, 2).reshape(-1)
    def mix(a, b):
        return np.stack([a.reshape(16, 8, -1), b.reshape(16, 8, -1)], 1).reshape(256, -1)
    out = []
    for par in (0, 1):
        r, i = re[:H, par::2], im[:H, par::2]
        out.append(np.block([[r, i], [-i, r]]))
    for par in (0, 1):
        r, i = re[par::2][:, order], im[par::2][:, order]
        out.append(mix(np.block([r, -i]), np.block([i, r])))
    for par in (0, 1):
        r, i = re[par::2, :H], -im[par::2, :H]
        out.append(np.block([[r, i], [-i, r]]))
    for par in (0, 1):
        r, i = re[order][:, par::2], -im[order][:, par::2]
        out.append(mix(np.block([r, -i]), np.block([i, r])))
    return np.stack(out).astype(ml_dtypes.bfloat16)

def dot(a, b):
    return jnp.dot(a, b, preferred_element_type=f32)

def halves(x):
    x = x.reshape(16, 2, 8, x.shape[-1])
    return x[:, 0].reshape(128, x.shape[-1]), x[:, 1].reshape(128, x.shape[-1])


def parity_matrix():
    order = np.concatenate([np.arange(0, N, 2), np.arange(1, N, 2)])
    return np.eye(N)[order].astype(ml_dtypes.bfloat16)


def prep_kernel(off, amp, out, sem):
    ty = lax.axis_index("ty")
    copies = []
    for i in range(POS):
        tile = off[ty, 0, 2 * i] // TILE_R
        rank = jnp.int32(0)
        for j in range(i):
            rank = rank + (off[ty, 0, 2 * j] // TILE_R == tile).astype(jnp.int32)
        copies.append(pltpu.make_async_copy(amp.at[i], out.at[tile, rank], sem.at[i]))
        copies[i].start()
    for copy in copies:
        copy.wait()


def prepare(everyone, amplitude, sources):
    hbm = pl.BlockSpec(memory_space=pl.ANY)
    return pl.pallas_call(
        prep_kernel,
        out_shape=jax.ShapeDtypeStruct((sources, 2, N, N), bf),
        in_specs=[pl.BlockSpec(memory_space=pltpu.SMEM), hbm],
        out_specs=hbm,
        scratch_shapes=[pltpu.SemaphoreType.DMA((POS,))],
    )(everyone, amplitude)


def scan(off, source, places):
    ty = lax.axis_index("ty")
    rows, cols = [jnp.int32(-1)] * 2, [jnp.int32(0)] * 2
    seen = jnp.int32(0)
    for i in range(POS):
        r, c = off[source, 0, 2 * i], off[source, 0, 2 * i + 1]
        mine = r // TILE_R == ty
        for q in range(2):
            take = mine & (seen == q)
            rows[q] = jnp.where(take, r % TILE_R, rows[q])
            cols[q] = jnp.where(take, c % TILE_C, cols[q])
        seen = seen + mine.astype(jnp.int32)
    for q in range(2):
        places[source * 4 + 2 * q] = rows[q]
        places[source * 4 + 2 * q + 1] = cols[q]
    return rows, cols


def find(places, source):
    return [places[4 * source], places[4 * source + 2]], [places[4 * source + 1], places[4 * source + 3]]


def p1(probe, pat, A):
    pr, pi = probe[0], probe[1]
    qr, qi = pat[0], pat[1]
    er = pr * qr - pi * qi
    ei = pr * qi + pi * qr
    A[0, :, :H] = (er[:, :H] + er[:, H:]).astype(bf)
    A[0, :, H:] = (ei[:, :H] + ei[:, H:]).astype(bf)
    A[1, :, :H] = (er[:, :H] - er[:, H:]).astype(bf)
    A[1, :, H:] = (ei[:, :H] - ei[:, H:]).astype(bf)


def p2(tab, A, Bb):
    for p in (0, 1):
        t, b = halves(dot(A[p], tab[p]))
        s = (t + b).astype(bf)
        d = (t - b).astype(bf)
        ls = slice(p * H, p * H + H)
        Bb[0, :H, ls] = s[:, :H]
        Bb[0, H:, ls] = s[:, H:]
        Bb[1, :H, ls] = d[:, :H]
        Bb[1, H:, ls] = d[:, H:]


def p3(first, tab, Bb, far, inten):
    for p in (0, 1):
        r, i = halves(dot(tab[2 + p], Bb[p]))
        far[p, 0] = r
        far[p, 1] = i
        t = r * r + i * i
        inten[p] = t if first else inten[p] + t


def p4(amp, inten, fac):
    for p in (0, 1):
        a = amp[p * H:(p + 1) * H].astype(f32)
        fac[p] = 1.0 - a * lax.rsqrt(jnp.maximum(inten[p], 0.25))


def p5(far, fac, C):
    for p in (0, 1):
        f = fac[p]
        rr = (far[p, 0] * f).astype(bf)
        ri = (far[p, 1] * f).astype(bf)
        rs = slice(p * H, p * H + H)
        C[0, rs, :H] = rr[:, :H]
        C[0, rs, H:] = ri[:, :H]
        C[1, rs, :H] = rr[:, H:]
        C[1, rs, H:] = ri[:, H:]


def p6(tab, C, G):
    e = dot(C[0], tab[4])
    o = dot(C[1], tab[5])
    s = (e + o).astype(bf)
    d = (e - o).astype(bf)
    for p in (0, 1):
        rs = slice(p * H, p * H + H)
        G[p, :H, :H] = s[rs, :H]
        G[p, :H, H:] = d[rs, :H]
        G[p, H:, :H] = s[rs, H:]
        G[p, H:, H:] = d[rs, H:]


def both(a, b):
    return jnp.stack([a.reshape(16, 8, 256), b.reshape(16, 8, 256)], 1).reshape(256, 256)


def p7(first, tab, G, probe, pat, grad, total, m):
    er, ei = halves(dot(tab[6], G[0]))
    r_, i_ = halves(dot(tab[7], G[1]))
    br = both(er + r_, er - r_)
    bi = both(ei + i_, ei - i_)
    pr, pi = probe[0], probe[1]
    qr, qi = pat[0], pat[1]
    gr = pr * br + pi * bi
    gi = pr * bi - pi * br
    grad[0] = gr if first else grad[0] + gr
    grad[1] = gi if first else grad[1] + gi
    total[0, m] += qr * br + qi * bi
    total[1, m] += qr * bi - qi * br


def fetch(ext, pat, r, c):
    ct = c // 128
    sh = c % 128
    lane = lax.broadcasted_iota(jnp.int32, (128, 128), 1)
    keep = lane < 128 - sh
    for k in (0, 1):
        for h in (0, 1):
            x = []
            for t in range(3):
                v = jnp.concatenate([ext[k, ct + t, pl.ds(r + 128 * h + row0(i), 8, stride=S)] for i in range(16)], axis=0)
                x.append(pltpu.roll(v, 128 - sh, axis=1))
            for t in (0, 1):
                y = jnp.where(keep, x[t], x[t + 1])
                for i in range(16):
                    pat[k, 16 * i + 8 * h:16 * i + 8 * h + 8, t * H:t * H + H] = y[8 * i:8 * i + 8]

def deposit(grid, grad, r, c):
    ct = c // 128
    sh = c % 128
    lane = lax.broadcasted_iota(jnp.int32, (256, 128), 1)
    keep = lane >= sh
    for k in (0, 1):
        x = grad[k].astype(bf).astype(f32)
        a = pltpu.roll(x[:, :H], sh, axis=1)
        b = pltpu.roll(x[:, H:], sh, axis=1)
        z = jnp.zeros_like(a)
        for t, y in enumerate((jnp.where(keep, a, z), jnp.where(keep, b, a), jnp.where(keep, z, b))):
            for i in range(16):
                for h in (0, 1):
                    ds = pl.ds(r + 128 * h + row0(i), 8, stride=S)
                    grid[k, ct + t, ds] = grid[k, ct + t, ds] + y[16 * i + 8 * h:16 * i + 8 * h + 8]


def forward_kernel(off, spec, right, lower, corner, probe, tab, far, pat, inten, places, ext, A, Bb):
    s = pl.program_id(0)

    @pl.when(s == 0)
    def _():
        for c in (0, 1):
            for t in range(10):
                ls = slice(t * H, t * H + H)
                l2 = slice(t * H - 1024, t * H - 1024 + H)
                ext[c, t, :512] = (spec[c, :, ls] if t < 8 else right[c, :, l2]).astype(bf).astype(f32)
                ext[c, t, 512:] = (lower[c, :, ls] if t < 8 else corner[c, :, l2]).astype(f32)

    rows, cols = scan(off, s, places)

    @pl.when(rows[0] >= 0)
    def _():
        items = [(q, m) for q in range(2) for m in range(4)]
        for t in range(len(items) + 2):
            if 0 <= t - 1 < len(items):
                q, m = items[t - 1]
                p2(tab, A.at[q, m], Bb.at[q, m])
            if 0 <= t - 2 < len(items):
                q, m = items[t - 2]
                p3(m == 0, tab, Bb.at[q, m], far.at[0, q, m], inten.at[0, q])
            if t < len(items):
                q, m = items[t]
                if m == 0:
                    fetch(ext, pat.at[0, q], rows[q], cols[q])
                p1(probe.at[:, m], pat.at[0, q], A.at[q, m])


def backward_kernel(off, probe, tab, amp, far, pat, inten, main_o, down_o, right_o, corner_o, total_o, grid, total, fac, C, G, grad):
    s = pl.program_id(0)

    @pl.when(s == 0)
    def _():
        grid[...] = jnp.zeros_like(grid)
        total[...] = jnp.zeros_like(total)

    rows, cols = find(off, s)

    @pl.when(rows[0] >= 0)
    def _():
        items = [(q, m) for q in range(2) for m in range(4)]
        for t in range(len(items) + 2):
            if 0 <= t - 1 < len(items):
                q, m = items[t - 1]
                p6(tab, C.at[q, m], G.at[q, m])
            if 0 <= t - 2 < len(items):
                q, m = items[t - 2]
                p7(m == 0, tab, G.at[q, m], probe.at[:, m], pat.at[0, q], grad.at[q], total, m)
                if m == 3:
                    deposit(grid, grad.at[q], rows[q], cols[q])
            if t < len(items):
                q, m = items[t]
                if m == 0:
                    p4(amp.at[0, q], inten.at[0, q], fac.at[q])
                p5(far.at[0, q, m], fac.at[q], C.at[q, m])

    @pl.when(s == pl.num_programs(0) - 1)
    def _():
        for c in (0, 1):
            for t in range(10):
                ls = slice(t * H, t * H + H)
                l2 = slice(t * H - 1024, t * H - 1024 + H)
                if t < 8:
                    main_o[c, :, ls] = grid[c, t, :512]
                    down_o[c, :, ls] = grid[c, t, 512:].astype(bf)
                else:
                    right_o[c, :, l2] = grid[c, t, :512].astype(bf)
                    corner_o[c, :, l2] = grid[c, t, 512:].astype(bf)
            for m in range(4):
                for i in range(32):
                    for t in range(2):
                        ds = pl.ds(128 * (i % 2) + row0(i // 2), 8, stride=S)
                        total_o[c, m, t, ds] = total[c, m, 8 * i:8 * i + 8, t * H:t * H + H]


def whole(*shape):
    return pl.BlockSpec(shape, lambda i, o: (0,) * len(shape), pipeline_mode=pl.Buffered(1))


def each(*shape):
    return pl.BlockSpec((1, *shape), lambda i, o: (i,) + (0,) * len(shape))


def like(shape, dtype):
    return jax.ShapeDtypeStruct(shape, dtype)


def forward(off, spec, right, lower, corner, probe, tab, sources):
    return pl.pallas_call(
        forward_kernel,
        out_shape=[like((sources, 2, 4, 2, 2, 128, 256), f32), like((sources, 2, 2, 256, 256), f32), like((sources, 2, 2, 128, 256), f32),
                   like((4 * sources,), jnp.int32)],
        grid_spec=pltpu.PrefetchScalarGridSpec(
            num_scalar_prefetch=1, grid=(sources,),
            in_specs=[whole(2, 512, 1024), whole(2, 512, 256), whole(2, 256, 1024), whole(2, 256, 256), whole(2, 4, 256, 256), whole(8, 256, 256)],
            out_specs=[each(2, 4, 2, 2, 128, 256), each(2, 2, 256, 256), each(2, 2, 128, 256), pl.BlockSpec(memory_space=pltpu.SMEM)],
            scratch_shapes=[pltpu.VMEM((2, 10, 768, 128), f32), pltpu.VMEM((2, 4, 2, 256, 256), bf), pltpu.VMEM((2, 4, 2, 256, 256), bf)]),
        compiler_params=pltpu.CompilerParams(vmem_limit_bytes=VMEM_LIMIT),
        cost_estimate=pl.CostEstimate(flops=32 * 2**29, bytes_accessed=100 * 2**20, transcendentals=0),
    )(off, spec, right, lower, corner, probe, tab)


def backward(off, probe, tab, amp, far, pat, inten, sources):
    return pl.pallas_call(
        backward_kernel,
        out_shape=[like((2, 512, 1024), f32), like((2, 256, 1024), bf), like((2, 512, 256), bf), like((2, 256, 256), bf), like((2, 4, 2, 256, 128), f32)],
        grid_spec=pltpu.PrefetchScalarGridSpec(
            num_scalar_prefetch=1, grid=(sources,),
            in_specs=[whole(2, 4, 256, 256), whole(8, 256, 256), each(2, 256, 256), each(2, 4, 2, 2, 128, 256), each(2, 2, 256, 256), each(2, 2, 128, 256)],
            out_specs=[whole(2, 512, 1024), whole(2, 256, 1024), whole(2, 512, 256), whole(2, 256, 256), whole(2, 4, 2, 256, 128)],
            scratch_shapes=[pltpu.VMEM((2, 10, 768, 128), f32), pltpu.VMEM((2, 4, 256, 256), f32), pltpu.VMEM((2, 2, 128, 256), f32), pltpu.VMEM((2, 4, 2, 256, 256), bf),
                            pltpu.VMEM((2, 4, 2, 256, 256), bf), pltpu.VMEM((2, 2, 256, 256), f32)]),
        compiler_params=pltpu.CompilerParams(vmem_limit_bytes=VMEM_LIMIT),
        cost_estimate=pl.CostEstimate(flops=32 * 2**29, bytes_accessed=100 * 2**20, transcendentals=0),
    )(off, probe, tab, amp, far, pat, inten)


def spread(axis, size, reach):
    lax.fori_loop(1, size, lambda d, c: (reach(d), c)[1], 0)


def beyond(axis, d, size):
    place = {"ty": lax.axis_index("ty"), "tx": lax.axis_index("tx")}
    place[axis] = lax.rem(place[axis] + d, size)
    return (place["ty"], place["tx"])


def gather_kernel(n_ty, n_tx, own, spec, probe, amp, perm, out, lower_o, right_o, corner_o, probe_o, amp_o,
                  top, side, half_top, half_side, split, raw, send, recv, send_h, recv_h, sem):
    ty, tx = lax.axis_index("ty"), lax.axis_index("tx")
    above, left = lax.rem(ty + n_ty - 1, n_ty), lax.rem(tx + n_tx - 1, n_tx)
    barrier = pltpu.get_barrier_semaphore()

    def greet(device):
        pl.semaphore_signal(barrier, inc=1, device_id=device, device_id_type=MESH)

    spread("ty", n_ty, lambda d: greet(beyond("ty", d, n_ty)))
    greet((ty, lax.rem(tx + 1, n_tx)))
    load_side = pltpu.make_async_copy(spec.at[:, :, 0:N], side, sem.at[0])
    load_top = pltpu.make_async_copy(spec.at[:, 0:N], top, sem.at[1])
    load_top.start()
    load_side.start()
    load_raw = pltpu.make_async_copy(amp, raw, sem.at[2])
    load_raw.start()
    pl.semaphore_wait(barrier, n_ty)

    def copy(d):
        return pltpu.make_async_remote_copy(
            src_ref=own, dst_ref=out.at[ty], send_sem=send.at[d], recv_sem=recv.at[d],
            device_id=beyond("ty", d, n_ty), device_id_type=MESH)

    def halo(k, src, dst, device):
        return pltpu.make_async_remote_copy(
            src_ref=src, dst_ref=dst, send_sem=send_h.at[k], recv_sem=recv_h.at[k], device_id=device, device_id_type=MESH)

    spread("ty", n_ty, lambda d: copy(d).start())
    out[ty] = own[...]
    load_top.wait()
    half_top[:, :, 0:N] = top[:, :, 0:N].astype(bf)
    first = halo(0, half_top.at[:, :, 0:N], lower_o.at[:, :, 0:N], (above, tx))
    first.start()
    half_top[:, :, N:TILE_C] = top[:, :, N:TILE_C].astype(bf)
    rest = halo(1, half_top.at[:, :, N:TILE_C], lower_o.at[:, :, N:TILE_C], (above, tx))
    rest.start()
    load_side.wait()
    half_side[...] = side[...].astype(bf)
    right = halo(2, half_side, right_o, (ty, left))
    right.start()
    first.wait()
    corner = halo(3, lower_o.at[:, :, 0:N], corner_o, (ty, left))
    corner.start()
    for c in (0, 1):
        for t in (0, 1):
            split[c, :, t] = probe[c, :, :, t * H:t * H + H]
    for c in (0, 1):
        for m in range(4):
            for t in (0, 1):
                for i in range(32):
                    ds = pl.ds(128 * (i % 2) + row0(i // 2), 8, stride=S)
                    probe_o[c, m, 8 * i:8 * i + 8, t * H:t * H + H] = split[c, m, t, ds]
    load_raw.wait()

    def reorder(i, carry):
        a = dot(perm[...], raw[i].astype(bf)).astype(bf)
        amp_o[i] = lax.dot_general(a, perm[...], (((1,), (1,)), ((), ())), preferred_element_type=f32).astype(bf)
        return carry

    lax.fori_loop(0, POS, reorder, 0)
    spread("ty", n_ty, lambda d: copy(d).wait())
    right.wait()
    corner.wait()
    rest.wait()


def gather(offsets, specimen, probe, amplitude, n_ty, n_tx):
    own = jnp.pad(offsets.reshape(1, 2 * POS), ((0, 7), (0, 128 - 2 * POS)))
    vmem = pl.BlockSpec(memory_space=pltpu.VMEM)
    hbm = pl.BlockSpec(memory_space=pl.ANY)
    dma = pltpu.SemaphoreType.DMA
    return pl.pallas_call(
        functools.partial(gather_kernel, n_ty, n_tx),
        out_shape=[like((n_ty, 8, 128), jnp.int32), like((2, N, TILE_C), bf), like((2, TILE_R, N), bf), like((2, N, N), bf),
                   like(probe.shape, f32), like(amplitude.shape, bf)],
        in_specs=[vmem, hbm, vmem, hbm, vmem],
        out_specs=[vmem, hbm, hbm, hbm, vmem, vmem],
        scratch_shapes=[
            pltpu.VMEM((2, N, TILE_C), f32), pltpu.VMEM((2, TILE_R, N), f32),
            pltpu.VMEM((2, N, TILE_C), bf), pltpu.VMEM((2, TILE_R, N), bf), pltpu.VMEM((2, 4, 2, N, H), f32),
            pltpu.VMEM(amplitude.shape, f32), dma((n_ty,)), dma((n_ty,)), dma((4,)), dma((4,)), dma((3,))],
        compiler_params=pltpu.CompilerParams(collective_id=0, has_side_effects=True, vmem_limit_bytes=VMEM_LIMIT),
    )(own, specimen, probe, amplitude, parity_matrix())


def finish_kernel(n_ty, n_tx, scale, total, down, right, corner, probe_o, down_o, right_o,
                  cast, rax, ray, sx, sy, rbx, rby, gx, gy, hx, hy, arrived, edge, send_ty, recv_ty, send_tx, recv_tx, send_h, recv_h, sem):
    ty, tx = lax.axis_index("ty"), lax.axis_index("tx")
    nx, ny = ROWS_X // n_tx, (ROWS - ROWS_X) // n_ty
    ux, uy = nx // n_ty, ny // n_tx
    barrier = pltpu.get_barrier_semaphore()

    def greet(device):
        pl.semaphore_signal(barrier, inc=1, device_id=device, device_id_type=MESH)

    spread("ty", n_ty, lambda d: greet(beyond("ty", d, n_ty)))
    spread("tx", n_tx, lambda d: greet(beyond("tx", d, n_tx)))
    load = pltpu.make_async_copy(down.at[:, :, 0:N], edge, sem)
    load.start()
    cast[...] = total[...].astype(bf)
    load.wait()
    pl.semaphore_wait(barrier, n_ty + n_tx - 2)

    def over_ty(stage, d, src, dst):
        return pltpu.make_async_remote_copy(
            src_ref=src, dst_ref=dst, send_sem=send_ty.at[stage, d], recv_sem=recv_ty.at[stage, d],
            device_id=beyond("ty", d, n_ty), device_id_type=MESH)

    def over_tx(stage, d, src, dst):
        return pltpu.make_async_remote_copy(
            src_ref=src, dst_ref=dst, send_sem=send_tx.at[stage, d], recv_sem=recv_tx.at[stage, d],
            device_id=beyond("tx", d, n_tx), device_id_type=MESH)

    def rows(k, n, first=0):
        return pl.ds(pl.multiple_of(first + k * n, 8), n)

    def halo(k, src, dst, device):
        return pltpu.make_async_remote_copy(
            src_ref=src, dst_ref=dst, send_sem=send_h.at[k], recv_sem=recv_h.at[k], device_id=device, device_id_type=MESH)

    below, beside = lax.rem(ty + 1, n_ty), lax.rem(tx + 1, n_tx)
    cross = halo(0, corner, arrived, (ty, beside))
    side = halo(1, right, right_o, (ty, beside))
    pieces = [halo(2 + k, edge if k == 0 else down.at[:, :, k * N:k * N + N], down_o.at[:, :, k * N:k * N + N], (below, tx)) for k in range(PIECES)]
    cross.start()
    side.start()

    def ax(d):
        peer = lax.rem(tx + d, n_tx)
        return over_tx(0, d, cast.at[rows(peer, nx)], rax.at[d])

    def ay(d):
        peer = lax.rem(ty + d, n_ty)
        return over_ty(0, d, cast.at[rows(peer, ny, ROWS_X)], ray.at[d])

    spread("tx", n_tx, lambda d: ax(d).start())
    spread("ty", n_ty, lambda d: ay(d).start())
    pieces[1].start()
    pieces[2].start()
    spread("tx", n_tx, lambda d: ax(d).wait())
    sx[...] = lax.fori_loop(1, n_tx, lambda d, t: t + rax[d].astype(f32), total[rows(tx, nx)])

    def bx(d):
        peer = lax.rem(ty + d, n_ty)
        return over_ty(1, d, sx.at[rows(peer, ux)], rbx.at[d])

    spread("ty", n_ty, lambda d: bx(d).start())
    spread("ty", n_ty, lambda d: ay(d).wait())
    sy[...] = lax.fori_loop(1, n_ty, lambda d, t: t + ray[d].astype(f32), total[rows(ty, ny, ROWS_X)])

    def by(d):
        peer = lax.rem(tx + d, n_tx)
        return over_tx(1, d, sy.at[rows(peer, uy)], rby.at[d])

    spread("tx", n_tx, lambda d: by(d).start())
    pieces[3].start()
    spread("ty", n_ty, lambda d: bx(d).wait())
    gx[rows(ty, ux)] = scale * lax.fori_loop(1, n_ty, lambda d, t: t + rbx[d], sx[rows(ty, ux)])

    def cx(d):
        return over_ty(2, d, gx.at[rows(ty, ux)], gx.at[rows(ty, ux)])

    spread("ty", n_ty, lambda d: cx(d).start())
    spread("tx", n_tx, lambda d: by(d).wait())
    gy[rows(tx, uy)] = scale * lax.fori_loop(1, n_tx, lambda d, t: t + rby[d], sy[rows(tx, uy)])

    def cy(d):
        return over_tx(2, d, gy.at[rows(tx, uy)], gy.at[rows(tx, uy)])

    spread("tx", n_tx, lambda d: cy(d).start())
    cross.wait()
    edge[...] = (edge[...].astype(f32) + arrived[...].astype(f32)).astype(bf)
    pieces[0].start()
    spread("ty", n_ty, lambda d: cx(d).wait())
    hx[...] = gx[...].astype(bf)

    def dx(d):
        return over_tx(3, d, hx, probe_o.at[rows(tx, nx)])

    spread("tx", n_tx, lambda d: dx(d).start())
    probe_o[rows(tx, nx)] = hx[...]
    spread("tx", n_tx, lambda d: cy(d).wait())
    hy[...] = gy[...].astype(bf)

    def dy(d):
        return over_ty(3, d, hy, probe_o.at[rows(ty, ny, ROWS_X)])

    spread("ty", n_ty, lambda d: dy(d).start())
    probe_o[rows(ty, ny, ROWS_X)] = hy[...]
    spread("tx", n_tx, lambda d: dx(d).wait())
    spread("ty", n_ty, lambda d: dy(d).wait())
    for h in (side, *pieces):
        h.wait()


def finish(total, down, right, corner, scale, n_ty, n_tx):
    nx, ny = ROWS_X // n_tx, (ROWS - ROWS_X) // n_ty
    vmem = pl.BlockSpec(memory_space=pltpu.VMEM)
    hbm = pl.BlockSpec(memory_space=pl.ANY)
    dma = pltpu.SemaphoreType.DMA
    return pl.pallas_call(
        functools.partial(finish_kernel, n_ty, n_tx, scale),
        out_shape=[like((ROWS, H), bf), like(down.shape, bf), like(right.shape, bf)],
        in_specs=[vmem, hbm, hbm, hbm],
        out_specs=[vmem, hbm, hbm],
        scratch_shapes=[
            pltpu.VMEM((ROWS, H), bf), pltpu.VMEM((n_tx, nx, H), bf), pltpu.VMEM((n_ty, ny, H), bf),
            pltpu.VMEM((nx, H), f32), pltpu.VMEM((ny, H), f32), pltpu.VMEM((n_ty, nx // n_ty, H), f32), pltpu.VMEM((n_tx, ny // n_tx, H), f32),
            pltpu.VMEM((nx, H), f32), pltpu.VMEM((ny, H), f32), pltpu.VMEM((nx, H), bf), pltpu.VMEM((ny, H), bf),
            pltpu.VMEM((2, N, N), bf), pltpu.VMEM((2, N, N), bf),
            dma((4, n_ty)), dma((4, n_ty)), dma((4, n_tx)), dma((4, n_tx)), dma((PIECES + 2,)), dma((PIECES + 2,)), dma],
        compiler_params=pltpu.CompilerParams(collective_id=1, has_side_effects=True, vmem_limit_bytes=VMEM_LIMIT),
    )(total.reshape(ROWS, H), down, right, corner)


def close_kernel(main, down, right, probe, object_o, probe_o):
    b = pl.program_id(1)

    @pl.when(b == 0)
    def _():
        object_o[0, :, 0:N] = main[0, :, 0:N] + (down[0, :, 0:N].astype(f32) + right[0].astype(f32))
        object_o[0, :, N:TILE_C] = main[0, :, N:TILE_C] + down[0, :, N:TILE_C].astype(f32)

    @pl.when(b == 1)
    def _():
        object_o[0, :, 0:N] = main[0, :, 0:N] + right[0].astype(f32)
        object_o[0, :, N:TILE_C] = main[0, :, N:TILE_C]

    for m in (0, 1):
        for t in (0, 1):
            at = (2 * m + t) * N
            probe_o[0, m, :, t * H:t * H + H] = probe[0, at:at + N].astype(f32)


def close(main, down, right, probe):
    def spec(*shape):
        return pl.BlockSpec((1, *shape), lambda c, b: (c, b) + (0,) * (len(shape) - 1))

    return pl.pallas_call(
        close_kernel,
        out_shape=[like(main.shape, f32), like((2, 4, N, N), f32)],
        grid=(2, TILE_R // N),
        in_specs=[spec(N, TILE_C), pl.BlockSpec((1, N, TILE_C), lambda c, b: (c, 0, 0)), spec(N, N), spec(ROWS // 4, H)],
        out_specs=[spec(N, TILE_C), spec(2, N, N)],
        compiler_params=pltpu.CompilerParams(vmem_limit_bytes=VMEM_LIMIT),
    )(main, down, right, probe.reshape(2, ROWS // 2, H))


def on_device(specimen, probe, amplitude, offsets):
    n_ty, n_tx = lax.axis_size("ty"), lax.axis_size("tx")
    positions = offsets.shape[0] * n_ty * n_tx
    everyone, lower, right, corner, arranged, sorted_amp = gather(offsets.reshape(-1), specimen, probe, amplitude, n_ty, n_tx)
    slots = prepare(everyone, sorted_amp, n_ty)
    arrived = lax.all_to_all(slots, "ty", split_axis=0, concat_axis=0, tiled=True)
    tables = make_tables()
    far, pat, inten, places = forward(everyone, specimen, right, lower, corner, arranged, tables, n_ty)
    main, down, rt, cn, total = backward(places, arranged, tables, arrived, far, pat, inten, n_ty)
    scale = float(probe.shape[1] / np.sqrt(positions))
    probe_grad, down, rt = finish(total, down, rt, cn, scale, n_ty, n_tx)
    object_grad, probe_grad = close(main, down, rt, probe_grad)
    return (object_grad, probe_grad)


def solution(mesh):
    in_specs = (P(None, "ty", "tx"), P(), P(("ty", "tx"), None, None), P(("ty", "tx"), None))
    out_specs = (P(None, "ty", "tx"), P())
    return jax.shard_map(on_device, mesh=mesh, in_specs=in_specs, out_specs=out_specs, check_vma=False)
```

```python
import functools

import jax
import jax.numpy as jnp
import ml_dtypes
import numpy as np
from jax import lax
from jax.experimental import pallas as pl
from jax.experimental.pallas import tpu as pltpu
from jax.sharding import PartitionSpec as P

bf = jnp.bfloat16
f32 = jnp.float32
N = 256
H = 128
TILE_R = 512
TILE_C = 1024
POS = 12
VMEM_LIMIT = 60 * 2**20
ROWS = 4096
ROWS_X = 3072
PIECES = 4
MESH = pl.DeviceIdType.MESH
S = 2
B = 16 // S

def row0(i):
    return i // S * 8 * S + i % S

def make_tables():
    k = np.arange(N)
    ang = ((k[:, None] * k[None, :]) % N).astype(np.float64) * (2 * np.pi / N)
    re = (np.cos(ang) / 16).astype(np.float32).astype(ml_dtypes.bfloat16).astype(np.float32)
    im = (-np.sin(ang) / 16).astype(np.float32).astype(ml_dtypes.bfloat16).astype(np.float32)
    order = np.arange(128).reshape(B, 8, S).swapaxes(1, 2).reshape(-1)
    def mix(a, b):
        return np.stack([a.reshape(16, 8, -1), b.reshape(16, 8, -1)], 1).reshape(256, -1)
    out = []
    for par in (0, 1):
        r, i = re[:H, par::2], im[:H, par::2]
        out.append(np.block([[r, i], [-i, r]]))
    for par in (0, 1):
        r, i = re[par::2][:, order], im[par::2][:, order]
        out.append(mix(np.block([r, -i]), np.block([i, r])))
    for par in (0, 1):
        r, i = re[par::2, :H], -im[par::2, :H]
        out.append(np.block([[r, i], [-i, r]]))
    for par in (0, 1):
        r, i = re[order][:, par::2], -im[order][:, par::2]
        out.append(mix(np.block([r, -i]), np.block([i, r])))
    return np.stack(out).astype(ml_dtypes.bfloat16)

def dot(a, b):
    return jnp.dot(a, b, preferred_element_type=f32)

def halves(x):
    x = x.reshape(16, 2, 8, x.shape[-1])
    return x[:, 0].reshape(128, x.shape[-1]), x[:, 1].reshape(128, x.shape[-1])


def parity_matrix():
    order = np.concatenate([np.arange(0, N, 2), np.arange(1, N, 2)])
    return np.eye(N)[order].astype(ml_dtypes.bfloat16)


def prep_kernel(off, amp, out, sem):
    ty = lax.axis_index("ty")
    copies = []
    for i in range(POS):
        tile = off[ty, 0, 2 * i] // TILE_R
        rank = jnp.int32(0)
        for j in range(i):
            rank = rank + (off[ty, 0, 2 * j] // TILE_R == tile).astype(jnp.int32)
        copies.append(pltpu.make_async_copy(amp.at[i], out.at[tile, rank], sem.at[i]))
        copies[i].start()
    for copy in copies:
        copy.wait()


def prepare(everyone, amplitude, sources):
    hbm = pl.BlockSpec(memory_space=pl.ANY)
    return pl.pallas_call(
        prep_kernel,
        out_shape=jax.ShapeDtypeStruct((sources, 2, N, N), bf),
        in_specs=[pl.BlockSpec(memory_space=pltpu.SMEM), pl.BlockSpec(memory_space=pltpu.VMEM)],
        out_specs=hbm,
        scratch_shapes=[pltpu.SemaphoreType.DMA((POS,))],
        compiler_params=pltpu.CompilerParams(vmem_limit_bytes=VMEM_LIMIT),
    )(everyone, amplitude)


def scan(off, source, places):
    ty = lax.axis_index("ty")
    rows, cols = [jnp.int32(-1)] * 2, [jnp.int32(0)] * 2
    seen = jnp.int32(0)
    for i in range(POS):
        r, c = off[source, 0, 2 * i], off[source, 0, 2 * i + 1]
        mine = r // TILE_R == ty
        for q in range(2):
            take = mine & (seen == q)
            rows[q] = jnp.where(take, r % TILE_R, rows[q])
            cols[q] = jnp.where(take, c % TILE_C, cols[q])
        seen = seen + mine.astype(jnp.int32)
    for q in range(2):
        places[source * 4 + 2 * q] = rows[q]
        places[source * 4 + 2 * q + 1] = cols[q]
    return rows, cols


def find(places, source):
    return [places[4 * source], places[4 * source + 2]], [places[4 * source + 1], places[4 * source + 3]]


def p1(probe, pat, A):
    pr, pi = probe[0], probe[1]
    qr, qi = pat[0], pat[1]
    er = pr * qr - pi * qi
    ei = pr * qi + pi * qr
    A[0, :, :H] = (er[:, :H] + er[:, H:]).astype(bf)
    A[0, :, H:] = (ei[:, :H] + ei[:, H:]).astype(bf)
    A[1, :, :H] = (er[:, :H] - er[:, H:]).astype(bf)
    A[1, :, H:] = (ei[:, :H] - ei[:, H:]).astype(bf)


def p2(tab, A, Bb):
    for p in (0, 1):
        t, b = halves(dot(A[p], tab[p]))
        s = (t + b).astype(bf)
        d = (t - b).astype(bf)
        ls = slice(p * H, p * H + H)
        Bb[0, :H, ls] = s[:, :H]
        Bb[0, H:, ls] = s[:, H:]
        Bb[1, :H, ls] = d[:, :H]
        Bb[1, H:, ls] = d[:, H:]


def p3(first, tab, Bb, far, inten):
    for p in (0, 1):
        r, i = halves(dot(tab[2 + p], Bb[p]))
        far[p, 0] = r
        far[p, 1] = i
        t = r * r + i * i
        inten[p] = t if first else inten[p] + t


def p4(amp, inten, fac):
    for p in (0, 1):
        a = amp[p * H:(p + 1) * H].astype(f32)
        fac[p] = 1.0 - a * lax.rsqrt(jnp.maximum(inten[p], 0.25))


def p5(far, fac, C):
    for p in (0, 1):
        f = fac[p]
        rr = (far[p, 0] * f).astype(bf)
        ri = (far[p, 1] * f).astype(bf)
        rs = slice(p * H, p * H + H)
        C[0, rs, :H] = rr[:, :H]
        C[0, rs, H:] = ri[:, :H]
        C[1, rs, :H] = rr[:, H:]
        C[1, rs, H:] = ri[:, H:]


def p6(tab, C, G):
    e = dot(C[0], tab[4])
    o = dot(C[1], tab[5])
    s = (e + o).astype(bf)
    d = (e - o).astype(bf)
    for p in (0, 1):
        rs = slice(p * H, p * H + H)
        G[p, :H, :H] = s[rs, :H]
        G[p, :H, H:] = d[rs, :H]
        G[p, H:, :H] = s[rs, H:]
        G[p, H:, H:] = d[rs, H:]


def both(a, b):
    return jnp.stack([a.reshape(16, 8, 256), b.reshape(16, 8, 256)], 1).reshape(256, 256)


def p7(first, tab, G, probe, pat, grad, total, m):
    er, ei = halves(dot(tab[6], G[0]))
    r_, i_ = halves(dot(tab[7], G[1]))
    br = both(er + r_, er - r_)
    bi = both(ei + i_, ei - i_)
    pr, pi = probe[0], probe[1]
    qr, qi = pat[0], pat[1]
    gr = pr * br + pi * bi
    gi = pr * bi - pi * br
    grad[0] = gr if first else grad[0] + gr
    grad[1] = gi if first else grad[1] + gi
    total[0, m] += qr * br + qi * bi
    total[1, m] += qr * bi - qi * br


def fetch(ext, pat, r, c):
    ct = c // 128
    sh = c % 128
    lane = lax.broadcasted_iota(jnp.int32, (128, 128), 1)
    keep = lane < 128 - sh
    for k in (0, 1):
        for h in (0, 1):
            x = []
            for t in range(3):
                v = jnp.concatenate([ext[k, ct + t, pl.ds(r + 128 * h + row0(i), 8, stride=S)] for i in range(16)], axis=0)
                x.append(pltpu.roll(v, 128 - sh, axis=1))
            for t in (0, 1):
                y = jnp.where(keep, x[t], x[t + 1])
                for i in range(16):
                    pat[k, 16 * i + 8 * h:16 * i + 8 * h + 8, t * H:t * H + H] = y[8 * i:8 * i + 8]

def deposit(grid, grad, r, c):
    ct = c // 128
    sh = c % 128
    lane = lax.broadcasted_iota(jnp.int32, (256, 128), 1)
    keep = lane >= sh
    for k in (0, 1):
        x = grad[k].astype(bf).astype(f32)
        a = pltpu.roll(x[:, :H], sh, axis=1)
        b = pltpu.roll(x[:, H:], sh, axis=1)
        z = jnp.zeros_like(a)
        for t, y in enumerate((jnp.where(keep, a, z), jnp.where(keep, b, a), jnp.where(keep, z, b))):
            for i in range(16):
                for h in (0, 1):
                    ds = pl.ds(r + 128 * h + row0(i), 8, stride=S)
                    grid[k, ct + t, ds] = grid[k, ct + t, ds] + y[16 * i + 8 * h:16 * i + 8 * h + 8]


def forward_kernel(off, spec, right, lower, corner, probe, tab, far, pat, inten, places, ext, A, Bb):
    s = pl.program_id(0)

    @pl.when(s == 0)
    def _():
        for c in (0, 1):
            for t in range(10):
                ls = slice(t * H, t * H + H)
                l2 = slice(t * H - 1024, t * H - 1024 + H)
                ext[c, t, :512] = (spec[c, :, ls] if t < 8 else right[c, :, l2]).astype(bf).astype(f32)
                ext[c, t, 512:] = (lower[c, :, ls] if t < 8 else corner[c, :, l2]).astype(f32)

    rows, cols = scan(off, s, places)

    @pl.when(rows[0] >= 0)
    def _():
        items = [(q, m) for q in range(2) for m in range(4)]
        for t in range(len(items) + 2):
            if 0 <= t - 1 < len(items):
                q, m = items[t - 1]
                p2(tab, A.at[q, m], Bb.at[q, m])
            if 0 <= t - 2 < len(items):
                q, m = items[t - 2]
                p3(m == 0, tab, Bb.at[q, m], far.at[0, q, m], inten.at[0, q])
            if t < len(items):
                q, m = items[t]
                if m == 0:
                    fetch(ext, pat.at[0, q], rows[q], cols[q])
                p1(probe.at[:, m], pat.at[0, q], A.at[q, m])


def backward_kernel(off, probe, tab, amp, far, pat, inten, main_o, down_o, right_o, corner_o, total_o, grid, total, fac, C, G, grad):
    s = pl.program_id(0)

    @pl.when(s == 0)
    def _():
        grid[...] = jnp.zeros_like(grid)
        total[...] = jnp.zeros_like(total)

    rows, cols = find(off, s)

    @pl.when(rows[0] >= 0)
    def _():
        items = [(q, m) for q in range(2) for m in range(4)]
        for t in range(len(items) + 2):
            if 0 <= t - 1 < len(items):
                q, m = items[t - 1]
                p6(tab, C.at[q, m], G.at[q, m])
            if 0 <= t - 2 < len(items):
                q, m = items[t - 2]
                p7(m == 0, tab, G.at[q, m], probe.at[:, m], pat.at[0, q], grad.at[q], total, m)
                if m == 3:
                    deposit(grid, grad.at[q], rows[q], cols[q])
            if t < len(items):
                q, m = items[t]
                if m == 0:
                    p4(amp.at[0, q], inten.at[0, q], fac.at[q])
                p5(far.at[0, q, m], fac.at[q], C.at[q, m])

    @pl.when(s == pl.num_programs(0) - 1)
    def _():
        for c in (0, 1):
            for t in range(10):
                ls = slice(t * H, t * H + H)
                l2 = slice(t * H - 1024, t * H - 1024 + H)
                if t < 8:
                    main_o[c, :, ls] = grid[c, t, :512]
                    down_o[c, :, ls] = grid[c, t, 512:].astype(bf)
                else:
                    right_o[c, :, l2] = grid[c, t, :512].astype(bf)
                    corner_o[c, :, l2] = grid[c, t, 512:].astype(bf)
            for m in range(4):
                for i in range(32):
                    for t in range(2):
                        ds = pl.ds(128 * (i % 2) + row0(i // 2), 8, stride=S)
                        total_o[c, m, t, ds] = total[c, m, 8 * i:8 * i + 8, t * H:t * H + H]


def whole(*shape):
    return pl.BlockSpec(shape, lambda i, o: (0,) * len(shape), pipeline_mode=pl.Buffered(1))


def each(*shape):
    return pl.BlockSpec((1, *shape), lambda i, o: (i,) + (0,) * len(shape))


def like(shape, dtype):
    return jax.ShapeDtypeStruct(shape, dtype)


def forward(off, spec, right, lower, corner, probe, tab, sources):
    return pl.pallas_call(
        forward_kernel,
        out_shape=[like((sources, 2, 4, 2, 2, 128, 256), f32), like((sources, 2, 2, 256, 256), f32), like((sources, 2, 2, 128, 256), f32),
                   like((4 * sources,), jnp.int32)],
        grid_spec=pltpu.PrefetchScalarGridSpec(
            num_scalar_prefetch=1, grid=(sources,),
            in_specs=[whole(2, 512, 1024), whole(2, 512, 256), whole(2, 256, 1024), whole(2, 256, 256), whole(2, 4, 256, 256), whole(8, 256, 256)],
            out_specs=[each(2, 4, 2, 2, 128, 256), each(2, 2, 256, 256), each(2, 2, 128, 256), pl.BlockSpec(memory_space=pltpu.SMEM)],
            scratch_shapes=[pltpu.VMEM((2, 10, 768, 128), f32), pltpu.VMEM((2, 4, 2, 256, 256), bf), pltpu.VMEM((2, 4, 2, 256, 256), bf)]),
        compiler_params=pltpu.CompilerParams(vmem_limit_bytes=VMEM_LIMIT),
        cost_estimate=pl.CostEstimate(flops=32 * 2**29, bytes_accessed=100 * 2**20, transcendentals=0),
    )(off, spec, right, lower, corner, probe, tab)


def backward(off, probe, tab, amp, far, pat, inten, sources):
    return pl.pallas_call(
        backward_kernel,
        out_shape=[like((2, 512, 1024), f32), like((2, 256, 1024), bf), like((2, 512, 256), bf), like((2, 256, 256), bf), like((2, 4, 2, 256, 128), f32)],
        grid_spec=pltpu.PrefetchScalarGridSpec(
            num_scalar_prefetch=1, grid=(sources,),
            in_specs=[whole(2, 4, 256, 256), whole(8, 256, 256), each(2, 256, 256), each(2, 4, 2, 2, 128, 256), each(2, 2, 256, 256), each(2, 2, 128, 256)],
            out_specs=[whole(2, 512, 1024), whole(2, 256, 1024), whole(2, 512, 256), whole(2, 256, 256), whole(2, 4, 2, 256, 128)],
            scratch_shapes=[pltpu.VMEM((2, 10, 768, 128), f32), pltpu.VMEM((2, 4, 256, 256), f32), pltpu.VMEM((2, 2, 128, 256), f32), pltpu.VMEM((2, 4, 2, 256, 256), bf),
                            pltpu.VMEM((2, 4, 2, 256, 256), bf), pltpu.VMEM((2, 2, 256, 256), f32)]),
        compiler_params=pltpu.CompilerParams(vmem_limit_bytes=VMEM_LIMIT),
        cost_estimate=pl.CostEstimate(flops=32 * 2**29, bytes_accessed=100 * 2**20, transcendentals=0),
    )(off, probe, tab, amp, far, pat, inten)


def spread(axis, size, reach):
    lax.fori_loop(1, size, lambda d, c: (reach(d), c)[1], 0)


def beyond(axis, d, size):
    place = {"ty": lax.axis_index("ty"), "tx": lax.axis_index("tx")}
    place[axis] = lax.rem(place[axis] + d, size)
    return (place["ty"], place["tx"])


def gather_kernel(n_ty, n_tx, own, spec, probe, amp, perm, out, lower_o, right_o, corner_o, probe_o, amp_o,
                  top, side, half_top, half_side, split, raw, send, recv, send_h, recv_h, sem):
    ty, tx = lax.axis_index("ty"), lax.axis_index("tx")
    above, left = lax.rem(ty + n_ty - 1, n_ty), lax.rem(tx + n_tx - 1, n_tx)
    barrier = pltpu.get_barrier_semaphore()

    def greet(device):
        pl.semaphore_signal(barrier, inc=1, device_id=device, device_id_type=MESH)

    spread("ty", n_ty, lambda d: greet(beyond("ty", d, n_ty)))
    greet((ty, lax.rem(tx + 1, n_tx)))
    load_side = pltpu.make_async_copy(spec.at[:, :, 0:N], side, sem.at[0])
    load_top = pltpu.make_async_copy(spec.at[:, 0:N], top, sem.at[1])
    load_top.start()
    load_side.start()
    load_raw = pltpu.make_async_copy(amp, raw, sem.at[2])
    load_raw.start()
    pl.semaphore_wait(barrier, n_ty)

    def copy(d):
        return pltpu.make_async_remote_copy(
            src_ref=own, dst_ref=out.at[ty], send_sem=send.at[d], recv_sem=recv.at[d],
            device_id=beyond("ty", d, n_ty), device_id_type=MESH)

    def halo(k, src, dst, device):
        return pltpu.make_async_remote_copy(
            src_ref=src, dst_ref=dst, send_sem=send_h.at[k], recv_sem=recv_h.at[k], device_id=device, device_id_type=MESH)

    spread("ty", n_ty, lambda d: copy(d).start())
    out[ty] = own[...]
    load_top.wait()
    half_top[:, :, 0:N] = top[:, :, 0:N].astype(bf)
    first = halo(0, half_top.at[:, :, 0:N], lower_o.at[:, :, 0:N], (above, tx))
    first.start()
    half_top[:, :, N:TILE_C] = top[:, :, N:TILE_C].astype(bf)
    rest = halo(1, half_top.at[:, :, N:TILE_C], lower_o.at[:, :, N:TILE_C], (above, tx))
    rest.start()
    load_side.wait()
    half_side[...] = side[...].astype(bf)
    right = halo(2, half_side, right_o, (ty, left))
    right.start()
    first.wait()
    corner = halo(3, lower_o.at[:, :, 0:N], corner_o, (ty, left))
    corner.start()
    for c in (0, 1):
        for t in (0, 1):
            split[c, :, t] = probe[c, :, :, t * H:t * H + H]
    for c in (0, 1):
        for m in range(4):
            for t in (0, 1):
                for i in range(32):
                    ds = pl.ds(128 * (i % 2) + row0(i // 2), 8, stride=S)
                    probe_o[c, m, 8 * i:8 * i + 8, t * H:t * H + H] = split[c, m, t, ds]
    load_raw.wait()

    def reorder(i, carry):
        a = dot(perm[...], raw[i].astype(bf)).astype(bf)
        amp_o[i] = lax.dot_general(a, perm[...], (((1,), (1,)), ((), ())), preferred_element_type=f32).astype(bf)
        return carry

    lax.fori_loop(0, POS, reorder, 0)
    spread("ty", n_ty, lambda d: copy(d).wait())
    right.wait()
    corner.wait()
    rest.wait()


def gather(offsets, specimen, probe, amplitude, n_ty, n_tx):
    own = jnp.pad(offsets.reshape(1, 2 * POS), ((0, 7), (0, 128 - 2 * POS)))
    vmem = pl.BlockSpec(memory_space=pltpu.VMEM)
    hbm = pl.BlockSpec(memory_space=pl.ANY)
    dma = pltpu.SemaphoreType.DMA
    return pl.pallas_call(
        functools.partial(gather_kernel, n_ty, n_tx),
        out_shape=[like((n_ty, 8, 128), jnp.int32), like((2, N, TILE_C), bf), like((2, TILE_R, N), bf), like((2, N, N), bf),
                   like(probe.shape, f32), like(amplitude.shape, bf)],
        in_specs=[vmem, hbm, vmem, hbm, vmem],
        out_specs=[vmem, hbm, hbm, hbm, vmem, vmem],
        scratch_shapes=[
            pltpu.VMEM((2, N, TILE_C), f32), pltpu.VMEM((2, TILE_R, N), f32),
            pltpu.VMEM((2, N, TILE_C), bf), pltpu.VMEM((2, TILE_R, N), bf), pltpu.VMEM((2, 4, 2, N, H), f32),
            pltpu.VMEM(amplitude.shape, f32), dma((n_ty,)), dma((n_ty,)), dma((4,)), dma((4,)), dma((3,))],
        compiler_params=pltpu.CompilerParams(collective_id=0, has_side_effects=True, vmem_limit_bytes=VMEM_LIMIT),
    )(own, specimen, probe, amplitude, parity_matrix())


def finish_kernel(n_ty, n_tx, scale, total, down, right, corner, probe_o, down_o, right_o,
                  cast, rax, ray, sx, sy, rbx, rby, gx, gy, hx, hy, arrived, edge, send_ty, recv_ty, send_tx, recv_tx, send_h, recv_h, sem):
    ty, tx = lax.axis_index("ty"), lax.axis_index("tx")
    nx, ny = ROWS_X // n_tx, (ROWS - ROWS_X) // n_ty
    ux, uy = nx // n_ty, ny // n_tx
    barrier = pltpu.get_barrier_semaphore()

    def greet(device):
        pl.semaphore_signal(barrier, inc=1, device_id=device, device_id_type=MESH)

    spread("ty", n_ty, lambda d: greet(beyond("ty", d, n_ty)))
    spread("tx", n_tx, lambda d: greet(beyond("tx", d, n_tx)))
    load = pltpu.make_async_copy(down.at[:, :, 0:N], edge, sem)
    load.start()
    cast[...] = total[...].astype(bf)
    load.wait()
    pl.semaphore_wait(barrier, n_ty + n_tx - 2)

    def over_ty(stage, d, src, dst):
        return pltpu.make_async_remote_copy(
            src_ref=src, dst_ref=dst, send_sem=send_ty.at[stage, d], recv_sem=recv_ty.at[stage, d],
            device_id=beyond("ty", d, n_ty), device_id_type=MESH)

    def over_tx(stage, d, src, dst):
        return pltpu.make_async_remote_copy(
            src_ref=src, dst_ref=dst, send_sem=send_tx.at[stage, d], recv_sem=recv_tx.at[stage, d],
            device_id=beyond("tx", d, n_tx), device_id_type=MESH)

    def rows(k, n, first=0):
        return pl.ds(pl.multiple_of(first + k * n, 8), n)

    def halo(k, src, dst, device):
        return pltpu.make_async_remote_copy(
            src_ref=src, dst_ref=dst, send_sem=send_h.at[k], recv_sem=recv_h.at[k], device_id=device, device_id_type=MESH)

    below, beside = lax.rem(ty + 1, n_ty), lax.rem(tx + 1, n_tx)
    cross = halo(0, corner, arrived, (ty, beside))
    side = halo(1, right, right_o, (ty, beside))
    pieces = [halo(2 + k, edge if k == 0 else down.at[:, :, k * N:k * N + N], down_o.at[:, :, k * N:k * N + N], (below, tx)) for k in range(PIECES)]
    cross.start()
    side.start()

    def ax(d):
        peer = lax.rem(tx + d, n_tx)
        return over_tx(0, d, cast.at[rows(peer, nx)], rax.at[d])

    def ay(d):
        peer = lax.rem(ty + d, n_ty)
        return over_ty(0, d, cast.at[rows(peer, ny, ROWS_X)], ray.at[d])

    spread("tx", n_tx, lambda d: ax(d).start())
    spread("ty", n_ty, lambda d: ay(d).start())
    pieces[1].start()
    pieces[2].start()
    spread("tx", n_tx, lambda d: ax(d).wait())
    sx[...] = lax.fori_loop(1, n_tx, lambda d, t: t + rax[d].astype(f32), total[rows(tx, nx)])

    def bx(d):
        peer = lax.rem(ty + d, n_ty)
        return over_ty(1, d, sx.at[rows(peer, ux)], rbx.at[d])

    spread("ty", n_ty, lambda d: bx(d).start())
    spread("ty", n_ty, lambda d: ay(d).wait())
    sy[...] = lax.fori_loop(1, n_ty, lambda d, t: t + ray[d].astype(f32), total[rows(ty, ny, ROWS_X)])

    def by(d):
        peer = lax.rem(tx + d, n_tx)
        return over_tx(1, d, sy.at[rows(peer, uy)], rby.at[d])

    spread("tx", n_tx, lambda d: by(d).start())
    pieces[3].start()
    spread("ty", n_ty, lambda d: bx(d).wait())
    gx[rows(ty, ux)] = scale * lax.fori_loop(1, n_ty, lambda d, t: t + rbx[d], sx[rows(ty, ux)])

    def cx(d):
        return over_ty(2, d, gx.at[rows(ty, ux)], gx.at[rows(ty, ux)])

    spread("ty", n_ty, lambda d: cx(d).start())
    spread("tx", n_tx, lambda d: by(d).wait())
    gy[rows(tx, uy)] = scale * lax.fori_loop(1, n_tx, lambda d, t: t + rby[d], sy[rows(tx, uy)])

    def cy(d):
        return over_tx(2, d, gy.at[rows(tx, uy)], gy.at[rows(tx, uy)])

    spread("tx", n_tx, lambda d: cy(d).start())
    cross.wait()
    edge[...] = (edge[...].astype(f32) + arrived[...].astype(f32)).astype(bf)
    pieces[0].start()
    spread("ty", n_ty, lambda d: cx(d).wait())
    hx[...] = gx[...].astype(bf)

    def dx(d):
        return over_tx(3, d, hx, probe_o.at[rows(tx, nx)])

    spread("tx", n_tx, lambda d: dx(d).start())
    probe_o[rows(tx, nx)] = hx[...]
    spread("tx", n_tx, lambda d: cy(d).wait())
    hy[...] = gy[...].astype(bf)

    def dy(d):
        return over_ty(3, d, hy, probe_o.at[rows(ty, ny, ROWS_X)])

    spread("ty", n_ty, lambda d: dy(d).start())
    probe_o[rows(ty, ny, ROWS_X)] = hy[...]
    spread("tx", n_tx, lambda d: dx(d).wait())
    spread("ty", n_ty, lambda d: dy(d).wait())
    for h in (side, *pieces):
        h.wait()


def finish(total, down, right, corner, scale, n_ty, n_tx):
    nx, ny = ROWS_X // n_tx, (ROWS - ROWS_X) // n_ty
    vmem = pl.BlockSpec(memory_space=pltpu.VMEM)
    hbm = pl.BlockSpec(memory_space=pl.ANY)
    dma = pltpu.SemaphoreType.DMA
    return pl.pallas_call(
        functools.partial(finish_kernel, n_ty, n_tx, scale),
        out_shape=[like((ROWS, H), bf), like(down.shape, bf), like(right.shape, bf)],
        in_specs=[vmem, hbm, hbm, hbm],
        out_specs=[vmem, hbm, hbm],
        scratch_shapes=[
            pltpu.VMEM((ROWS, H), bf), pltpu.VMEM((n_tx, nx, H), bf), pltpu.VMEM((n_ty, ny, H), bf),
            pltpu.VMEM((nx, H), f32), pltpu.VMEM((ny, H), f32), pltpu.VMEM((n_ty, nx // n_ty, H), f32), pltpu.VMEM((n_tx, ny // n_tx, H), f32),
            pltpu.VMEM((nx, H), f32), pltpu.VMEM((ny, H), f32), pltpu.VMEM((nx, H), bf), pltpu.VMEM((ny, H), bf),
            pltpu.VMEM((2, N, N), bf), pltpu.VMEM((2, N, N), bf),
            dma((4, n_ty)), dma((4, n_ty)), dma((4, n_tx)), dma((4, n_tx)), dma((PIECES + 2,)), dma((PIECES + 2,)), dma],
        compiler_params=pltpu.CompilerParams(collective_id=1, has_side_effects=True, vmem_limit_bytes=VMEM_LIMIT),
    )(total.reshape(ROWS, H), down, right, corner)


def close_kernel(main, down, right, probe, object_o, probe_o):
    b = pl.program_id(1)

    @pl.when(b == 0)
    def _():
        object_o[0, :, 0:N] = main[0, :, 0:N] + (down[0, :, 0:N].astype(f32) + right[0].astype(f32))
        object_o[0, :, N:TILE_C] = main[0, :, N:TILE_C] + down[0, :, N:TILE_C].astype(f32)

    @pl.when(b == 1)
    def _():
        object_o[0, :, 0:N] = main[0, :, 0:N] + right[0].astype(f32)
        object_o[0, :, N:TILE_C] = main[0, :, N:TILE_C]

    for m in (0, 1):
        for t in (0, 1):
            at = (2 * m + t) * N
            probe_o[0, m, :, t * H:t * H + H] = probe[0, at:at + N].astype(f32)


def close(main, down, right, probe):
    def spec(*shape):
        return pl.BlockSpec((1, *shape), lambda c, b: (c, b) + (0,) * (len(shape) - 1))

    return pl.pallas_call(
        close_kernel,
        out_shape=[like(main.shape, f32), like((2, 4, N, N), f32)],
        grid=(2, TILE_R // N),
        in_specs=[spec(N, TILE_C), pl.BlockSpec((1, N, TILE_C), lambda c, b: (c, 0, 0)), spec(N, N), spec(ROWS // 4, H)],
        out_specs=[spec(N, TILE_C), spec(2, N, N)],
        compiler_params=pltpu.CompilerParams(vmem_limit_bytes=VMEM_LIMIT),
    )(main, down, right, probe.reshape(2, ROWS // 2, H))


def on_device(specimen, probe, amplitude, offsets):
    n_ty, n_tx = lax.axis_size("ty"), lax.axis_size("tx")
    positions = offsets.shape[0] * n_ty * n_tx
    everyone, lower, right, corner, arranged, sorted_amp = gather(offsets.reshape(-1), specimen, probe, amplitude, n_ty, n_tx)
    slots = prepare(everyone, sorted_amp, n_ty)
    arrived = lax.all_to_all(slots, "ty", split_axis=0, concat_axis=0, tiled=True)
    tables = make_tables()
    far, pat, inten, places = forward(everyone, specimen, right, lower, corner, arranged, tables, n_ty)
    main, down, rt, cn, total = backward(places, arranged, tables, arrived, far, pat, inten, n_ty)
    scale = float(probe.shape[1] / np.sqrt(positions))
    probe_grad, down, rt = finish(total, down, rt, cn, scale, n_ty, n_tx)
    object_grad, probe_grad = close(main, down, rt, probe_grad)
    return (object_grad, probe_grad)


def solution(mesh):
    in_specs = (P(None, "ty", "tx"), P(), P(("ty", "tx"), None, None), P(("ty", "tx"), None))
    out_specs = (P(None, "ty", "tx"), P())
    return jax.shard_map(on_device, mesh=mesh, in_specs=in_specs, out_specs=out_specs, check_vma=False)
```

```python
import functools

import jax
import jax.numpy as jnp
import ml_dtypes
import numpy as np
from jax import lax
from jax.experimental import pallas as pl
from jax.experimental.pallas import tpu as pltpu
from jax.sharding import PartitionSpec as P

bf = jnp.bfloat16
f32 = jnp.float32
N = 256
H = 128
TILE_R = 512
TILE_C = 1024
POS = 12
VMEM_LIMIT = 60 * 2**20
ROWS = 4096
ROWS_X = 2048
PIECES = 4
MESH = pl.DeviceIdType.MESH
S = 2
B = 16 // S

def row0(i):
    return i // S * 8 * S + i % S

def make_tables():
    k = np.arange(N)
    ang = ((k[:, None] * k[None, :]) % N).astype(np.float64) * (2 * np.pi / N)
    re = (np.cos(ang) / 16).astype(np.float32).astype(ml_dtypes.bfloat16).astype(np.float32)
    im = (-np.sin(ang) / 16).astype(np.float32).astype(ml_dtypes.bfloat16).astype(np.float32)
    order = np.arange(128).reshape(B, 8, S).swapaxes(1, 2).reshape(-1)
    def mix(a, b):
        return np.stack([a.reshape(16, 8, -1), b.reshape(16, 8, -1)], 1).reshape(256, -1)
    out = []
    for par in (0, 1):
        r, i = re[:H, par::2], im[:H, par::2]
        out.append(np.block([[r, i], [-i, r]]))
    for par in (0, 1):
        r, i = re[par::2][:, order], im[par::2][:, order]
        out.append(mix(np.block([r, -i]), np.block([i, r])))
    for par in (0, 1):
        r, i = re[par::2, :H], -im[par::2, :H]
        out.append(np.block([[r, i], [-i, r]]))
    for par in (0, 1):
        r, i = re[order][:, par::2], -im[order][:, par::2]
        out.append(mix(np.block([r, -i]), np.block([i, r])))
    return np.stack(out).astype(ml_dtypes.bfloat16)

def dot(a, b):
    return jnp.dot(a, b, preferred_element_type=f32)

def halves(x):
    x = x.reshape(16, 2, 8, x.shape[-1])
    return x[:, 0].reshape(128, x.shape[-1]), x[:, 1].reshape(128, x.shape[-1])


def parity_matrix():
    order = np.concatenate([np.arange(0, N, 2), np.arange(1, N, 2)])
    return np.eye(N)[order].astype(ml_dtypes.bfloat16)


def prep_kernel(off, amp, out, sem):
    ty = lax.axis_index("ty")
    copies = []
    for i in range(POS):
        tile = off[ty, 0, 2 * i] // TILE_R
        rank = jnp.int32(0)
        for j in range(i):
            rank = rank + (off[ty, 0, 2 * j] // TILE_R == tile).astype(jnp.int32)
        copies.append(pltpu.make_async_copy(amp.at[i], out.at[tile, rank], sem.at[i]))
        copies[i].start()
    for copy in copies:
        copy.wait()


def prepare(everyone, amplitude, sources):
    hbm = pl.BlockSpec(memory_space=pl.ANY)
    return pl.pallas_call(
        prep_kernel,
        out_shape=jax.ShapeDtypeStruct((sources, 2, N, N), bf),
        in_specs=[pl.BlockSpec(memory_space=pltpu.SMEM), pl.BlockSpec(memory_space=pltpu.VMEM)],
        out_specs=hbm,
        scratch_shapes=[pltpu.SemaphoreType.DMA((POS,))],
        compiler_params=pltpu.CompilerParams(vmem_limit_bytes=VMEM_LIMIT),
    )(everyone, amplitude)


def scan(off, source, places):
    ty = lax.axis_index("ty")
    rows, cols = [jnp.int32(-1)] * 2, [jnp.int32(0)] * 2
    seen = jnp.int32(0)
    for i in range(POS):
        r, c = off[source, 0, 2 * i], off[source, 0, 2 * i + 1]
        mine = r // TILE_R == ty
        for q in range(2):
            take = mine & (seen == q)
            rows[q] = jnp.where(take, r % TILE_R, rows[q])
            cols[q] = jnp.where(take, c % TILE_C, cols[q])
        seen = seen + mine.astype(jnp.int32)
    for q in range(2):
        places[source * 4 + 2 * q] = rows[q]
        places[source * 4 + 2 * q + 1] = cols[q]
    return rows, cols


def find(places, source):
    return [places[4 * source], places[4 * source + 2]], [places[4 * source + 1], places[4 * source + 3]]


def p1(probe, pat, A):
    pr, pi = probe[0], probe[1]
    qr, qi = pat[0], pat[1]
    er = pr * qr - pi * qi
    ei = pr * qi + pi * qr
    A[0, :, :H] = (er[:, :H] + er[:, H:]).astype(bf)
    A[0, :, H:] = (ei[:, :H] + ei[:, H:]).astype(bf)
    A[1, :, :H] = (er[:, :H] - er[:, H:]).astype(bf)
    A[1, :, H:] = (ei[:, :H] - ei[:, H:]).astype(bf)


def p2(tab, A, Bb):
    for p in (0, 1):
        t, b = halves(dot(A[p], tab[p]))
        s = (t + b).astype(bf)
        d = (t - b).astype(bf)
        ls = slice(p * H, p * H + H)
        Bb[0, :H, ls] = s[:, :H]
        Bb[0, H:, ls] = s[:, H:]
        Bb[1, :H, ls] = d[:, :H]
        Bb[1, H:, ls] = d[:, H:]


def p3(first, tab, Bb, far, inten):
    for p in (0, 1):
        r, i = halves(dot(tab[2 + p], Bb[p]))
        far[p, 0] = r
        far[p, 1] = i
        t = r * r + i * i
        inten[p] = t if first else inten[p] + t


def p4(amp, inten, fac):
    for p in (0, 1):
        a = amp[p * H:(p + 1) * H].astype(f32)
        fac[p] = 1.0 - a * lax.rsqrt(jnp.maximum(inten[p], 0.25))


def p5(far, fac, C):
    for p in (0, 1):
        f = fac[p]
        rr = (far[p, 0] * f).astype(bf)
        ri = (far[p, 1] * f).astype(bf)
        rs = slice(p * H, p * H + H)
        C[0, rs, :H] = rr[:, :H]
        C[0, rs, H:] = ri[:, :H]
        C[1, rs, :H] = rr[:, H:]
        C[1, rs, H:] = ri[:, H:]


def p6(tab, C, G):
    e = dot(C[0], tab[4])
    o = dot(C[1], tab[5])
    s = (e + o).astype(bf)
    d = (e - o).astype(bf)
    for p in (0, 1):
        rs = slice(p * H, p * H + H)
        G[p, :H, :H] = s[rs, :H]
        G[p, :H, H:] = d[rs, :H]
        G[p, H:, :H] = s[rs, H:]
        G[p, H:, H:] = d[rs, H:]


def both(a, b):
    return jnp.stack([a.reshape(16, 8, 256), b.reshape(16, 8, 256)], 1).reshape(256, 256)


def p7(first, tab, G, probe, pat, grad, total, m):
    er, ei = halves(dot(tab[6], G[0]))
    r_, i_ = halves(dot(tab[7], G[1]))
    br = both(er + r_, er - r_)
    bi = both(ei + i_, ei - i_)
    pr, pi = probe[0], probe[1]
    qr, qi = pat[0], pat[1]
    gr = pr * br + pi * bi
    gi = pr * bi - pi * br
    grad[0] = gr if first else grad[0] + gr
    grad[1] = gi if first else grad[1] + gi
    total[0, m] += qr * br + qi * bi
    total[1, m] += qr * bi - qi * br


def fetch(ext, pat, r, c):
    ct = c // 128
    sh = c % 128
    lane = lax.broadcasted_iota(jnp.int32, (128, 128), 1)
    keep = lane < 128 - sh
    for k in (0, 1):
        for h in (0, 1):
            x = []
            for t in range(3):
                v = jnp.concatenate([ext[k, ct + t, pl.ds(r + 128 * h + row0(i), 8, stride=S)] for i in range(16)], axis=0)
                x.append(pltpu.roll(v, 128 - sh, axis=1))
            for t in (0, 1):
                y = jnp.where(keep, x[t], x[t + 1])
                for i in range(16):
                    pat[k, 16 * i + 8 * h:16 * i + 8 * h + 8, t * H:t * H + H] = y[8 * i:8 * i + 8]

def deposit(grid, grad, r, c):
    ct = c // 128
    sh = c % 128
    lane = lax.broadcasted_iota(jnp.int32, (256, 128), 1)
    keep = lane >= sh
    for k in (0, 1):
        x = grad[k].astype(bf).astype(f32)
        a = pltpu.roll(x[:, :H], sh, axis=1)
        b = pltpu.roll(x[:, H:], sh, axis=1)
        z = jnp.zeros_like(a)
        for t, y in enumerate((jnp.where(keep, a, z), jnp.where(keep, b, a), jnp.where(keep, z, b))):
            for i in range(16):
                for h in (0, 1):
                    ds = pl.ds(r + 128 * h + row0(i), 8, stride=S)
                    grid[k, ct + t, ds] = grid[k, ct + t, ds] + y[16 * i + 8 * h:16 * i + 8 * h + 8]


def forward_kernel(off, spec, right, lower, corner, probe, tab, far, pat, inten, places, ext, A, Bb):
    s = pl.program_id(0)

    @pl.when(s == 0)
    def _():
        for c in (0, 1):
            for t in range(10):
                ls = slice(t * H, t * H + H)
                l2 = slice(t * H - 1024, t * H - 1024 + H)
                ext[c, t, :512] = (spec[c, :, ls] if t < 8 else right[c, :, l2]).astype(bf).astype(f32)
                ext[c, t, 512:] = (lower[c, :, ls] if t < 8 else corner[c, :, l2]).astype(f32)

    rows, cols = scan(off, s, places)

    @pl.when(rows[0] >= 0)
    def _():
        items = [(q, m) for q in range(2) for m in range(4)]
        for t in range(len(items) + 2):
            if 0 <= t - 1 < len(items):
                q, m = items[t - 1]
                p2(tab, A.at[q, m], Bb.at[q, m])
            if 0 <= t - 2 < len(items):
                q, m = items[t - 2]
                p3(m == 0, tab, Bb.at[q, m], far.at[0, q, m], inten.at[0, q])
            if t < len(items):
                q, m = items[t]
                if m == 0:
                    fetch(ext, pat.at[0, q], rows[q], cols[q])
                p1(probe.at[:, m], pat.at[0, q], A.at[q, m])


def backward_kernel(off, probe, tab, amp, far, pat, inten, main_o, down_o, right_o, corner_o, total_o, grid, total, fac, C, G, grad):
    s = pl.program_id(0)

    @pl.when(s == 0)
    def _():
        grid[...] = jnp.zeros_like(grid)
        total[...] = jnp.zeros_like(total)

    rows, cols = find(off, s)

    @pl.when(rows[0] >= 0)
    def _():
        items = [(q, m) for q in range(2) for m in range(4)]
        for t in range(len(items) + 2):
            if 0 <= t - 1 < len(items):
                q, m = items[t - 1]
                p6(tab, C.at[q, m], G.at[q, m])
            if 0 <= t - 2 < len(items):
                q, m = items[t - 2]
                p7(m == 0, tab, G.at[q, m], probe.at[:, m], pat.at[0, q], grad.at[q], total, m)
                if m == 3:
                    deposit(grid, grad.at[q], rows[q], cols[q])
            if t < len(items):
                q, m = items[t]
                if m == 0:
                    p4(amp.at[0, q], inten.at[0, q], fac.at[q])
                p5(far.at[0, q, m], fac.at[q], C.at[q, m])

    @pl.when(s == pl.num_programs(0) - 1)
    def _():
        for c in (0, 1):
            for t in range(10):
                ls = slice(t * H, t * H + H)
                l2 = slice(t * H - 1024, t * H - 1024 + H)
                if t < 8:
                    main_o[c, :, ls] = grid[c, t, :512]
                    down_o[c, :, ls] = grid[c, t, 512:].astype(bf)
                else:
                    right_o[c, :, l2] = grid[c, t, :512].astype(bf)
                    corner_o[c, :, l2] = grid[c, t, 512:].astype(bf)
            for m in range(4):
                for i in range(32):
                    for t in range(2):
                        ds = pl.ds(128 * (i % 2) + row0(i // 2), 8, stride=S)
                        total_o[c, m, t, ds] = total[c, m, 8 * i:8 * i + 8, t * H:t * H + H]


def whole(*shape):
    return pl.BlockSpec(shape, lambda i, o: (0,) * len(shape), pipeline_mode=pl.Buffered(1))


def each(*shape):
    return pl.BlockSpec((1, *shape), lambda i, o: (i,) + (0,) * len(shape))


def like(shape, dtype):
    return jax.ShapeDtypeStruct(shape, dtype)


def forward(off, spec, right, lower, corner, probe, tab, sources):
    return pl.pallas_call(
        forward_kernel,
        out_shape=[like((sources, 2, 4, 2, 2, 128, 256), f32), like((sources, 2, 2, 256, 256), f32), like((sources, 2, 2, 128, 256), f32),
                   like((4 * sources,), jnp.int32)],
        grid_spec=pltpu.PrefetchScalarGridSpec(
            num_scalar_prefetch=1, grid=(sources,),
            in_specs=[whole(2, 512, 1024), whole(2, 512, 256), whole(2, 256, 1024), whole(2, 256, 256), whole(2, 4, 256, 256), whole(8, 256, 256)],
            out_specs=[each(2, 4, 2, 2, 128, 256), each(2, 2, 256, 256), each(2, 2, 128, 256), pl.BlockSpec(memory_space=pltpu.SMEM)],
            scratch_shapes=[pltpu.VMEM((2, 10, 768, 128), f32), pltpu.VMEM((2, 4, 2, 256, 256), bf), pltpu.VMEM((2, 4, 2, 256, 256), bf)]),
        compiler_params=pltpu.CompilerParams(vmem_limit_bytes=VMEM_LIMIT),
        cost_estimate=pl.CostEstimate(flops=32 * 2**29, bytes_accessed=100 * 2**20, transcendentals=0),
    )(off, spec, right, lower, corner, probe, tab)


def backward(off, probe, tab, amp, far, pat, inten, sources):
    return pl.pallas_call(
        backward_kernel,
        out_shape=[like((2, 512, 1024), f32), like((2, 256, 1024), bf), like((2, 512, 256), bf), like((2, 256, 256), bf), like((2, 4, 2, 256, 128), f32)],
        grid_spec=pltpu.PrefetchScalarGridSpec(
            num_scalar_prefetch=1, grid=(sources,),
            in_specs=[whole(2, 4, 256, 256), whole(8, 256, 256), each(2, 256, 256), each(2, 4, 2, 2, 128, 256), each(2, 2, 256, 256), each(2, 2, 128, 256)],
            out_specs=[whole(2, 512, 1024), whole(2, 256, 1024), whole(2, 512, 256), whole(2, 256, 256), whole(2, 4, 2, 256, 128)],
            scratch_shapes=[pltpu.VMEM((2, 10, 768, 128), f32), pltpu.VMEM((2, 4, 256, 256), f32), pltpu.VMEM((2, 2, 128, 256), f32), pltpu.VMEM((2, 4, 2, 256, 256), bf),
                            pltpu.VMEM((2, 4, 2, 256, 256), bf), pltpu.VMEM((2, 2, 256, 256), f32)]),
        compiler_params=pltpu.CompilerParams(vmem_limit_bytes=VMEM_LIMIT),
        cost_estimate=pl.CostEstimate(flops=32 * 2**29, bytes_accessed=100 * 2**20, transcendentals=0),
    )(off, probe, tab, amp, far, pat, inten)


def spread(axis, size, reach):
    lax.fori_loop(1, size, lambda d, c: (reach(d), c)[1], 0)


def beyond(axis, d, size):
    place = {"ty": lax.axis_index("ty"), "tx": lax.axis_index("tx")}
    place[axis] = lax.rem(place[axis] + d, size)
    return (place["ty"], place["tx"])


def gather_kernel(n_ty, n_tx, own, spec, probe_in, amp, perm, out, lower_o, right_o, corner_o, probe_o, amp_o,
                  top, side, half_top, half_side, probe, split, raw, send, recv, send_h, recv_h, sem):
    ty, tx = lax.axis_index("ty"), lax.axis_index("tx")
    above, left = lax.rem(ty + n_ty - 1, n_ty), lax.rem(tx + n_tx - 1, n_tx)
    barrier = pltpu.get_barrier_semaphore()

    def greet(device):
        pl.semaphore_signal(barrier, inc=1, device_id=device, device_id_type=MESH)

    spread("ty", n_ty, lambda d: greet(beyond("ty", d, n_ty)))
    greet((ty, lax.rem(tx + 1, n_tx)))
    load_side = pltpu.make_async_copy(spec.at[:, :, 0:N], side, sem.at[0])
    load_top = pltpu.make_async_copy(spec.at[:, 0:N], top, sem.at[1])
    load_top.start()
    load_side.start()
    load_raw = pltpu.make_async_copy(amp, raw, sem.at[2])
    load_raw.start()
    load_probe = pltpu.make_async_copy(probe_in, probe, sem.at[3])
    load_probe.start()
    pl.semaphore_wait(barrier, n_ty)

    def copy(d):
        return pltpu.make_async_remote_copy(
            src_ref=own, dst_ref=out.at[ty], send_sem=send.at[d], recv_sem=recv.at[d],
            device_id=beyond("ty", d, n_ty), device_id_type=MESH)

    def halo(k, src, dst, device):
        return pltpu.make_async_remote_copy(
            src_ref=src, dst_ref=dst, send_sem=send_h.at[k], recv_sem=recv_h.at[k], device_id=device, device_id_type=MESH)

    spread("ty", n_ty, lambda d: copy(d).start())
    out[ty] = own[...]
    load_top.wait()
    half_top[:, :, 0:N] = top[:, :, 0:N].astype(bf)
    first = halo(0, half_top.at[:, :, 0:N], lower_o.at[:, :, 0:N], (above, tx))
    first.start()
    half_top[:, :, N:TILE_C] = top[:, :, N:TILE_C].astype(bf)
    rest = halo(1, half_top.at[:, :, N:TILE_C], lower_o.at[:, :, N:TILE_C], (above, tx))
    rest.start()
    load_side.wait()
    half_side[...] = side[...].astype(bf)
    right = halo(2, half_side, right_o, (ty, left))
    right.start()
    first.wait()
    corner = halo(3, lower_o.at[:, :, 0:N], corner_o, (ty, left))
    corner.start()
    load_probe.wait()
    for c in (0, 1):
        for t in (0, 1):
            split[c, :, t] = probe[c, :, :, t * H:t * H + H]
    for c in (0, 1):
        for m in range(4):
            for t in (0, 1):
                for i in range(32):
                    ds = pl.ds(128 * (i % 2) + row0(i // 2), 8, stride=S)
                    probe_o[c, m, 8 * i:8 * i + 8, t * H:t * H + H] = split[c, m, t, ds]
    load_raw.wait()

    def reorder(i, carry):
        a = dot(perm[...], raw[i].astype(bf)).astype(bf)
        amp_o[i] = lax.dot_general(a, perm[...], (((1,), (1,)), ((), ())), preferred_element_type=f32).astype(bf)
        return carry

    lax.fori_loop(0, POS, reorder, 0)
    spread("ty", n_ty, lambda d: copy(d).wait())
    right.wait()
    corner.wait()
    rest.wait()


def gather(offsets, specimen, probe, amplitude, n_ty, n_tx):
    own = jnp.pad(offsets.reshape(1, 2 * POS), ((0, 7), (0, 128 - 2 * POS)))
    vmem = pl.BlockSpec(memory_space=pltpu.VMEM)
    hbm = pl.BlockSpec(memory_space=pl.ANY)
    dma = pltpu.SemaphoreType.DMA
    return pl.pallas_call(
        functools.partial(gather_kernel, n_ty, n_tx),
        out_shape=[like((n_ty, 8, 128), jnp.int32), like((2, N, TILE_C), bf), like((2, TILE_R, N), bf), like((2, N, N), bf),
                   like(probe.shape, f32), like(amplitude.shape, bf)],
        in_specs=[vmem, hbm, hbm, hbm, vmem],
        out_specs=[vmem, hbm, hbm, hbm, vmem, vmem],
        scratch_shapes=[
            pltpu.VMEM((2, N, TILE_C), f32), pltpu.VMEM((2, TILE_R, N), f32),
            pltpu.VMEM((2, N, TILE_C), bf), pltpu.VMEM((2, TILE_R, N), bf), pltpu.VMEM(probe.shape, f32), pltpu.VMEM((2, 4, 2, N, H), f32),
            pltpu.VMEM(amplitude.shape, f32), dma((n_ty,)), dma((n_ty,)), dma((4,)), dma((4,)), dma((4,))],
        compiler_params=pltpu.CompilerParams(collective_id=0, has_side_effects=True, vmem_limit_bytes=VMEM_LIMIT),
    )(own, specimen, probe, amplitude, parity_matrix())


def finish_kernel(n_ty, n_tx, scale, total_in, down, right, corner, probe_o, down_o, right_o,
                  total, cast, rax, ray, sx, sy, rbx, rby, gx, gy, arrived, edge, send_ty, recv_ty, send_tx, recv_tx, send_h, recv_h, sem):
    ty, tx = lax.axis_index("ty"), lax.axis_index("tx")
    nx, ny = ROWS_X // n_tx, (ROWS - ROWS_X) // n_ty
    ux, uy = nx // n_ty, ny // n_tx
    barrier = pltpu.get_barrier_semaphore()

    def greet(device):
        pl.semaphore_signal(barrier, inc=1, device_id=device, device_id_type=MESH)

    spread("ty", n_ty, lambda d: greet(beyond("ty", d, n_ty)))
    spread("tx", n_tx, lambda d: greet(beyond("tx", d, n_tx)))
    load_total = pltpu.make_async_copy(total_in, total, sem.at[0])
    load_total.start()
    load = pltpu.make_async_copy(down.at[:, :, 0:N], edge, sem.at[1])
    load.start()
    load_total.wait()
    cast[...] = total[...].astype(bf)
    load.wait()
    pl.semaphore_wait(barrier, n_ty + n_tx - 2)

    def over_ty(stage, d, src, dst):
        return pltpu.make_async_remote_copy(
            src_ref=src, dst_ref=dst, send_sem=send_ty.at[stage, d], recv_sem=recv_ty.at[stage, d],
            device_id=beyond("ty", d, n_ty), device_id_type=MESH)

    def over_tx(stage, d, src, dst):
        return pltpu.make_async_remote_copy(
            src_ref=src, dst_ref=dst, send_sem=send_tx.at[stage, d], recv_sem=recv_tx.at[stage, d],
            device_id=beyond("tx", d, n_tx), device_id_type=MESH)

    def rows(k, n, first=0):
        return pl.ds(pl.multiple_of(first + k * n, 16), n)

    def halo(k, src, dst, device):
        return pltpu.make_async_remote_copy(
            src_ref=src, dst_ref=dst, send_sem=send_h.at[k], recv_sem=recv_h.at[k], device_id=device, device_id_type=MESH)

    below, beside = lax.rem(ty + 1, n_ty), lax.rem(tx + 1, n_tx)
    cross = halo(0, corner, arrived, (ty, beside))
    side = halo(1, right, right_o, (ty, beside))
    pieces = [halo(2 + k, edge if k == 0 else down.at[:, :, k * N:k * N + N], down_o.at[:, :, k * N:k * N + N], (below, tx)) for k in range(PIECES)]
    cross.start()
    side.start()

    def ax(d):
        peer = lax.rem(tx + d, n_tx)
        return over_tx(0, d, cast.at[rows(peer, nx)], rax.at[d])

    def ay(d):
        peer = lax.rem(ty + d, n_ty)
        return over_ty(0, d, cast.at[rows(peer, ny, ROWS_X)], ray.at[d])

    spread("tx", n_tx, lambda d: ax(d).start())
    spread("ty", n_ty, lambda d: ay(d).start())
    pieces[1].start()
    pieces[2].start()
    spread("tx", n_tx, lambda d: ax(d).wait())
    sx[...] = lax.fori_loop(1, n_tx, lambda d, t: t + rax[d].astype(f32), total[rows(tx, nx)])

    def bx(d):
        peer = lax.rem(ty + d, n_ty)
        return over_ty(1, d, sx.at[rows(peer, ux)], rbx.at[d])

    spread("ty", n_ty, lambda d: bx(d).start())
    spread("ty", n_ty, lambda d: ay(d).wait())
    sy[...] = lax.fori_loop(1, n_ty, lambda d, t: t + ray[d].astype(f32), total[rows(ty, ny, ROWS_X)])

    def by(d):
        peer = lax.rem(tx + d, n_tx)
        return over_tx(1, d, sy.at[rows(peer, uy)], rby.at[d])

    spread("tx", n_tx, lambda d: by(d).start())
    pieces[3].start()
    spread("ty", n_ty, lambda d: bx(d).wait())
    gx[rows(ty, ux)] = (scale * lax.fori_loop(1, n_ty, lambda d, t: t + rbx[d], sx[rows(ty, ux)])).astype(bf)

    def cx(d):
        return over_ty(2, d, gx.at[rows(ty, ux)], gx.at[rows(ty, ux)])

    spread("ty", n_ty, lambda d: cx(d).start())
    spread("tx", n_tx, lambda d: by(d).wait())
    gy[rows(tx, uy)] = (scale * lax.fori_loop(1, n_tx, lambda d, t: t + rby[d], sy[rows(tx, uy)])).astype(bf)

    def cy(d):
        return over_tx(2, d, gy.at[rows(tx, uy)], gy.at[rows(tx, uy)])

    spread("tx", n_tx, lambda d: cy(d).start())
    cross.wait()
    edge[...] = (edge[...].astype(f32) + arrived[...].astype(f32)).astype(bf)
    pieces[0].start()
    spread("ty", n_ty, lambda d: cx(d).wait())

    def dx(d):
        return over_tx(3, d, gx, probe_o.at[rows(tx, nx)])

    spread("tx", n_tx, lambda d: dx(d).start())
    probe_o[rows(tx, nx)] = gx[...]
    spread("tx", n_tx, lambda d: cy(d).wait())

    def dy(d):
        return over_ty(3, d, gy, probe_o.at[rows(ty, ny, ROWS_X)])

    spread("ty", n_ty, lambda d: dy(d).start())
    probe_o[rows(ty, ny, ROWS_X)] = gy[...]
    spread("tx", n_tx, lambda d: dx(d).wait())
    spread("ty", n_ty, lambda d: dy(d).wait())
    for h in (side, *pieces):
        h.wait()


def finish(total, down, right, corner, scale, n_ty, n_tx):
    nx, ny = ROWS_X // n_tx, (ROWS - ROWS_X) // n_ty
    vmem = pl.BlockSpec(memory_space=pltpu.VMEM)
    hbm = pl.BlockSpec(memory_space=pl.ANY)
    dma = pltpu.SemaphoreType.DMA
    return pl.pallas_call(
        functools.partial(finish_kernel, n_ty, n_tx, scale),
        out_shape=[like((ROWS, H), bf), like(down.shape, bf), like(right.shape, bf)],
        in_specs=[hbm, hbm, hbm, hbm],
        out_specs=[vmem, hbm, hbm],
        scratch_shapes=[
            pltpu.VMEM((ROWS, H), f32), pltpu.VMEM((ROWS, H), bf), pltpu.VMEM((n_tx, nx, H), bf), pltpu.VMEM((n_ty, ny, H), bf),
            pltpu.VMEM((nx, H), f32), pltpu.VMEM((ny, H), f32), pltpu.VMEM((n_ty, nx // n_ty, H), f32), pltpu.VMEM((n_tx, ny // n_tx, H), f32),
            pltpu.VMEM((nx, H), bf), pltpu.VMEM((ny, H), bf),
            pltpu.VMEM((2, N, N), bf), pltpu.VMEM((2, N, N), bf),
            dma((4, n_ty)), dma((4, n_ty)), dma((4, n_tx)), dma((4, n_tx)), dma((PIECES + 2,)), dma((PIECES + 2,)), dma((2,))],
        compiler_params=pltpu.CompilerParams(collective_id=1, has_side_effects=True, vmem_limit_bytes=VMEM_LIMIT),
    )(total.reshape(ROWS, H), down, right, corner)


def close_kernel(main, down, right, probe, object_o, probe_o):
    b = pl.program_id(1)

    @pl.when(b == 0)
    def _():
        object_o[0, :, 0:N] = main[0, :, 0:N] + (down[0, :, 0:N].astype(f32) + right[0].astype(f32))
        object_o[0, :, N:TILE_C] = main[0, :, N:TILE_C] + down[0, :, N:TILE_C].astype(f32)

    @pl.when(b == 1)
    def _():
        object_o[0, :, 0:N] = main[0, :, 0:N] + right[0].astype(f32)
        object_o[0, :, N:TILE_C] = main[0, :, N:TILE_C]

    for m in (0, 1):
        for t in (0, 1):
            at = (2 * m + t) * N
            probe_o[0, m, :, t * H:t * H + H] = probe[0, at:at + N].astype(f32)


def close(main, down, right, probe):
    def spec(*shape):
        return pl.BlockSpec((1, *shape), lambda c, b: (c, b) + (0,) * (len(shape) - 1))

    return pl.pallas_call(
        close_kernel,
        out_shape=[like(main.shape, f32), like((2, 4, N, N), f32)],
        grid=(2, TILE_R // N),
        in_specs=[spec(N, TILE_C), pl.BlockSpec((1, N, TILE_C), lambda c, b: (c, 0, 0)), spec(N, N), spec(ROWS // 4, H)],
        out_specs=[spec(N, TILE_C), spec(2, N, N)],
        compiler_params=pltpu.CompilerParams(vmem_limit_bytes=VMEM_LIMIT),
    )(main, down, right, probe.reshape(2, ROWS // 2, H))


def on_device(specimen, probe, amplitude, offsets):
    n_ty, n_tx = lax.axis_size("ty"), lax.axis_size("tx")
    positions = offsets.shape[0] * n_ty * n_tx
    everyone, lower, right, corner, arranged, sorted_amp = gather(offsets.reshape(-1), specimen, probe, amplitude, n_ty, n_tx)
    slots = prepare(everyone, sorted_amp, n_ty)
    arrived = lax.all_to_all(slots, "ty", split_axis=0, concat_axis=0, tiled=True)
    tables = make_tables()
    far, pat, inten, places = forward(everyone, specimen, right, lower, corner, arranged, tables, n_ty)
    main, down, rt, cn, total = backward(places, arranged, tables, arrived, far, pat, inten, n_ty)
    scale = float(probe.shape[1] / np.sqrt(positions))
    probe_grad, down, rt = finish(total, down, rt, cn, scale, n_ty, n_tx)
    object_grad, probe_grad = close(main, down, rt, probe_grad)
    return (object_grad, probe_grad)


def solution(mesh):
    in_specs = (P(None, "ty", "tx"), P(), P(("ty", "tx"), None, None), P(("ty", "tx"), None))
    out_specs = (P(None, "ty", "tx"), P())
    return jax.shard_map(on_device, mesh=mesh, in_specs=in_specs, out_specs=out_specs, check_vma=False)
```
